32 devices in a mesh: stream: 4 (over x, core), items: 8 (over z, y).
Axes of the slice: x: 2, y: 2, z: 4, core: 2. Of those that a mesh axis runs over, the one named last changes fastest.
Arguments:
- tokens: bfloat16 [32, 264, 768], P('items', 'stream'), may hold values from -6 to 6
- cotangent: bfloat16 [32, 264, 768], P('items', 'stream'), may hold values from -6 to 6
- text_len: int32 [32], P('items'), may hold values from 4 to 40, as said below
- attn_in: bfloat16 [2, 768, 2304], replicated, may hold values from -0.21875 to 0.21875
- attn_bias: bfloat16 [2, 2, 768], replicated, may hold values from -3 to 3
- attn_out: bfloat16 [2, 768, 768], replicated, may hold values from -0.875 to 0.875
- out_bias: bfloat16 [2, 768], replicated, may hold values from -3 to 3
- norm_gain: bfloat16 [2, 2, 768], replicated, may hold values from 0.25 to 1.75
- norm_bias: bfloat16 [2, 2, 768], replicated, may hold values from -2 to 2
- ffn_in: bfloat16 [3, 768, 3072], replicated, may hold values from -0.21875 to 0.21875
- ffn_in_bias: bfloat16 [3, 3072], replicated, may hold values from -2 to 2
- ffn_out: bfloat16 [3, 3072, 768], replicated, may hold values from -0.109375 to 0.109375
- ffn_out_bias: bfloat16 [3, 768], replicated, may hold values from -2 to 2
Outputs:
- mixed: bfloat16 [32, 264, 768], P('items', 'stream')
- tokens_grad: float32 [32, 264, 768], P('items', 'stream')
- attn_in_grad: float32 [2, 768, 2304], P(None, 'items')
- attn_bias_grad: float32 [2, 2, 768], P(None, None, 'items')
- attn_out_grad: float32 [2, 768, 768], P(None, 'items')
- out_bias_grad: float32 [2, 768], P(None, 'items')
- norm_gain_grad: float32 [2, 2, 768], P(None, None, 'items')
- norm_bias_grad: float32 [2, 2, 768], P(None, None, 'items')
- ffn_in_grad: float32 [3, 768, 3072], P(None, 'items')
- ffn_in_bias_grad: float32 [3, 3072], P(None, 'items')
- ffn_out_grad: float32 [3, 3072, 768], P(None, 'items')
- ffn_out_bias_grad: float32 [3, 768], P(None, 'items')
The draws below stay inside these ranges and needn't reach their ends.
Inputs may be any that keep to these rules, and one draw needn't show every extreme that they name: `text_len`: one item of every draw has exactly 40 text tokens.
All inputs are finite; a program needn't handle non-finite values.
Results may differ from the reference program's by a relative error of at most 0.014.
Values may be sent and summed in bfloat16 or wider, within the bound.
No kernel may reach another device: no remote copies, remote signals or barrier semaphores. Data moves between devices by JAX's collectives and lax.ppermute only.
A program may use at most 320 MiB of HBM per device.

```python
import jax
import jax.numpy as jnp
from jax import lax

D = 768
HEADS = 12
HEAD_DIM = 64
FF = 3072
SLOTS = 66
PATCHES = 197
TEXT = 40
ITEMS = 32
N_STREAM = 4


def draw_text_len(key, part):
    key = jax.random.fold_in(key, 11)
    draw_key, pick_key = jax.random.split(key)
    lengths = jax.random.randint(draw_key, (ITEMS,), 4, TEXT + 1)
    chosen = jax.random.randint(pick_key, (), 0, ITEMS)
    return lengths.at[chosen].set(TEXT).astype(jnp.int32)


def shard_levels(own_key, dims, shards, low, top_value):
    def one(position, parts):
        steps = jax.random.uniform(jax.random.fold_in(jax.random.fold_in(own_key, 6), position), (parts,), jnp.float32, low / len(shards), top_value / len(shards))
        return jnp.repeat(jnp.exp(steps), dims[position] // parts).reshape((-1,) + (1,) * (len(dims) - position - 1))

    level = one(*shards[0])
    for cut in shards[1:]:
        level = level * one(*cut)
    return level


def normal_values(rng, shape, spread, bound, cuts=(), kind=jnp.bfloat16):
    level = shard_levels(rng, shape, cuts, -0.22, 0.18) if cuts else 1.0
    values = jax.random.normal(rng, shape, jnp.float32) * spread * level
    return jnp.minimum(jnp.maximum(values, -bound), bound).astype(kind)


def setup_inputs(seed: int = 0) -> dict:
    splits = jax.random.split(jax.random.key(seed), 14)
    return {
        "tokens": normal_values(splits[0], (ITEMS, N_STREAM * SLOTS, D), 1.0, 6.0, ((0, 8), (1, 4))),
        "cotangent": normal_values(splits[1], (ITEMS, N_STREAM * SLOTS, D), 1.0, 6.0, ((0, 8), (1, 4))),
        "text_len": draw_text_len(jax.random.fold_in(splits[13], 71), 0),
        "attn_in": normal_values(splits[3], (2, D, 3 * D), D ** -0.5, 0.21875),
        "attn_bias": normal_values(splits[4], (2, 2, D), 0.5, 3.0),
        "attn_out": normal_values(splits[5], (2, D, D), (D // 16) ** -0.5, 0.875),
        "out_bias": normal_values(splits[6], (2, D), 0.5, 3.0),
        "norm_gain": jnp.clip(1.0 + 0.15 * jax.random.normal(splits[7], (2, 2, D), jnp.float32), 0.25, 1.75).astype(jnp.bfloat16),
        "norm_bias": normal_values(splits[8], (2, 2, D), 0.3, 2.0),
        "ffn_in": normal_values(splits[9], (3, D, FF), D ** -0.5, 0.21875),
        "ffn_in_bias": normal_values(splits[10], (3, FF), 0.3, 2.0),
        "ffn_out": normal_values(splits[11], (3, FF, D), FF ** -0.5, 0.109375),
        "ffn_out_bias": normal_values(splits[12], (3, D), 0.3, 2.0),
    }


@jax.custom_vjp
def low(v):
    return lax.optimization_barrier(v.astype(jnp.bfloat16)).astype(jnp.float32)

@jax.custom_vjp
def low_back(v):
    return v

def low_keep(v):
    return (low(v), None)

def low_pass(kept, grad):
    return (grad,)

def back_keep(v):
    return (v, None)

def back_low(kept, grad):
    return (low(grad),)
low.defvjp(low_keep, low_pass)
low_back.defvjp(back_keep, back_low)
norm_eps = 1e-06
highest = lax.Precision.HIGHEST

def gelu_exact(values):
    return 0.5 * values * (1.0 + lax.erf(values * 0.7071067811865476))

def layer_norm(values, gain, offset):
    row_mean = lax.optimization_barrier(jnp.mean(values, axis=-1, keepdims=True))
    centred = values - row_mean
    row_var = lax.optimization_barrier(jnp.mean(centred * centred, axis=-1, keepdims=True))
    return centred * lax.rsqrt(row_var + norm_eps) * gain + offset

def matmul(left, right):
    return jnp.einsum('bld,df->blf', left, right, precision=highest)

def slot_live(text_len):
    places = jnp.arange(N_STREAM, dtype=jnp.int32)
    patch_counts = jnp.clip(PATCHES - places * SLOTS, 0, SLOTS)
    counts = jnp.where(places[None, :] == N_STREAM - 1, text_len[:, None].astype(jnp.int32), patch_counts[None, :])
    inside = jnp.arange(SLOTS, dtype=jnp.int32)
    return (inside[None, None, :] < counts[:, :, None]).reshape(text_len.shape[0], N_STREAM * SLOTS)

def attend_group(group):
    queries, keys_all, values_all, live = group
    grouped = queries.shape[0]
    length = queries.shape[1]
    query_heads = queries.reshape(grouped, length, HEADS, HEAD_DIM)
    key_heads = keys_all.reshape(grouped, length, HEADS, HEAD_DIM)
    value_heads = values_all.reshape(grouped, length, HEADS, HEAD_DIM)
    raw_scores = jnp.einsum('gqhd,gkhd->ghqk', query_heads, key_heads, precision=highest) * HEAD_DIM ** (-0.5)
    scores = low_back(jnp.where(live[:, None, None, :], raw_scores, -1e+30))
    row_max = lax.optimization_barrier(jnp.max(scores, axis=-1, keepdims=True))
    exponent = jnp.exp(scores - row_max)
    softmaxed = low(exponent / lax.optimization_barrier(jnp.sum(exponent, axis=-1, keepdims=True)))
    context = jnp.einsum('ghqk,gkhd->gqhd', softmaxed, value_heads, precision=highest)
    return context.reshape(grouped, length, HEADS * HEAD_DIM)

def attention(queries, keys_all, values_all, live):
    blocks = queries.shape[0] // 8

    def grouped_view(value):
        return value.reshape((blocks, 8) + value.shape[1:])
    mapped = lax.map(jax.checkpoint(attend_group), (grouped_view(queries), grouped_view(keys_all), grouped_view(values_all), grouped_view(live)))
    return mapped.reshape(queries.shape)

def feed(normed, ffn_in, ffn_in_bias, ffn_out, ffn_out_bias, expert):
    pre_act = low_back(matmul(normed, ffn_in[expert]) + ffn_in_bias[expert])
    activated = low(gelu_exact(pre_act))
    return low_back(matmul(activated, ffn_out[expert]) + ffn_out_bias[expert])

def forward(tokens, attn_in, attn_bias, attn_out, out_bias, norm_gain, norm_bias, ffn_in, ffn_in_bias, ffn_out, ffn_out_bias, live, text_rows):
    state = tokens
    for layer_no in range(2):
        normed = low(layer_norm(state, norm_gain[layer_no, 0], norm_bias[layer_no, 0]))
        packed = matmul(normed, attn_in[layer_no])
        queries = low_back(low(packed[:, :, :D] + attn_bias[layer_no, 0]))
        keys_all = low_back(low(packed[:, :, D:2 * D]))
        values_all = low_back(low(packed[:, :, 2 * D:] + attn_bias[layer_no, 1]))
        context = low_back(low(attention(queries, keys_all, values_all, live)))
        branch = low_back(matmul(context, attn_out[layer_no]) + out_bias[layer_no])
        state = state + branch
        normed_two = low(layer_norm(state, norm_gain[layer_no, 1], norm_bias[layer_no, 1]))
        if layer_no == 0:
            vision = feed(normed_two, ffn_in, ffn_in_bias, ffn_out, ffn_out_bias, 0)
            language = feed(normed_two, ffn_in, ffn_in_bias, ffn_out, ffn_out_bias, 1)
            branch_two = jnp.where(text_rows, language, vision)
        else:
            branch_two = feed(normed_two, ffn_in, ffn_in_bias, ffn_out, ffn_out_bias, 2)
        state = state + branch_two
    return state

def reference(tokens, cotangent, text_len, attn_in, attn_bias, attn_out, out_bias, norm_gain, norm_bias, ffn_in, ffn_in_bias, ffn_out, ffn_out_bias):
    live = slot_live(text_len)
    text_rows = (jnp.arange(N_STREAM * SLOTS, dtype=jnp.int32) >= (N_STREAM - 1) * SLOTS)[None, :, None]
    floats = tuple((value.astype(jnp.float32) for value in (tokens, attn_in, attn_bias, attn_out, out_bias, norm_gain, norm_bias, ffn_in, ffn_in_bias, ffn_out, ffn_out_bias)))

    def run(*params):
        return forward(*params, live, text_rows)
    result, pull = jax.vjp(run, *floats)
    grads = pull(cotangent.astype(jnp.float32) * live.astype(jnp.float32)[:, :, None])
    return (result.astype(jnp.bfloat16), grads[0], grads[1], grads[2], grads[3], grads[4], grads[5], grads[6], grads[7], grads[8], grads[9], grads[10])
```

```python
import functools
import jax
import jax.numpy as jnp
from jax import lax
from jax.experimental import pallas as pl
from jax.experimental.pallas import tpu as pltpu
from jax.sharding import PartitionSpec as P

HEADS = 12
PATCHES = 197
TEXT = 40
F32 = jnp.float32
BF = jnp.bfloat16
EPS = 1e-06
FILL = -1e30
MIB = 1 << 20


def dot(left, right, dims=((1,), (0,))):
    return lax.dot_general(left, right, (dims, ((), ())), preferred_element_type=F32)


NT = ((1,), (1,))
TN = ((0,), (0,))


def norm_stats(values):
    row_mean = jnp.mean(values, axis=-1, keepdims=True)
    centred = values - row_mean
    row_var = jnp.mean(centred * centred, axis=-1, keepdims=True)
    inv_std = lax.rsqrt(row_var + EPS)
    return centred * inv_std, inv_std


def norm_back(grad_out, values, gain):
    scaled, inv_std = norm_stats(values)
    grad_scaled = grad_out * gain
    mean_first = jnp.mean(grad_scaled, axis=-1, keepdims=True)
    mean_second = jnp.mean(grad_scaled * scaled, axis=-1, keepdims=True)
    grad_in = inv_std * (grad_scaled - mean_first - scaled * mean_second)
    gain_sum = jnp.sum(grad_out * scaled, axis=0, keepdims=True)
    offset_sum = jnp.sum(grad_out, axis=0, keepdims=True)
    return grad_in, gain_sum, offset_sum


def gelu_parts(pre):
    cumulative = 0.5 * (1.0 + lax.erf(pre * 0.7071067811865476))
    density = jnp.exp(-0.5 * pre * pre) * 0.3989422804014327
    return pre * cumulative, cumulative + pre * density


def params(limit_mib):
    return pltpu.CompilerParams(vmem_limit_bytes=limit_mib * MIB)


def cost(flops, moved, trans=0):
    return pl.CostEstimate(flops=int(flops), bytes_accessed=int(moved), transcendentals=int(trans))


def whole(shape):
    return pl.BlockSpec(shape, lambda *_: (0,) * len(shape))


def layer_block(shape, index):
    return pl.BlockSpec((1,) + shape, lambda *_: (index,) + (0,) * len(shape))


SMEM = pl.BlockSpec(memory_space=pltpu.SMEM)


class Dims:
    def __init__(self, slots, streams, width, hidden, item_devs):
        self.slots = slots
        self.text_at = slots * (streams - 1)
        self.rows = slots * streams
        self.full = -(-self.rows // 16) * 16
        self.live = -(-(self.text_at + TEXT) // 16) * 16
        self.keys = -(-self.live // 128) * 128
        self.vis = -(-self.text_at // 16) * 16
        self.lang = self.text_at // 16 * 16
        self.width = width
        self.hidden = hidden
        self.streams = streams
        self.item_devs = item_devs
        self.share = width // item_devs


def fwd_attn_body(dm, sc, x, gain, offset, win, bias, wout, obias, n1o, qo, ko, vo, po, ctxo, x1o, n2o, n2live, ctx_s):
    width = dm.width
    xv = x[...].astype(F32)
    scaled, _ = norm_stats(xv)
    n1 = (scaled * gain[0, 0:1].astype(F32) + offset[0, 0:1].astype(F32)).astype(BF)
    n1o[...] = n1[: dm.live]
    w = win.at[0]
    q = (dot(n1, w[:, 0:width]) + bias[0, 0:1].astype(F32)).astype(BF) * 0.125
    q = q.astype(BF)
    k = dot(n1[: dm.keys], w[:, width : 2 * width]).astype(BF)
    v = (dot(n1[: dm.keys], w[:, 2 * width :]) + bias[0, 1:2].astype(F32)).astype(BF)
    qo[...] = q[: dm.live]
    ko[...] = k
    vo[...] = v
    col = lax.broadcasted_iota(jnp.int32, (1, dm.keys), 1)
    valid = (col < PATCHES) | ((col >= dm.text_at) & (col < dm.text_at + sc[0]))
    low_lane = lax.broadcasted_iota(jnp.int32, (1, 128), 1) < 64
    for pair in range(HEADS // 2):
        lanes = slice(pair * 128, pair * 128 + 128)
        qp, kp, vp = q[:, lanes], k[:, lanes], v[:, lanes]
        outs = []
        for j in range(2):
            qm = jnp.where(low_lane if j == 0 else ~low_lane, qp, jnp.zeros_like(qp))
            scores = jnp.where(valid, dot(qm, kp, NT), FILL)
            top = jnp.max(scores, axis=-1, keepdims=True)
            expo = jnp.exp(scores - top)
            probs = (expo / jnp.sum(expo, axis=-1, keepdims=True)).astype(BF)
            po[2 * pair + j] = probs[: dm.live]
            outs.append(dot(probs, vp))
        ctx_s[:, lanes] = jnp.where(low_lane, outs[0], outs[1]).astype(BF)
    ctx = ctx_s[...]
    ctxo[...] = ctx[: dm.live]
    x1 = xv + (dot(ctx, wout[0]) + obias[0].astype(F32))
    x1o[...] = x1
    scaled, _ = norm_stats(x1)
    n2 = (scaled * gain[0, 1:2].astype(F32) + offset[0, 1:2].astype(F32)).astype(BF)
    n2o[...] = n2
    n2live[...] = n2[: dm.live]


def fwd_attn(dm, layer, sc, x, norm_gain, norm_bias, attn_in, attn_bias, attn_out, out_bias):
    d, full, live, keys = dm.width, dm.full, dm.live, dm.keys
    sds = jax.ShapeDtypeStruct
    shapes = [
        sds((live, d), BF),
        sds((live, d), BF),
        sds((keys, d), BF),
        sds((keys, d), BF),
        sds((HEADS, live, keys), BF),
        sds((live, d), BF),
        sds((full, d), F32),
        sds((full, d), BF),
        sds((live, d), BF),
    ]
    return pl.pallas_call(
        functools.partial(fwd_attn_body, dm),
        grid=(1,),
        in_specs=[
            SMEM,
            whole((full, d)),
            layer_block((2, d), layer),
            layer_block((2, d), layer),
            layer_block((d, 3 * d), layer),
            layer_block((2, d), layer),
            layer_block((d, d), layer),
            layer_block((1, d), layer),
        ],
        out_specs=[whole(s.shape) for s in shapes],
        out_shape=shapes,
        scratch_shapes=[pltpu.VMEM((full, d), BF)],
        compiler_params=params(40),
        cost_estimate=cost(2 * full * d * d * 4 + 4 * full * keys * d, 8e6, HEADS * full * keys),
    )(sc, x, norm_gain, norm_bias, attn_in, attn_bias, attn_out, out_bias[:, None])


TILE = 1024


def fwd_ff_one_body(dm, last, n2, x1, wi, bi, wo, bo, slope, x2, acc):
    t = pl.program_id(0)
    act, slope_v = gelu_parts(dot(n2[...], wi[0]) + bi[0].astype(F32))
    slope[...] = slope_v[: dm.live].astype(BF)
    part = dot(act.astype(BF), wo[0])

    @pl.when(t == 0)
    def _():
        acc[...] = part + (x1[...] + bo[0].astype(F32))

    @pl.when(t > 0)
    def _():
        acc[...] += part

    @pl.when(t == pl.num_programs(0) - 1)
    def _():
        x2[...] = acc[...].astype(x2.dtype)


def fwd_ff_one(dm, expert, n2, x1, ffn_in, ffn_in_bias, ffn_out, ffn_out_bias):
    d, full, hid = dm.width, dm.full, dm.hidden
    sds = jax.ShapeDtypeStruct
    return pl.pallas_call(
        functools.partial(fwd_ff_one_body, dm, True),
        grid=(hid // TILE,),
        in_specs=[
            whole((full, d)),
            whole((full, d)),
            pl.BlockSpec((1, d, TILE), lambda t: (expert, 0, t)),
            pl.BlockSpec((1, 1, TILE), lambda t: (expert, 0, t)),
            pl.BlockSpec((1, TILE, d), lambda t: (expert, t, 0)),
            layer_block((1, d), expert),
        ],
        out_specs=[pl.BlockSpec((dm.live, TILE), lambda t: (0, t)), whole((full, d))],
        out_shape=[sds((dm.live, hid), BF), sds((full, d), BF)],
        scratch_shapes=[pltpu.VMEM((full, d), F32)],
        compiler_params=params(40),
        cost_estimate=cost(4 * full * d * hid, 12e6, 2 * full * hid),
    )(n2, x1, ffn_in, ffn_in_bias[:, None], ffn_out, ffn_out_bias[:, None])


def fwd_ff_two_body(dm, n2, x1, wv, wl, bi, wov, wol, bo, slope_v, slope_l, x2, acc):
    t = pl.program_id(0)
    vis, lang, text_at = dm.vis, dm.lang, dm.text_at
    rows_v = lax.broadcasted_iota(jnp.int32, (vis, 1), 0) < text_at
    rows_l = lax.broadcasted_iota(jnp.int32, (dm.full - lang, 1), 0) + lang >= text_at
    act_v, sv = gelu_parts(dot(n2[0:vis], wv[0]) + bi[0, 0:1].astype(F32))
    act_l, sl = gelu_parts(dot(n2[lang:], wl[0]) + bi[1, 0:1].astype(F32))
    slope_v[...] = sv.astype(BF)
    slope_l[...] = sl[: dm.live - lang].astype(BF)
    part_v = dot(act_v.astype(BF), wov[0])
    part_l = dot(act_l.astype(BF), wol[0])

    @pl.when(t == 0)
    def _():
        acc[...] = x1[...]
        part_vb = part_v + bo[0, 0:1].astype(F32)
        part_lb = part_l + bo[1, 0:1].astype(F32)
        acc[0:vis] += jnp.where(rows_v, part_vb, 0.0)
        acc[lang:] += jnp.where(rows_l, part_lb, 0.0)

    @pl.when(t > 0)
    def _():
        acc[0:vis] += jnp.where(rows_v, part_v, 0.0)
        acc[lang:] += jnp.where(rows_l, part_l, 0.0)

    @pl.when(t == pl.num_programs(0) - 1)
    def _():
        x2[...] = acc[...]


def fwd_ff_two(dm, n2, x1, ffn_in, ffn_in_bias, ffn_out, ffn_out_bias):
    d, full, hid = dm.width, dm.full, dm.hidden
    sds = jax.ShapeDtypeStruct
    count = ffn_in.shape[0]
    return pl.pallas_call(
        functools.partial(fwd_ff_two_body, dm),
        grid=(hid // TILE,),
        in_specs=[
            whole((full, d)),
            whole((full, d)),
            pl.BlockSpec((1, d, TILE), lambda t: (0, 0, t)),
            pl.BlockSpec((1, d, TILE), lambda t: (1, 0, t)),
            pl.BlockSpec((count, 1, TILE), lambda t: (0, 0, t)),
            pl.BlockSpec((1, TILE, d), lambda t: (0, t, 0)),
            pl.BlockSpec((1, TILE, d), lambda t: (1, t, 0)),
            whole((count, 1, d)),
        ],
        out_specs=[
            pl.BlockSpec((dm.vis, TILE), lambda t: (0, t)),
            pl.BlockSpec((dm.live - dm.lang, TILE), lambda t: (0, t)),
            whole((full, d)),
        ],
        out_shape=[sds((dm.vis, hid), BF), sds((dm.live - dm.lang, hid), BF), sds((full, d), F32)],
        scratch_shapes=[pltpu.VMEM((full, d), F32)],
        compiler_params=params(40),
        cost_estimate=cost(4 * full * d * hid, 21e6, 2 * full * hid),
    )(n2, x1, ffn_in, ffn_in, ffn_in_bias[:, None], ffn_out, ffn_out, ffn_out_bias[:, None])


def finish_ff_back(dm, g, gn, x1, gain, go, ga, sums):
    grad_in, gain_sum, offset_sum = norm_back(gn, x1[0 : dm.live], gain[0, 1:2].astype(F32))
    out = g[...] + grad_in
    go[...] = out
    low = out.astype(BF)
    ga[...] = low
    sums[0:1] = gain_sum
    sums[1:2] = offset_sum
    sums[2:3] = jnp.sum(low.astype(F32), axis=0, keepdims=True)


def back_ff_one_body(dm, g, gf, x1, gain, slope, wo, wi, go, ga, sums, hsum, acc):
    t = pl.program_id(0)
    gpre = (dot(gf[...], wo[0], NT) * slope[...].astype(F32)).astype(BF)
    hsum[...] = jnp.sum(gpre.astype(F32), axis=0, keepdims=True)
    part = dot(gpre, wi[0], NT)

    @pl.when(t == 0)
    def _():
        acc[...] = part

    @pl.when(t > 0)
    def _():
        acc[...] += part

    @pl.when(t == pl.num_programs(0) - 1)
    def _():
        sums[3:4] = jnp.sum(gf[...].astype(F32), axis=0, keepdims=True)
        finish_ff_back(dm, g, acc[...], x1, gain, go, ga, sums)


def back_ff_one(dm, layer, expert, g, gf, x1, norm_gain, slope, ffn_in, ffn_out):
    d, live, hid = dm.width, dm.live, dm.hidden
    sds = jax.ShapeDtypeStruct
    return pl.pallas_call(
        functools.partial(back_ff_one_body, dm),
        grid=(hid // TILE,),
        in_specs=[
            whole((live, d)),
            whole((live, d)),
            whole((dm.full, d)),
            layer_block((2, d), layer),
            pl.BlockSpec((live, TILE), lambda t: (0, t)),
            pl.BlockSpec((1, TILE, d), lambda t: (expert, t, 0)),
            pl.BlockSpec((1, d, TILE), lambda t: (expert, 0, t)),
        ],
        out_specs=[
            whole((live, d)),
            whole((live, d)),
            whole((4, d)),
            pl.BlockSpec((1, TILE), lambda t: (0, t)),
        ],
        out_shape=[sds((live, d), F32), sds((live, d), BF), sds((4, d), F32), sds((1, hid), F32)],
        scratch_shapes=[pltpu.VMEM((live, d), F32)],
        compiler_params=params(40),
        cost_estimate=cost(4 * live * d * hid, 13e6),
    )(g, gf, x1, norm_gain, slope, ffn_out, ffn_in)


def back_ff_two_body(dm, g, gf, x1, gain, slv, sll, wov, wol, wv, wl, go, ga, sums, hsum, acc):
    t = pl.program_id(0)
    vis, lang, text_at, live = dm.vis, dm.lang, dm.text_at, dm.live
    rows_v = lax.broadcasted_iota(jnp.int32, (vis, 1), 0) < text_at
    rows_l = lax.broadcasted_iota(jnp.int32, (live - lang, 1), 0) + lang >= text_at
    gv = jnp.where(rows_v, gf[0:vis].astype(F32), 0.0)
    gl = jnp.where(rows_l, gf[lang:].astype(F32), 0.0)
    pre_v = (dot(gv.astype(BF), wov[0], NT) * slv[...].astype(F32)).astype(BF)
    pre_l = (dot(gl.astype(BF), wol[0], NT) * sll[...].astype(F32)).astype(BF)
    hsum[0:1] = jnp.sum(pre_v.astype(F32), axis=0, keepdims=True)
    hsum[1:2] = jnp.sum(pre_l.astype(F32), axis=0, keepdims=True)
    part_v = dot(pre_v, wv[0], NT)
    part_l = dot(pre_l, wl[0], NT)

    @pl.when(t == 0)
    def _():
        acc[...] = jnp.zeros_like(acc)

    acc[0:vis] += part_v
    acc[lang:] += part_l

    @pl.when(t == pl.num_programs(0) - 1)
    def _():
        sums[3:4] = jnp.sum(gv, axis=0, keepdims=True)
        sums[4:5] = jnp.sum(gl, axis=0, keepdims=True)
        finish_ff_back(dm, g, acc[...], x1, gain, go, ga, sums)


def back_ff_two(dm, layer, g, gf, x1, norm_gain, slope_v, slope_l, ffn_in, ffn_out):
    d, live, hid = dm.width, dm.live, dm.hidden
    sds = jax.ShapeDtypeStruct
    return pl.pallas_call(
        functools.partial(back_ff_two_body, dm),
        grid=(hid // TILE,),
        in_specs=[
            whole((live, d)),
            whole((live, d)),
            whole((dm.full, d)),
            layer_block((2, d), layer),
            pl.BlockSpec((dm.vis, TILE), lambda t: (0, t)),
            pl.BlockSpec((live - dm.lang, TILE), lambda t: (0, t)),
            pl.BlockSpec((1, TILE, d), lambda t: (0, t, 0)),
            pl.BlockSpec((1, TILE, d), lambda t: (1, t, 0)),
            pl.BlockSpec((1, d, TILE), lambda t: (0, 0, t)),
            pl.BlockSpec((1, d, TILE), lambda t: (1, 0, t)),
        ],
        out_specs=[
            whole((live, d)),
            whole((live, d)),
            whole((5, d)),
            pl.BlockSpec((2, TILE), lambda t: (0, t)),
        ],
        out_shape=[sds((live, d), F32), sds((live, d), BF), sds((5, d), F32), sds((2, hid), F32)],
        scratch_shapes=[pltpu.VMEM((live, d), F32)],
        compiler_params=params(40),
        cost_estimate=cost(4 * live * d * hid, 22e6),
    )(g, gf, x1, norm_gain, slope_v, slope_l, ffn_out, ffn_out, ffn_in, ffn_in)


def back_attn_body(dm, g, ga, q, k, v, p, x, gain, win, wout, dqkv, go, gfo, sums):
    width, live = dm.width, dm.live
    gc = dot(ga[...], wout[0], NT).astype(BF)
    low_lane = lax.broadcasted_iota(jnp.int32, (1, 128), 1) < 64
    for pair in range(HEADS // 2):
        lanes = slice(pair * 128, pair * 128 + 128)
        gp, qp, kp, vp = gc[:, lanes], q[:, lanes], k[:, lanes], v[:, lanes]
        dqs, dks, dvs = [], [], []
        for j in range(2):
            gm = jnp.where(low_lane if j == 0 else ~low_lane, gp, jnp.zeros_like(gp))
            dprob = dot(gm, vp, NT)
            prob_low = p[2 * pair + j]
            prob = prob_low.astype(F32)
            inner = jnp.sum(prob * dprob, axis=-1, keepdims=True)
            ds = (prob * (dprob - inner)).astype(BF)
            dqs.append(dot(ds, kp))
            dks.append(dot(ds, qp, TN))
            dvs.append(dot(prob_low, gp, TN))
        dq = jnp.where(low_lane, dqs[0], dqs[1]) * 0.125
        dk = jnp.where(low_lane, dks[0], dks[1])
        dv = jnp.where(low_lane, dvs[0], dvs[1])
        dqkv[:, pair * 128 : pair * 128 + 128] = dq.astype(BF)
        dqkv[:, width + pair * 128 : width + pair * 128 + 128] = dk[:live].astype(BF)
        dqkv[:, 2 * width + pair * 128 : 2 * width + pair * 128 + 128] = dv[:live].astype(BF)
    packed = dqkv[...]
    gn = dot(packed, win[0], NT)
    grad_in, gain_sum, offset_sum = norm_back(gn, x[0:live].astype(F32), gain[0, 0:1].astype(F32))
    out = g[...] + grad_in
    go[...] = out
    gfo[...] = out.astype(BF)
    sums[0:1] = gain_sum
    sums[1:2] = offset_sum
    sums[2:3] = jnp.sum(packed[:, 0:width].astype(F32), axis=0, keepdims=True)
    sums[3:4] = jnp.sum(packed[:, 2 * width :].astype(F32), axis=0, keepdims=True)


def back_attn(dm, layer, g, ga, q, k, v, p, x, norm_gain, attn_in, attn_out):
    d, live, keys = dm.width, dm.live, dm.keys
    sds = jax.ShapeDtypeStruct
    shapes = [sds((live, 3 * d), BF), sds((live, d), F32), sds((live, d), BF), sds((4, d), F32)]
    return pl.pallas_call(
        functools.partial(back_attn_body, dm),
        grid=(1,),
        in_specs=[
            whole((live, d)),
            whole((live, d)),
            whole((live, d)),
            whole((keys, d)),
            whole((keys, d)),
            whole((HEADS, live, keys)),
            whole((dm.full, d)),
            layer_block((2, d), layer),
            layer_block((d, 3 * d), layer),
            layer_block((d, d), layer),
        ],
        out_specs=[whole(s.shape) for s in shapes],
        out_shape=shapes,
        compiler_params=params(40),
        cost_estimate=cost(2 * live * d * d * 4 + 10 * live * keys * d, 10e6),
    )(g, ga, q, k, v, p, x, norm_gain, attn_in, attn_out)


def store_shares(dm, ref, lead, row, value, flip):
    n, share = dm.item_devs, dm.share
    bits = n.bit_length() - 1
    for i in range(n):
        place = int(format(i, "0%db" % bits)[::-1], 2) if bits else 0
        ref[lead + (place ^ flip, slice(row, row + share))] = value[i * share : (i + 1) * share]


def in_kernel_shares(dm):
    return dm.share % 16 == 0


def wgrad_attn_body(dm, sc, n1, dqkv, ctx, ga, out):
    width = dm.width
    for quarter in range(4):
        if quarter < 3:
            value = dot(n1[...], dqkv[:, quarter * width : (quarter + 1) * width], TN).astype(BF)
        else:
            value = dot(ctx[...], ga[...], TN).astype(BF)
        if in_kernel_shares(dm):
            store_shares(dm, out, (quarter ^ sc[1],), 0, value, sc[2])
        else:
            out[quarter ^ sc[1]] = value


def wgrad_attn(dm, sc, n1, dqkv, ctx, ga):
    d, live, n, share = dm.width, dm.live, dm.item_devs, dm.share
    shape = (4, n, share, d) if in_kernel_shares(dm) else (4, d, d)
    out = pl.pallas_call(
        functools.partial(wgrad_attn_body, dm),
        grid=(1,),
        in_specs=[SMEM, whole((live, d)), whole((live, 3 * d)), whole((live, d)), whole((live, d))],
        out_specs=whole(shape),
        out_shape=jax.ShapeDtypeStruct(shape, BF),
        compiler_params=params(40),
        cost_estimate=cost(8 * live * d * d, 8e6),
    )(sc, n1, dqkv, ctx, ga)
    return out


def wgrad_ff_body(dm, experts, sc, *refs):
    d, live, streams = dm.width, dm.live, dm.streams
    n2s = refs[0:streams]
    gfs = refs[streams : 2 * streams]
    wi, wo, bi, out, n2a, gfa, acta, gpa = refs[2 * streams :]
    base = 0
    for index, (expert, start, stop, low, high) in enumerate(experts):
        size = stop - start
        total = size * streams
        rows = lax.broadcasted_iota(jnp.int32, (size, 1), 0) + start
        keep = (rows >= low) & (rows < high)
        for r in range(streams):
            n2a[r * size : (r + 1) * size] = n2s[r][start:stop]
            gpart = gfs[r][start:stop]
            if low > start or high < stop:
                gpart = jnp.where(keep, gpart.astype(F32), 0.0).astype(BF)
            gfa[r * size : (r + 1) * size] = gpart

        chunk = size if size >= 128 else total

        def step(c, carry, index=index, chunk=chunk):
            at = pl.ds(pl.multiple_of(c * chunk, 16), chunk)
            act, slope = gelu_parts(dot(n2a[at], wi[index]) + bi[index].astype(F32))
            acta[at] = act.astype(BF)
            gpa[at] = (dot(gfa[at], wo[index], NT) * slope).astype(BF)
            return carry

        lax.fori_loop(0, total // chunk, step, 0)
        grads = (
            (n2a, gpa),
            (acta, gfa),
        )
        for left, right in grads:
            value = dot(left[0:total], right[0:total], TN).astype(BF)
            if in_kernel_shares(dm):
                store_shares(dm, out, (), base, value, sc[2])
                base += dm.share
            else:
                out[base] = value
                base += 1


def wgrad_ff(dm, experts, sc, n2s, gfs, wi, wo, bi):
    d, live, n, share = dm.width, dm.live, dm.item_devs, dm.share
    count = len(experts)
    shape = (n, 2 * count * share, d) if in_kernel_shares(dm) else (2 * count, d, d)
    top = max(stop - start for _, start, stop, _, _ in experts) * dm.streams
    return pl.pallas_call(
        functools.partial(wgrad_ff_body, dm, experts),
        grid=(1,),
        in_specs=[SMEM] + [whole((live, d))] * (2 * dm.streams) + [whole((count, d, d)), whole((count, d, d)), whole((count, 1, d))],
        out_specs=whole(shape),
        out_shape=jax.ShapeDtypeStruct(shape, BF),
        scratch_shapes=[pltpu.VMEM((top, d), BF)] * 4,
        compiler_params=params(48),
        cost_estimate=cost(8 * live * 4 * d * d, 12e6, 2 * live * 4 * d),
    )(sc, *n2s, *gfs, wi, wo, bi)


def swap(value, axis, bit):
    size = lax.axis_size(axis)
    return lax.ppermute(value, axis, [(i, i ^ bit) for i in range(size)])


def by_index(blocks, index):
    return lax.dynamic_index_in_dim(blocks, index, 0, keepdims=False)


def exchange(blocks, stream):
    rel = [by_index(blocks, stream ^ r) for r in range(4)]
    far = swap(jnp.stack([rel[2], rel[3]]), "stream", 2)
    near = swap(jnp.stack([rel[1], far[1]]), "stream", 1)
    got = jnp.stack([rel[0], near[0], far[0], near[1]])
    return jnp.stack([by_index(got, stream ^ r) for r in range(4)])


def gather_rel(value):
    far = swap(value, "stream", 2)
    near = swap(value, "stream", 1)
    both = swap(far, "stream", 1)
    return [value, near, far, both]


def halve_items(value):
    bit = 1
    while bit < lax.axis_size("items"):
        half = value.shape[0] // 2
        value = value[:half] + swap(value[half:], "items", bit)
        bit *= 2
    return value[0]


def gather_quarters(value, stream):
    far = swap(value, "stream", 2)
    pair = jnp.stack([value, far])
    near = swap(pair, "stream", 1)
    got = jnp.stack([pair[0], near[0], pair[1], near[1]])
    return [by_index(got, stream ^ r) for r in range(4)]


def reverse_bits(index, count):
    bits = count.bit_length() - 1
    out = index * 0
    for b in range(bits):
        out = out | (((index >> b) & 1) << (bits - 1 - b))
    return out


def per_device(
    tokens,
    cotangent,
    text_len,
    attn_in,
    attn_bias,
    attn_out,
    out_bias,
    norm_gain,
    norm_bias,
    ffn_in,
    ffn_in_bias,
    ffn_out,
    ffn_out_bias,
):
    streams = lax.axis_size("stream")
    item_devs = lax.axis_size("items")
    stream = lax.axis_index("stream")
    item = lax.axis_index("items")
    _, slots, width = tokens.shape
    hidden = ffn_in.shape[2]
    dm = Dims(slots, streams, width, hidden, item_devs)
    share = dm.share
    flip = reverse_bits(item, item_devs)
    own_len = by_index(text_len, stream)
    sc = jnp.stack([own_len, stream, flip]).astype(jnp.int32)

    x0 = exchange(tokens, stream).reshape(dm.rows, width)
    x0 = jnp.pad(x0, ((0, dm.full - dm.rows), (0, 0)))

    part = hidden // (item_devs * streams)
    wi_q = by_index(
        jnp.moveaxis(ffn_in.reshape(3, width, item_devs, streams, part), 3, 0), stream
    ).reshape(3, width, width)
    wo_q = by_index(
        jnp.moveaxis(ffn_out.reshape(3, item_devs, streams, part, width), 2, 0), stream
    ).reshape(3, width, width)
    bi_q = by_index(
        jnp.moveaxis(ffn_in_bias.reshape(3, item_devs, streams, part), 2, 0), stream
    ).reshape(3, 1, width)

    a0 = fwd_attn(dm, 0, sc, x0, norm_gain, norm_bias, attn_in, attn_bias, attn_out, out_bias)
    n1_0, q_0, k_0, v_0, p_0, ctx_0, x1_0, n2_0, n2l_0 = a0
    n2_all_0 = gather_rel(n2l_0)
    sv_0, sl_0, x2_0 = fwd_ff_two(dm, n2_0, x1_0, ffn_in, ffn_in_bias, ffn_out, ffn_out_bias)
    a1 = fwd_attn(dm, 1, sc, x2_0, norm_gain, norm_bias, attn_in, attn_bias, attn_out, out_bias)
    n1_1, q_1, k_1, v_1, p_1, ctx_1, x1_1, n2_1, n2l_1 = a1
    n2_all_1 = gather_rel(n2l_1)
    s_1, mixed_own = fwd_ff_one(dm, 2, n2_1, x1_1, ffn_in, ffn_in_bias, ffn_out, ffn_out_bias)
    mixed = exchange(mixed_own[: dm.rows].reshape(streams, slots, width), stream)

    cot = exchange(cotangent, stream).reshape(dm.rows, width)[: dm.live]
    row = jnp.arange(dm.live, dtype=jnp.int32)
    live_row = (row < PATCHES) | ((row >= dm.text_at) & (row < dm.text_at + own_len))
    gf_1 = jnp.where(live_row[:, None], cot, jnp.zeros_like(cot))
    gf_all_1 = gather_rel(gf_1)
    g, ga_1, fs_1, hs_1 = back_ff_one(dm, 1, 2, gf_1.astype(F32), gf_1, x1_1, norm_gain, s_1, ffn_in, ffn_out)
    live, vis, lang, text_at = dm.live, dm.vis, dm.lang, dm.text_at
    join = wgrad_ff(dm, ((2, 0, live, 0, live),), sc, n2_all_1, gf_all_1, wi_q[2:3], wo_q[2:3], bi_q[2:3])
    dqkv_1, g, gf_0, as_1 = back_attn(dm, 1, g, ga_1, q_1, k_1, v_1, p_1, x2_0, norm_gain, attn_in, attn_out)
    att_1 = wgrad_attn(dm, sc, n1_1, dqkv_1, ctx_1, ga_1)
    gf_all_0 = gather_rel(gf_0)
    g, ga_0, fs_0, hs_0 = back_ff_two(dm, 0, g, gf_0, x1_0, norm_gain, sv_0, sl_0, ffn_in, ffn_out)
    two = wgrad_ff(
        dm,
        ((0, 0, vis, 0, text_at), (1, lang, live, text_at, live)),
        sc, n2_all_0, gf_all_0, wi_q[0:2], wo_q[0:2], bi_q[0:2],
    )
    dqkv_0, g, _, as_0 = back_attn(dm, 0, g, ga_0, q_0, k_0, v_0, p_0, x0, norm_gain, attn_in, attn_out)
    att_0 = wgrad_attn(dm, sc, n1_0, dqkv_0, ctx_0, ga_0)

    if not in_kernel_shares(dm):
        order = jnp.stack([reverse_bits(jnp.int32(i), item_devs) for i in range(item_devs)]) ^ item

        def reorder(value, lead):
            value = value.reshape(value.shape[:lead] + (item_devs, share, width))
            return jnp.take(value, order, axis=lead)

        join = jnp.moveaxis(reorder(join, 1), 0, 1).reshape(item_devs, 2 * share, width)
        two = jnp.moveaxis(reorder(two, 1), 0, 1).reshape(item_devs, 4 * share, width)
        att_1 = reorder(att_1, 1)
        att_0 = reorder(att_0, 1)

    def halve_stream(value):
        near = swap(jnp.stack([value[1], value[3]]), "stream", 1)
        low = value[0] + near[0]
        high = value[2] + near[1]
        return low + swap(high, "stream", 2)

    join_q = gather_quarters(halve_items(join), stream)
    att_1_q = gather_quarters(halve_items(halve_stream(att_1)), stream)
    two_q = gather_quarters(halve_items(two), stream)
    att_0_q = gather_quarters(halve_items(halve_stream(att_0)), stream)

    def ffn_outs(quarters, base):
        ins = jnp.stack([value[base : base + share] for value in quarters])
        outs = jnp.concatenate([value[base + share : base + 2 * share] for value in quarters], axis=0)
        ins = ins.reshape(streams, share, item_devs, part)
        ins = jnp.transpose(ins, (1, 2, 0, 3)).reshape(share, hidden)
        return ins.astype(F32), outs.astype(F32)

    join_in, join_out = ffn_outs(join_q, 0)
    vis_in, vis_out = ffn_outs(two_q, 0)
    lan_in, lan_out = ffn_outs(two_q, 2 * share)
    attn_in_grad = jnp.stack(
        [jnp.concatenate(att_0_q[:3], axis=-1), jnp.concatenate(att_1_q[:3], axis=-1)]
    ).astype(F32)
    attn_out_grad = jnp.stack([att_0_q[3], att_1_q[3]]).astype(F32)

    def shares(value):
        value = value.reshape(-1, item_devs, value.shape[-1] // item_devs)
        return jnp.moveaxis(value, 1, 0).reshape(item_devs, -1)

    pieces = [
        jnp.stack([as_0[2:4], as_1[2:4]]),
        jnp.stack([fs_0[2], fs_1[2]]),
        jnp.stack([jnp.stack([as_0[0], fs_0[0]]), jnp.stack([as_1[0], fs_1[0]])]),
        jnp.stack([jnp.stack([as_0[1], fs_0[1]]), jnp.stack([as_1[1], fs_1[1]])]),
        jnp.concatenate([hs_0, hs_1], axis=0),
        jnp.concatenate([fs_0[3:5], fs_1[3:4]], axis=0),
    ]
    flat = [shares(value) for value in pieces]
    small = jnp.concatenate(flat, axis=1)
    order = jnp.stack([reverse_bits(jnp.int32(i), item_devs) for i in range(item_devs)]) ^ item
    small = halve_items(jnp.take(small, order, axis=0))
    small = small + swap(small, "stream", 1)
    small = small + swap(small, "stream", 2)
    outs = []
    at = 0
    for value, columns in zip(pieces, flat):
        size = columns.shape[1]
        outs.append(small[at : at + size].reshape(value.shape[:-1] + (value.shape[-1] // item_devs,)))
        at += size

    g = jnp.pad(g.astype(BF), ((0, dm.rows - dm.live), (0, 0)))
    tokens_grad = exchange(g.reshape(streams, slots, width), stream).astype(F32)
    return (
        mixed,
        tokens_grad,
        attn_in_grad,
        outs[0],
        attn_out_grad,
        outs[1],
        outs[2],
        outs[3],
        jnp.stack([vis_in, lan_in, join_in]),
        outs[4],
        jnp.stack([vis_out, lan_out, join_out]),
        outs[5],
    )


def solution(mesh):
    return jax.shard_map(
        per_device,
        mesh=mesh,
        in_specs=(
            P("items", "stream", None),
            P("items", "stream", None),
            P("items"),
            P(),
            P(),
            P(),
            P(),
            P(),
            P(),
            P(),
            P(),
            P(),
            P(),
        ),
        out_specs=(
            P("items", "stream", None),
            P("items", "stream", None),
            P(None, "items", None),
            P(None, None, "items"),
            P(None, "items", None),
            P(None, "items"),
            P(None, None, "items"),
            P(None, None, "items"),
            P(None, "items", None),
            P(None, "items"),
            P(None, "items", None),
            P(None, "items"),
        ),
        check_vma=False,
    )
```

```python
import functools
import jax
import jax.numpy as jnp
from jax import lax
from jax.experimental import pallas as pl
from jax.experimental.pallas import tpu as pltpu
from jax.sharding import PartitionSpec as P

HEADS = 12
PATCHES = 197
TEXT = 40
F32 = jnp.float32
BF = jnp.bfloat16
EPS = 1e-06
FILL = -1e30
MIB = 1 << 20
PAD = 80
TILE = 1024


def dot(left, right, dims=((1,), (0,))):
    return lax.dot_general(left, right, (dims, ((), ())), preferred_element_type=F32)


NT = ((1,), (1,))
TN = ((0,), (0,))


def norm_stats(values):
    row_mean = jnp.mean(values, axis=-1, keepdims=True)
    centred = values - row_mean
    row_var = jnp.mean(centred * centred, axis=-1, keepdims=True)
    inv_std = lax.rsqrt(row_var + EPS)
    return centred * inv_std, inv_std


def norm_back(grad_out, values, gain):
    scaled, inv_std = norm_stats(values)
    grad_scaled = grad_out * gain
    mean_first = jnp.mean(grad_scaled, axis=-1, keepdims=True)
    mean_second = jnp.mean(grad_scaled * scaled, axis=-1, keepdims=True)
    grad_in = inv_std * (grad_scaled - mean_first - scaled * mean_second)
    gain_sum = jnp.sum(grad_out * scaled, axis=0, keepdims=True)
    offset_sum = jnp.sum(grad_out, axis=0, keepdims=True)
    return grad_in, gain_sum, offset_sum


def gelu_parts(pre):
    cumulative = 0.5 * (1.0 + lax.erf(pre * 0.7071067811865476))
    density = jnp.exp(-0.5 * pre * pre) * 0.3989422804014327
    return pre * cumulative, cumulative + pre * density


def params(limit_mib):
    return pltpu.CompilerParams(vmem_limit_bytes=limit_mib * MIB)


def cost():
    return pl.CostEstimate(flops=1, bytes_accessed=1, transcendentals=0)


def whole(shape):
    return pl.BlockSpec(shape, lambda *_: (0,) * len(shape))


def layer_block(shape, index):
    return pl.BlockSpec((1,) + shape, lambda *_: (index,) + (0,) * len(shape))


SMEM = pl.BlockSpec(memory_space=pltpu.SMEM)
ANY = pl.BlockSpec(memory_space=pl.ANY)
sds = jax.ShapeDtypeStruct


def run(body, args, deps=(), *, in_specs, **rest):
    count, extra = len(args), len(deps)

    def wrapped(*refs):
        body(*refs[:count], *refs[count + extra :])

    name = getattr(body, "func", body).__name__
    return pl.pallas_call(wrapped, in_specs=list(in_specs) + [ANY] * extra, name=name, **rest)(*args, *deps)


def first(shape):
    return lax.broadcasted_iota(jnp.int32, shape, 0)


def second(shape):
    return lax.broadcasted_iota(jnp.int32, shape, 1)


class Dims:
    def __init__(self, slots, streams, width, hidden, item_devs):
        self.slots = slots
        self.text_at = slots * (streams - 1)
        self.rows = slots * streams
        self.full = -(-self.rows // 16) * 16
        self.live = -(-(self.text_at + TEXT) // 16) * 16
        self.keys = -(-self.live // 128) * 128
        self.vis = -(-self.text_at // 16) * 16
        self.lang = self.text_at // 16 * 16
        self.width = width
        self.hidden = hidden
        self.streams = streams
        self.item_devs = item_devs
        self.share = width // item_devs
        self.bits = item_devs.bit_length() - 1
        self.order_a = list(range(self.bits))
        self.order_b = self.order_a[1:] + self.order_a[:1]
        self.tiled = self.share % 16 == 0

    def place(self, index, order):
        out = index * 0
        for k, bit in enumerate(order):
            out = out | (((index >> bit) & 1) << (self.bits - 1 - k))
        return out


def put_stage(dm, stage, pieces):
    stage[...] = jnp.zeros_like(stage)
    for r, piece in enumerate(pieces):
        stage[r * PAD : r * PAD + dm.slots] = piece


def slot_select(dm, rows, stream):
    shape = (rows, 4 * PAD)
    slot = first(shape)
    shard = jnp.zeros(shape, jnp.int32)
    for k in range(1, dm.streams):
        shard = shard + (slot >= k * dm.slots).astype(jnp.int32)
    place = slot - shard * dm.slots
    return second(shape) == ((shard ^ stream) * PAD + place), slot


def shard_rows(dm, rows, shard):
    shape = (-(-dm.slots // 8) * 8, rows)
    return ((second(shape) == first(shape) + shard * dm.slots) & (first(shape) < dm.slots)).astype(BF)


def split_shards(dm, value, stream, own, near, far):
    for r, ref in enumerate((own, near, far.at[0], far.at[1])):
        ref[...] = dot(shard_rows(dm, value.shape[0], stream ^ r), value)[: dm.slots].astype(BF)


def cot_prep_body(dm, sc, c0, c1, c2, c3, out, stage):
    stream = sc[1]
    pick, slot = slot_select(dm, dm.live, stream)
    for r in range(4):
        put_stage(dm, stage, [c[stream ^ r] for c in (c0, c1, c2, c3)])
        alive = (slot < PATCHES) | ((slot >= dm.text_at) & (slot < dm.text_at + sc[4 + (stream ^ r)]))
        out[r] = dot((pick & alive).astype(BF), stage[...]).astype(BF)


def cot_prep(dm, sc, pieces, deps):
    shape = pieces[0].shape
    return run(
        functools.partial(cot_prep_body, dm),
        (sc, *pieces),
        deps,
        grid=(1,),
        in_specs=[SMEM] + [whole(shape)] * 4,
        out_specs=whole((4, dm.live, dm.width)),
        out_shape=sds((4, dm.live, dm.width), BF),
        scratch_shapes=[pltpu.VMEM((4 * PAD, dm.width), BF)],
        compiler_params=params(24),
        cost_estimate=cost(),
    )


def join_shards_body(sc, own, near, far, out):
    stream = sc[1]
    for r, value in enumerate((own[...], near[0], far[0], near[1])):
        out[stream ^ r] = value.astype(out.dtype)


def join_shards(dm, sc, own, near, far, dtype):
    shape = (4, dm.slots, dm.width)
    return run(
        join_shards_body,
        (sc, own, near, far),
        grid=(1,),
        in_specs=[SMEM, whole(own.shape), whole(near.shape), whole(far.shape)],
        out_specs=whole(shape),
        out_shape=sds(shape, dtype),
        compiler_params=params(16),
        cost_estimate=cost(),
    )


def select_body(dm, sc, w, b, wo, bo):
    part = dm.hidden // (dm.item_devs * dm.streams)
    for s in range(dm.streams):

        @pl.when(sc[1] == s)
        def _(s=s):
            count = w.shape[2] // (part * dm.streams)
            starts = [i * part * dm.streams + s * part for i in range(count)]
            wo[0] = jnp.concatenate([w[0, :, at : at + part] for at in starts], axis=1)
            bo[0] = jnp.concatenate([b[0, :, at : at + part].astype(F32) for at in starts], axis=1)


def select_quarter(dm, sc, ffn_in, ffn_in_bias):
    d, streams = dm.width, dm.streams
    count = ffn_in.shape[0]
    wide = dm.hidden // 2
    return run(
        functools.partial(select_body, dm),
        (sc, ffn_in, ffn_in_bias[:, None]),
        grid=(count, 2),
        in_specs=[
            SMEM,
            pl.BlockSpec((1, d, wide), lambda e, t: (e, 0, t)),
            pl.BlockSpec((1, 1, wide), lambda e, t: (e, 0, t)),
        ],
        out_specs=[
            pl.BlockSpec((1, d, wide // streams), lambda e, t: (e, 0, t)),
            pl.BlockSpec((1, 1, wide // streams), lambda e, t: (e, 0, t)),
        ],
        out_shape=[sds((count, d, d), BF), sds((count, 1, d), F32)],
        compiler_params=params(24),
        cost_estimate=cost(),
    )

def fwd_attn_body(dm, sc, xv, gain, offset, win, bias, wout, obias, n1o, qo, ko, vo, po, ctxo, x1o, n2o, n2live, ctx_s):
    width = dm.width
    scaled, _ = norm_stats(xv)
    n1 = (scaled * gain[0, 0:1].astype(F32) + offset[0, 0:1].astype(F32)).astype(BF)
    n1o[...] = n1[: dm.live]
    w = win.at[0]
    q = (dot(n1, w[:, 0:width]) + bias[0, 0:1].astype(F32)).astype(BF) * 0.125
    q = q.astype(BF)
    k = dot(n1[: dm.keys], w[:, width : 2 * width]).astype(BF)
    v = (dot(n1[: dm.keys], w[:, 2 * width :]) + bias[0, 1:2].astype(F32)).astype(BF)
    qo[...] = q[: dm.live]
    ko[...] = k
    vo[...] = v
    col = lax.broadcasted_iota(jnp.int32, (1, dm.keys), 1)
    valid = (col < PATCHES) | ((col >= dm.text_at) & (col < dm.text_at + sc[0]))
    low_lane = lax.broadcasted_iota(jnp.int32, (1, 128), 1) < 64
    for pair in range(HEADS // 2):
        lanes = slice(pair * 128, pair * 128 + 128)
        qp, kp, vp = q[:, lanes], k[:, lanes], v[:, lanes]
        outs = []
        for j in range(2):
            qm = jnp.where(low_lane if j == 0 else ~low_lane, qp, jnp.zeros_like(qp))
            scores = jnp.where(valid, dot(qm, kp, NT), FILL)
            top = jnp.max(scores, axis=-1, keepdims=True)
            expo = jnp.exp(scores - top)
            probs = (expo / jnp.sum(expo, axis=-1, keepdims=True)).astype(BF)
            po[2 * pair + j] = probs[: dm.live]
            outs.append(dot(probs, vp))
        ctx_s[:, lanes] = jnp.where(low_lane, outs[0], outs[1]).astype(BF)
    ctx = ctx_s[...]
    ctxo[...] = ctx[: dm.live]
    x1 = xv + (dot(ctx, wout[0]) + obias[0].astype(F32))
    x1o[...] = x1
    scaled, _ = norm_stats(x1)
    n2 = (scaled * gain[0, 1:2].astype(F32) + offset[0, 1:2].astype(F32)).astype(BF)
    n2o[...] = n2
    n2live[...] = n2[: dm.live]


def fwd_attn_next_body(dm, sc, x, *refs):
    fwd_attn_body(dm, sc, x[...], *refs)


def fwd_attn_first_body(dm, sc, tokens, near, far, *refs):
    stream = sc[1]
    *refs, x0, ctx_s, stage = refs
    put_stage(dm, stage, [tokens[stream], near[0], far[stream & 1], near[1]])
    pick, _ = slot_select(dm, dm.full, stream)
    xv = dot(pick.astype(BF), stage[...])
    x0[...] = xv.astype(BF)
    fwd_attn_body(dm, sc, xv, *refs, ctx_s)


def fwd_attn(dm, layer, sc, inputs, norm_gain, norm_bias, attn_in, attn_bias, attn_out, out_bias, deps=()):
    d, full, live, keys = dm.width, dm.full, dm.live, dm.keys
    shapes = [
        sds((live, d), BF),
        sds((live, d), BF),
        sds((keys, d), BF),
        sds((keys, d), BF),
        sds((HEADS, live, keys), BF),
        sds((live, d), BF),
        sds((full, d), F32),
        sds((full, d), BF),
        sds((live, d), BF),
    ]
    scratch = [pltpu.VMEM((full, d), BF)]
    body = fwd_attn_next_body
    if len(inputs) > 1:
        body = fwd_attn_first_body
        shapes.append(sds((full, d), BF))
        scratch.append(pltpu.VMEM((4 * PAD, d), BF))
    return run(
        functools.partial(body, dm),
        (sc, *inputs, norm_gain, norm_bias, attn_in, attn_bias, attn_out, out_bias[:, None]),
        deps,
        grid=(1,),
        in_specs=[SMEM]
        + [whole(value.shape) for value in inputs]
        + [
            layer_block((2, d), layer),
            layer_block((2, d), layer),
            layer_block((d, 3 * d), layer),
            layer_block((2, d), layer),
            layer_block((d, d), layer),
            layer_block((1, d), layer),
        ],
        out_specs=[whole(s.shape) for s in shapes],
        out_shape=shapes,
        scratch_shapes=scratch,
        compiler_params=params(40),
        cost_estimate=cost(),
    )


def fwd_ff_two_body(dm, n2, x1, wv, wl, bi, wov, wol, bo, slope_v, slope_l, x2, acc):
    t = pl.program_id(0)
    vis, lang, text_at = dm.vis, dm.lang, dm.text_at
    rows_v = lax.broadcasted_iota(jnp.int32, (vis, 1), 0) < text_at
    rows_l = lax.broadcasted_iota(jnp.int32, (dm.full - lang, 1), 0) + lang >= text_at
    act_v, sv = gelu_parts(dot(n2[0:vis], wv[0]) + bi[0, 0:1].astype(F32))
    act_l, sl = gelu_parts(dot(n2[lang:], wl[0]) + bi[1, 0:1].astype(F32))
    slope_v[...] = sv.astype(BF)
    slope_l[...] = sl[: dm.live - lang].astype(BF)
    part_v = dot(act_v.astype(BF), wov[0])
    part_l = dot(act_l.astype(BF), wol[0])

    @pl.when(t == 0)
    def _():
        acc[...] = x1[...]
        part_vb = part_v + bo[0, 0:1].astype(F32)
        part_lb = part_l + bo[1, 0:1].astype(F32)
        acc[0:vis] += jnp.where(rows_v, part_vb, 0.0)
        acc[lang:] += jnp.where(rows_l, part_lb, 0.0)

    @pl.when(t > 0)
    def _():
        acc[0:vis] += jnp.where(rows_v, part_v, 0.0)
        acc[lang:] += jnp.where(rows_l, part_l, 0.0)

    @pl.when(t == pl.num_programs(0) - 1)
    def _():
        x2[...] = acc[...]


def fwd_ff_two(dm, n2, x1, ffn_in, ffn_in_bias, ffn_out, ffn_out_bias, deps=()):
    d, full, hid = dm.width, dm.full, dm.hidden
    count = ffn_in.shape[0]
    return run(
        functools.partial(fwd_ff_two_body, dm),
        (n2, x1, ffn_in, ffn_in, ffn_in_bias[:, None], ffn_out, ffn_out, ffn_out_bias[:, None]),
        deps,
        grid=(hid // TILE,),
        in_specs=[
            whole((full, d)),
            whole((full, d)),
            pl.BlockSpec((1, d, TILE), lambda t: (0, 0, t)),
            pl.BlockSpec((1, d, TILE), lambda t: (1, 0, t)),
            pl.BlockSpec((count, 1, TILE), lambda t: (0, 0, t)),
            pl.BlockSpec((1, TILE, d), lambda t: (0, t, 0)),
            pl.BlockSpec((1, TILE, d), lambda t: (1, t, 0)),
            whole((count, 1, d)),
        ],
        out_specs=[
            pl.BlockSpec((dm.vis, TILE), lambda t: (0, t)),
            pl.BlockSpec((dm.live - dm.lang, TILE), lambda t: (0, t)),
            whole((full, d)),
        ],
        out_shape=[sds((dm.vis, hid), BF), sds((dm.live - dm.lang, hid), BF), sds((full, d), F32)],
        scratch_shapes=[pltpu.VMEM((full, d), F32)],
        compiler_params=params(40),
        cost_estimate=cost(),
    )


def finish_ff_back(dm, g, gn, x1, gain, go, ga, sums):
    grad_in, gain_sum, offset_sum = norm_back(gn, x1[0 : dm.live], gain[0, 1:2].astype(F32))
    out = g + grad_in
    go[...] = out
    low = out.astype(BF)
    ga[...] = low
    sums[0:1] = gain_sum
    sums[1:2] = offset_sum
    sums[2:3] = jnp.sum(low.astype(F32), axis=0, keepdims=True)


def top_ff_body(dm, sc, n2, gf, x1, gain, wi, bi, wo, bo, own, near, far, go, ga, sums, hsum, accm, accg):
    t = pl.program_id(0)
    act, slope = gelu_parts(dot(n2[...], wi[0]) + bi[0].astype(F32))
    gpre = (dot(gf[0], wo[0], NT) * slope[: dm.live]).astype(BF)
    hsum[...] = jnp.sum(gpre.astype(F32), axis=0, keepdims=True)
    part = dot(act.astype(BF), wo[0])
    back = dot(gpre, wi[0], NT)

    @pl.when(t == 0)
    def _():
        accm[...] = part + (x1[...] + bo[0].astype(F32))
        accg[...] = back

    @pl.when(t > 0)
    def _():
        accm[...] += part
        accg[...] += back

    @pl.when(t == pl.num_programs(0) - 1)
    def _():
        split_shards(dm, accm[...].astype(BF), sc[1], own, near, far)
        g = gf[0].astype(F32)
        sums[3:4] = jnp.sum(g, axis=0, keepdims=True)
        finish_ff_back(dm, g, accg[...], x1, gain, go, ga, sums)


def top_ff(dm, layer, expert, sc, n2, gf, x1, norm_gain, ffn_in, ffn_in_bias, ffn_out, ffn_out_bias, deps=()):
    d, full, live, hid, slots = dm.width, dm.full, dm.live, dm.hidden, dm.slots
    shapes = [
        sds((slots, d), BF),
        sds((slots, d), BF),
        sds((2, slots, d), BF),
        sds((live, d), F32),
        sds((live, d), BF),
        sds((4, d), F32),
    ]
    return run(
        functools.partial(top_ff_body, dm),
        (sc, n2, gf, x1, norm_gain, ffn_in, ffn_in_bias[:, None], ffn_out, ffn_out_bias[:, None]),
        deps,
        grid=(hid // TILE,),
        in_specs=[
            SMEM,
            whole((full, d)),
            layer_block((live, d), 0),
            whole((full, d)),
            layer_block((2, d), layer),
            pl.BlockSpec((1, d, TILE), lambda t: (expert, 0, t)),
            pl.BlockSpec((1, 1, TILE), lambda t: (expert, 0, t)),
            pl.BlockSpec((1, TILE, d), lambda t: (expert, t, 0)),
            layer_block((1, d), expert),
        ],
        out_specs=[whole(s.shape) for s in shapes] + [pl.BlockSpec((1, TILE), lambda t: (0, t))],
        out_shape=shapes + [sds((1, hid), F32)],
        scratch_shapes=[pltpu.VMEM((full, d), F32), pltpu.VMEM((live, d), F32)],
        compiler_params=params(44),
        cost_estimate=cost(),
    )


def back_ff_two_body(dm, g, gf, x1, gain, slv, sll, wov, wol, wv, wl, go, ga, sums, hsum, acc):
    t = pl.program_id(0)
    vis, lang, text_at, live = dm.vis, dm.lang, dm.text_at, dm.live
    rows_v = lax.broadcasted_iota(jnp.int32, (vis, 1), 0) < text_at
    rows_l = lax.broadcasted_iota(jnp.int32, (live - lang, 1), 0) + lang >= text_at
    gv = jnp.where(rows_v, gf[0:vis].astype(F32), 0.0)
    gl = jnp.where(rows_l, gf[lang:].astype(F32), 0.0)
    pre_v = (dot(gv.astype(BF), wov[0], NT) * slv[...].astype(F32)).astype(BF)
    pre_l = (dot(gl.astype(BF), wol[0], NT) * sll[...].astype(F32)).astype(BF)
    hsum[0:1] = jnp.sum(pre_v.astype(F32), axis=0, keepdims=True)
    hsum[1:2] = jnp.sum(pre_l.astype(F32), axis=0, keepdims=True)
    part_v = dot(pre_v, wv[0], NT)
    part_l = dot(pre_l, wl[0], NT)

    @pl.when(t == 0)
    def _():
        acc[...] = jnp.zeros_like(acc)

    acc[0:vis] += part_v
    acc[lang:] += part_l

    @pl.when(t == pl.num_programs(0) - 1)
    def _():
        sums[3:4] = jnp.sum(gv, axis=0, keepdims=True)
        sums[4:5] = jnp.sum(gl, axis=0, keepdims=True)
        finish_ff_back(dm, g[...], acc[...], x1, gain, go, ga, sums)


def back_ff_two(dm, layer, g, gf, x1, norm_gain, slope_v, slope_l, ffn_in, ffn_out, deps=()):
    d, live, hid = dm.width, dm.live, dm.hidden
    return run(
        functools.partial(back_ff_two_body, dm),
        (g, gf, x1, norm_gain, slope_v, slope_l, ffn_out, ffn_out, ffn_in, ffn_in),
        deps,
        grid=(hid // TILE,),
        in_specs=[
            whole((live, d)),
            whole((live, d)),
            whole((dm.full, d)),
            layer_block((2, d), layer),
            pl.BlockSpec((dm.vis, TILE), lambda t: (0, t)),
            pl.BlockSpec((live - dm.lang, TILE), lambda t: (0, t)),
            pl.BlockSpec((1, TILE, d), lambda t: (0, t, 0)),
            pl.BlockSpec((1, TILE, d), lambda t: (1, t, 0)),
            pl.BlockSpec((1, d, TILE), lambda t: (0, 0, t)),
            pl.BlockSpec((1, d, TILE), lambda t: (1, 0, t)),
        ],
        out_specs=[
            whole((live, d)),
            whole((live, d)),
            whole((5, d)),
            pl.BlockSpec((2, TILE), lambda t: (0, t)),
        ],
        out_shape=[sds((live, d), F32), sds((live, d), BF), sds((5, d), F32), sds((2, hid), F32)],
        scratch_shapes=[pltpu.VMEM((live, d), F32)],
        compiler_params=params(40),
        cost_estimate=cost(),
    )


def back_attn_body(dm, bottom, sc, g, ga, q, k, v, p, x, gain, win, wout, dqkv, sums, *outs):
    width, live = dm.width, dm.live
    gc = dot(ga[...], wout[0], NT).astype(BF)
    low_lane = lax.broadcasted_iota(jnp.int32, (1, 128), 1) < 64
    for pair in range(HEADS // 2):
        lanes = slice(pair * 128, pair * 128 + 128)
        gp, qp, kp, vp = gc[:, lanes], q[:, lanes], k[:, lanes], v[:, lanes]
        dqs, dks, dvs = [], [], []
        for j in range(2):
            gm = jnp.where(low_lane if j == 0 else ~low_lane, gp, jnp.zeros_like(gp))
            dprob = dot(gm, vp, NT)
            prob_low = p[2 * pair + j]
            prob = prob_low.astype(F32)
            inner = jnp.sum(prob * dprob, axis=-1, keepdims=True)
            ds = (prob * (dprob - inner)).astype(BF)
            dqs.append(dot(ds, kp))
            dks.append(dot(ds, qp, TN))
            dvs.append(dot(prob_low, gp, TN))
        dq = jnp.where(low_lane, dqs[0], dqs[1]) * 0.125
        dk = jnp.where(low_lane, dks[0], dks[1])
        dv = jnp.where(low_lane, dvs[0], dvs[1])
        dqkv[:, pair * 128 : pair * 128 + 128] = dq.astype(BF)
        dqkv[:, width + pair * 128 : width + pair * 128 + 128] = dk[:live].astype(BF)
        dqkv[:, 2 * width + pair * 128 : 2 * width + pair * 128 + 128] = dv[:live].astype(BF)
    packed = dqkv[...]
    gn = dot(packed, win[0], NT)
    grad_in, gain_sum, offset_sum = norm_back(gn, x[0:live].astype(F32), gain[0, 0:1].astype(F32))
    out = g[...] + grad_in
    if bottom:
        split_shards(dm, out.astype(BF), sc[1], *outs)
    else:
        outs[0][...] = out
        outs[1][...] = out.astype(BF)
    sums[0:1] = gain_sum
    sums[1:2] = offset_sum
    sums[2:3] = jnp.sum(packed[:, 0:width].astype(F32), axis=0, keepdims=True)
    sums[3:4] = jnp.sum(packed[:, 2 * width :].astype(F32), axis=0, keepdims=True)


def back_attn(dm, layer, sc, g, ga, q, k, v, p, x, norm_gain, attn_in, attn_out, deps=()):
    d, live, keys, slots = dm.width, dm.live, dm.keys, dm.slots
    bottom = layer == 0
    shapes = [sds((live, 3 * d), BF), sds((4, d), F32)]
    if bottom:
        shapes += [sds((slots, d), BF), sds((slots, d), BF), sds((2, slots, d), BF)]
    else:
        shapes += [sds((live, d), F32), sds((live, d), BF)]
    return run(
        functools.partial(back_attn_body, dm, bottom),
        (sc, g, ga, q, k, v, p, x, norm_gain, attn_in, attn_out),
        deps,
        grid=(1,),
        in_specs=[
            SMEM,
            whole((live, d)),
            whole((live, d)),
            whole((live, d)),
            whole((keys, d)),
            whole((keys, d)),
            whole((HEADS, live, keys)),
            whole((dm.full, d)),
            layer_block((2, d), layer),
            layer_block((d, 3 * d), layer),
            layer_block((d, d), layer),
        ],
        out_specs=[whole(s.shape) for s in shapes],
        out_shape=shapes,
        compiler_params=params(40),
        cost_estimate=cost(),
    )


def store_shares(dm, refs, row, value, order, flip, stage):
    keep, send = refs
    n, share = dm.item_devs, dm.share
    half = n // 2
    for i in range(n):
        stage[i] = value[i * share : (i + 1) * share]
    for p in range(n):
        ref = keep if p < half else send
        index = unplace(dm, p ^ flip, order)
        ref[p % half, row : row + share] = stage[index]


def unplace(dm, place, order):
    out = place * 0
    for k, bit in enumerate(order):
        out = out | (((place >> (dm.bits - 1 - k)) & 1) << bit)
    return out


def wgrad_attn_body(dm, sc, n1, dqkv, ctx, ga, near, own, left, right):
    width = dm.width
    left[0] = n1[...]
    left[1] = ctx[...]
    for quarter in range(3):
        right[quarter] = dqkv[:, quarter * width : (quarter + 1) * width]
    right[3] = ga[...]
    for r in (1, 3, 0, 2):
        ref = near if r & 1 else own
        quarter = sc[1] ^ r
        value = dot(left[jnp.where(quarter == 3, 1, 0)], right[quarter], TN).astype(BF)
        if dm.tiled:
            for i in range(dm.item_devs):
                at = (r // 2, dm.place(i, dm.order_a) ^ sc[2])
                ref[at] = value[i * dm.share : (i + 1) * dm.share]
        else:
            ref[r // 2] = value


def wgrad_attn(dm, sc, n1, dqkv, ctx, ga, deps=()):
    d, live, n, share = dm.width, dm.live, dm.item_devs, dm.share
    shape = (2, n, share, d) if dm.tiled else (2, d, d)
    return run(
        functools.partial(wgrad_attn_body, dm),
        (sc, n1, dqkv, ctx, ga),
        deps,
        grid=(1,),
        in_specs=[SMEM, whole((live, d)), whole((live, 3 * d)), whole((live, d)), whole((live, d))],
        out_specs=[whole(shape)] * 2,
        out_shape=[sds(shape, BF)] * 2,
        scratch_shapes=[pltpu.VMEM((2, live, d), BF), pltpu.VMEM((4, live, d), BF)],
        compiler_params=params(40),
        cost_estimate=cost(),
    )


def wgrad_ff_body(dm, experts, stacked, sc, *refs):
    d, streams = dm.width, dm.streams
    n2s = refs[0:streams]
    gfs, refs = ([refs[streams].at[r] for r in range(streams)], refs[streams + 1 :]) if stacked else (refs[streams : 2 * streams], refs[2 * streams :])
    count = len(experts)
    wi, wo, bi = refs[:3]
    outs = refs[3 : 3 + 2 * count]
    n2a, gfa, acta, gpa, stage = refs[3 + 2 * count :]
    for index, (expert, start, stop, low, high, order) in enumerate(experts):
        size = stop - start
        total = size * streams
        rows = first((size, 1)) + start
        keep = (rows >= low) & (rows < high)
        for r in range(streams):
            n2a[r * size : (r + 1) * size] = n2s[r][start:stop]
            gpart = gfs[r][start:stop]
            if low > start or high < stop:
                gpart = jnp.where(keep, gpart.astype(F32), 0.0).astype(BF)
            gfa[r * size : (r + 1) * size] = gpart
        chunk = size if size >= 128 else total
        wi_e = wi.at[index]
        wo_e = wo[index].reshape(d, d)

        def step(c, carry, chunk=chunk, wi_e=wi_e, wo_e=wo_e, index=index):
            at = pl.ds(pl.multiple_of(c * chunk, 16), chunk)
            act, slope = gelu_parts(dot(n2a[at], wi_e[...]) + bi[index])
            acta[at] = act.astype(BF)
            gpa[at] = (dot(gfa[at], wo_e, NT) * slope).astype(BF)
            return carry

        lax.fori_loop(0, total // chunk, step, 0)
        for side, (left, right) in enumerate(((n2a, gpa), (acta, gfa))):
            value = dot(left[0:total], right[0:total], TN).astype(BF)
            if dm.tiled:
                store_shares(dm, outs[2 * index : 2 * index + 2], side * dm.share, value, order, sc[2] if order is dm.order_a else sc[3], stage)
            else:
                outs[2 * index + side][...] = value


def wgrad_ff(dm, experts, sc, n2s, gfs, wi, wo, bi, deps=()):
    d, live, n, share, streams = dm.width, dm.live, dm.item_devs, dm.share, dm.streams
    count = len(experts)
    base = experts[0][0]
    part = d // n
    stacked = len(gfs) == 1
    shape = (n // 2, 2 * share, d) if dm.tiled else (d, d)
    top = max(e[2] - e[1] for e in experts) * streams
    if dm.tiled:
        wo = wo.reshape(wo.shape[0], n, streams, part, d)
        wo_spec = pl.BlockSpec((count, n, None, part, d), lambda t, s: (base // count, 0, s[1], 0, 0))
    else:
        wo_spec = pl.BlockSpec((count, d, d), lambda t, s: (base // count, 0, 0))

    body = functools.partial(wgrad_ff_body, dm, experts, stacked)
    extra = len(deps)
    args = (*n2s, *gfs, wi, wo, bi)

    def wrapped(*refs):
        body(*refs[: 1 + len(args)], *refs[1 + len(args) + extra :])

    gf_specs = [pl.BlockSpec((streams, live, d), lambda t, s: (0, 0, 0))] if stacked else [pl.BlockSpec((live, d), lambda t, s: (0, 0))] * streams
    return pl.pallas_call(
        wrapped,
        grid_spec=pltpu.PrefetchScalarGridSpec(
            num_scalar_prefetch=1,
            grid=(1,),
            in_specs=[pl.BlockSpec((live, d), lambda t, s: (0, 0))] * streams
            + gf_specs
            + [
                pl.BlockSpec((count, d, d), lambda t, s: (base // count, 0, 0)),
                wo_spec,
                pl.BlockSpec((count, 1, d), lambda t, s: (base // count, 0, 0)),
            ]
            + [ANY] * extra,
            out_specs=[pl.BlockSpec(shape, lambda t, s: (0,) * len(shape))] * (2 * count),
            scratch_shapes=[pltpu.VMEM((top, d), BF)] * 4 + [pltpu.VMEM((n, share, d), BF)],
        ),
        out_shape=[sds(shape, BF)] * (2 * count),
        compiler_params=params(48),
        cost_estimate=cost(),
        name="wgrad_ff_body",
    )(sc, *args, *deps)


def finish_body(dm, experts, layers, first_rows, sc, own, near, far, both, *refs):
    share, part = dm.share, dm.hidden // (dm.item_devs * dm.streams)
    stage = refs[-1]
    outs = list(refs[-1 - 2 * bool(experts) - 2 * bool(layers) : -1])
    for r, piece in enumerate((own, near, far, both)):
        stage[sc[1] ^ r] = piece[...]
    at = 0
    if experts:
        ins, results = outs.pop(0), outs.pop(0)
        for index in range(experts):
            for i in range(dm.item_devs):
                lanes = slice(i * part, (i + 1) * part)
                block = [stage[q, at : at + share, lanes].astype(F32) for q in range(4)]
                ins[index, :, i * 4 * part : (i + 1) * 4 * part] = jnp.concatenate(block, axis=1)
            for q in range(4):
                results[index, q * share : (q + 1) * share] = stage[q, at + share : at + 2 * share].astype(F32)
            at += 2 * share
    if layers:
        packed, results = outs
        for index in range(layers):
            for q in range(3):
                packed[index, :, q * dm.width : (q + 1) * dm.width] = stage[q, at : at + share].astype(F32)
            results[index] = stage[3, at : at + share].astype(F32)
            at += share


def finish(dm, sc, pieces, experts, expert_at, layers, layer_at, bases, *deps):
    share, d, hid = dm.share, dm.width, dm.hidden
    shapes, specs = [], []
    if experts:
        shapes += [sds((3, share, hid), F32), sds((3, 4 * share, d), F32)]
        specs += [
            pl.BlockSpec((experts, share, hid), lambda t: (expert_at, 0, 0)),
            pl.BlockSpec((experts, 4 * share, d), lambda t: (expert_at, 0, 0)),
        ]
    if layers:
        shapes += [sds((2, share, 3 * d), F32), sds((2, share, d), F32)]
        specs += [
            pl.BlockSpec((layers, share, 3 * d), lambda t: (layer_at, 0, 0)),
            pl.BlockSpec((layers, share, d), lambda t: (layer_at, 0, 0)),
        ]
    rows = pieces[0].shape[0]
    extra = len(bases)

    def body(*refs):
        finish_body(dm, experts, layers, rows, *refs[:5], *refs[5 + extra + len(deps) :])

    return pl.pallas_call(
        body,
        grid=(1,),
        in_specs=[SMEM] + [whole((rows, d))] * 4 + [ANY] * (extra + len(deps)),
        out_specs=specs,
        out_shape=shapes,
        scratch_shapes=[pltpu.VMEM((4, rows, d), BF)],
        input_output_aliases={5 + k: k for k in range(extra)},
        compiler_params=params(40),
        cost_estimate=cost(),
        name="finish_body",
    )(sc, *pieces, *bases, *deps)


SMALL_ROWS = 32


def small_body(dm, sc, a0, a1, f0, f1, h0, h1, out):
    out[...] = jnp.zeros_like(out)
    share = dm.share
    wide = jnp.concatenate(
        [
            a0[2:4], a1[2:4],
            f0[2:3], f1[2:3],
            a0[0:1], f0[0:1], a1[0:1], f1[0:1],
            a0[1:2], f0[1:2], a1[1:2], f1[1:2],
            f0[3:5], f1[3:4],
        ],
        axis=0,
    )
    hidden = jnp.concatenate([h0[...], h1[...]], axis=0)
    count = wide.shape[0]
    for i in range(dm.item_devs):
        place = dm.place(i, dm.order_a) ^ sc[2]
        out[place, 0:count, 0:share] = wide[:, i * share : (i + 1) * share]
        for q in range(4):
            at = (i * 4 + q) * share
            out[place, count + 3 * q : count + 3 * q + 3, 0:share] = hidden[:, at : at + share]


def small_pack(dm, sc, values, deps):
    shape = (dm.item_devs, SMALL_ROWS, 128)
    return run(
        functools.partial(small_body, dm),
        (sc, *values),
        deps,
        grid=(1,),
        in_specs=[SMEM] + [whole(value.shape) for value in values],
        out_specs=whole(shape),
        out_shape=sds(shape, F32),
        compiler_params=params(16),
        cost_estimate=cost(),
    )


def small_out_body(dm, near, far, attn_bias, out_bias, gain, offset, hidden, ffn_bias):
    share = dm.share
    total = near[:, 0:share] + far[:, 0:share]
    for l in range(2):
        attn_bias[l] = total[2 * l : 2 * l + 2]
        gain[l] = total[6 + 2 * l : 8 + 2 * l]
        offset[l] = total[10 + 2 * l : 12 + 2 * l]
    out_bias[...] = total[4:6]
    ffn_bias[...] = total[14:17]
    hidden[...] = jnp.concatenate([total[17 + 3 * q : 20 + 3 * q] for q in range(4)], axis=1)


def small_unpack(dm, near, far, *deps):
    share = dm.share
    shapes = [(2, 2, share), (2, share), (2, 2, share), (2, 2, share), (3, 4 * share), (3, share)]
    return run(
        functools.partial(small_out_body, dm),
        (near, far),
        deps,
        grid=(1,),
        in_specs=[whole(near.shape)] * 2,
        out_specs=[whole(shape) for shape in shapes],
        out_shape=[sds(shape, F32) for shape in shapes],
        compiler_params=params(16),
        cost_estimate=cost(),
    )


def swap(value, axis, bit):
    size = lax.axis_size(axis)
    return lax.ppermute(value, axis, [(i, i ^ bit) for i in range(size)])


def by_index(blocks, index):
    return lax.dynamic_index_in_dim(blocks, index, 0, keepdims=False)


def gather_start(value):
    return [value, swap(value, "stream", 1), swap(value, "stream", 2)]


def gather_end(parts, *later):
    far = after(parts[2], *later) if later else parts[2]
    return parts + [swap(far, "stream", 1)]


def gather_rel(value):
    return gather_end(gather_start(value))


def after(value, *others):
    return lax.optimization_barrier((value, *others))[0]


def add_up(values):
    total = values[0].astype(F32)
    for value in values[1:]:
        total = total + value.astype(F32)
    return total


def add_body(count, *refs):
    refs[count][...] = add_up([ref[...] for ref in refs[:count]]).astype(refs[count].dtype)


def add_part(terms, size, index, deps=()):
    shape = (size,) + terms[0].shape[1:]
    return run(
        functools.partial(add_body, len(terms)),
        terms,
        deps,
        grid=(1,),
        in_specs=[pl.BlockSpec(shape, lambda t: (index, 0, 0))] * len(terms),
        out_specs=whole(shape),
        out_shape=sds(shape, terms[0].dtype),
        compiler_params=params(24),
        cost_estimate=cost(),
    )


def pieces_body(counts, *refs):
    out = refs[-1]
    row = at = 0
    for count in counts:
        terms = refs[at : at + count]
        rows = terms[0].shape[1]
        out[row : row + rows] = add_up([term[0] for term in terms]).astype(out.dtype)
        at += count
        row += rows


def add_pieces(sums, deps=()):
    terms = [term for value in sums for term in value.terms]
    rows = sum(value.terms[0].shape[1] for value in sums)
    shape = (rows, terms[0].shape[2])
    return run(
        functools.partial(pieces_body, [len(value.terms) for value in sums]),
        terms,
        deps,
        grid=(1,),
        in_specs=[pl.BlockSpec((1,) + term.shape[1:], lambda t: (0, 0, 0)) for term in terms],
        out_specs=whole(shape),
        out_shape=sds(shape, terms[0].dtype),
        compiler_params=params(24),
        cost_estimate=cost(),
    )


class Halving:
    def __init__(self, order, terms, size, send=None, deps=()):
        self.order = list(order)
        self.terms = list(terms)
        self.size = size
        if send is None:
            self.more(deps)
        else:
            self.send(send)

    def send(self, value):
        self.size //= 2
        self.last = value
        self.terms.append(swap(value, "items", 1 << self.order.pop(0)))

    def more(self, deps=()):
        if self.order:
            self.send(add_part(self.terms, self.size // 2, 1, deps))
        return self.last

    def drain(self):
        while self.order:
            self.more()
        return self


def per_device(
    tokens,
    cotangent,
    text_len,
    attn_in,
    attn_bias,
    attn_out,
    out_bias,
    norm_gain,
    norm_bias,
    ffn_in,
    ffn_in_bias,
    ffn_out,
    ffn_out_bias,
):
    streams = lax.axis_size("stream")
    item_devs = lax.axis_size("items")
    stream = lax.axis_index("stream")
    item = lax.axis_index("items")
    _, slots, width = tokens.shape
    hidden = ffn_in.shape[2]
    dm = Dims(slots, streams, width, hidden, item_devs)
    share = dm.share
    sc = jnp.stack([by_index(text_len, stream), stream, dm.place(item, dm.order_a), dm.place(item, dm.order_b)])
    sc = jnp.concatenate([sc, text_len]).astype(jnp.int32)

    far = swap(lax.dynamic_slice_in_dim(tokens, 2 * (1 - stream // 2), 2, 0), "stream", 2)
    near = swap(jnp.stack([by_index(tokens, stream ^ 1), by_index(far, 1 - stream % 2)]), "stream", 1)
    cots = gather_start(after(cotangent, near))

    part = hidden // (item_devs * streams)
    if dm.tiled:
        wi_q, bi_q = select_quarter(dm, sc, ffn_in, ffn_in_bias)
        wo_q = ffn_out
    else:
        wi_q = by_index(jnp.moveaxis(ffn_in.reshape(3, width, item_devs, streams, part), 3, 0), stream).reshape(3, width, width)
        wo_q = by_index(jnp.moveaxis(ffn_out.reshape(3, item_devs, streams, part, width), 2, 0), stream).reshape(3, width, width)
        bi_q = by_index(jnp.moveaxis(ffn_in_bias.reshape(3, item_devs, streams, part), 2, 0), stream).reshape(3, 1, width).astype(F32)

    layer_params = (norm_gain, norm_bias, attn_in, attn_bias, attn_out, out_bias)
    a0 = fwd_attn(dm, 0, sc, (tokens, near, far), *layer_params, deps=(bi_q,))
    n1_0, q_0, k_0, v_0, p_0, ctx_0, x1_0, n2_0, n2l_0, x_0 = a0
    cots = gather_end(cots, n2l_0)
    n2_all_0 = gather_start(n2l_0)
    sv_0, sl_0, x_1 = fwd_ff_two(dm, n2_0, x1_0, ffn_in, ffn_in_bias, ffn_out, ffn_out_bias)
    gf_all_1 = cot_prep(dm, sc, cots, (sv_0,))
    a1 = fwd_attn(dm, 1, sc, (x_1,), *layer_params, deps=(gf_all_1,))
    n1_1, q_1, k_1, v_1, p_1, ctx_1, x1_1, n2_1, n2l_1 = a1
    n2_all_0 = gather_end(n2_all_0, n2l_1)
    n2_all_1 = gather_start(n2l_1)
    mix_own, mix_near, mix_far, g, ga_1, fs_1, hs_1 = top_ff(
        dm, 1, 2, sc, n2_1, gf_all_1, x1_1, norm_gain, ffn_in, ffn_in_bias, ffn_out, ffn_out_bias
    )

    n2_all_1 = gather_end(n2_all_1, fs_1)

    def send_shards(own, near, far, dtype):
        far = swap(far, "stream", 2)
        near = swap(jnp.stack([near, far[1]]), "stream", 1)
        return join_shards(dm, sc, own, near, far, dtype)

    live, vis, lang, text_at = dm.live, dm.vis, dm.lang, dm.text_at

    def reorder(value, order):
        places = jnp.stack([dm.place(jnp.int32(i), order) for i in range(item_devs)])
        source = jnp.zeros((item_devs,), jnp.int32).at[places ^ dm.place(item, order)].set(jnp.arange(item_devs, dtype=jnp.int32))
        value = value.reshape(value.shape[:-2] + (item_devs, share, width))
        return jnp.take(value, source, axis=value.ndim - 3)

    def ff_halves(pair, order):
        if not dm.tiled:
            value = jnp.concatenate([reorder(side, order) for side in pair], axis=1)
            pair = value[: item_devs // 2], value[item_devs // 2 :]
        return Halving(order, [pair[0]], item_devs, pair[1])

    def attn_near(near, own):
        if not dm.tiled:
            near, own = reorder(near, dm.order_a), reorder(own, dm.order_a)
        near = swap(near, "stream", 1)
        return [value.reshape((-1,) + value.shape[2:]) for value in (own, near)]

    def attn_far(terms, deps):
        send = add_part(terms, item_devs, 1, deps)
        return [*terms, swap(send, "stream", 2)], send

    join = wgrad_ff(dm, ((2, 0, live, 0, live, dm.order_a),), sc, n2_all_1, (gf_all_1,), wi_q, wo_q, bi_q, deps=(fs_1,))
    join_sum = ff_halves(join, dm.order_a)
    mixed = send_shards(mix_own, mix_near, mix_far, BF)
    dqkv_1, as_1, g, gf_0 = back_attn(
        dm, 1, sc, g, ga_1, q_1, k_1, v_1, p_1, x_1, norm_gain, attn_in, attn_out, deps=(join[0],)
    )
    gf_all_0 = gather_start(gf_0)
    att_1 = wgrad_attn(dm, sc, n1_1, dqkv_1, ctx_1, ga_1)
    att_1_terms = attn_near(*att_1)
    g, ga_0, fs_0, hs_0 = back_ff_two(dm, 0, g, gf_0, x1_0, norm_gain, sv_0, sl_0, ffn_in, ffn_out, deps=(att_1[0],))
    gf_all_0 = gather_end(gf_all_0, fs_0)
    att_1_terms, last = attn_far(att_1_terms, (fs_0,))
    two = wgrad_ff(
        dm,
        ((0, 0, vis, 0, text_at, dm.order_a), (1, lang, live, text_at, live, dm.order_b)),
        sc, n2_all_0, gf_all_0, wi_q, wo_q, bi_q, deps=(last,),
    )
    vis_sum = ff_halves(two[0:2], dm.order_a)
    lan_sum = ff_halves(two[2:4], dm.order_b)
    last = join_sum.more((two[0],))
    dqkv_0, as_0, tg_own, tg_near, tg_far = back_attn(
        dm, 0, sc, g, ga_0, q_0, k_0, v_0, p_0, x_0, norm_gain, attn_in, attn_out, deps=(last,)
    )
    att_0 = wgrad_attn(dm, sc, n1_0, dqkv_0, ctx_0, ga_0)
    small = small_pack(dm, sc, (as_0, as_1, fs_0, fs_1, hs_0, hs_1), (att_0[0],))
    att_0_terms, last = attn_far(attn_near(*att_0), (small,))
    att_1_sum = Halving(dm.order_a, att_1_terms, item_devs, deps=(last,))
    tokens_grad = send_shards(tg_own, tg_near, tg_far, F32)
    half = item_devs // 2
    small_sum = Halving(dm.order_a, [small[:half]], item_devs, after(small[half:], last))
    last = join_sum.more((att_1_sum.last,))
    last = lan_sum.more((last,))
    last = small_sum.more((last,))
    last = vis_sum.more((last,))
    join_piece = add_pieces([join_sum.drain()], deps=(last,))
    join_all = gather_start(join_piece)
    last = att_1_sum.more((join_piece,))
    att_0_sum = Halving(dm.order_a, att_0_terms, item_devs, deps=(last,))
    last = small_sum.more((att_0_sum.last,))
    join_all = gather_end(join_all, last)
    results = finish(dm, sc, join_all, 1, 2, 0, 0, (), last)
    last = lan_sum.more((results[0],))
    last = att_1_sum.more((last,))
    last = vis_sum.more((last,))
    last = att_0_sum.more((last,))
    small_own = add_pieces([small_sum.drain()], deps=(last,))
    small_near = small_own + swap(small_own, "stream", 1)
    small_all = swap(small_near, "stream", 2)
    middle = add_pieces([vis_sum.drain(), lan_sum.drain(), att_1_sum.drain()], deps=(last,))
    middle_all = gather_start(middle)
    last = att_0_sum.more((middle,))
    middle_all = gather_end(middle_all, last)
    results = finish(dm, sc, middle_all, 2, 0, 1, 1, results, last)
    ffn_results = results[0:2]
    outs = small_unpack(dm, small_near, small_all, results[0])
    bottom = add_pieces([att_0_sum.drain()], deps=(outs[0],))
    attn_results = finish(dm, sc, gather_rel(bottom), 0, 0, 1, 0, results[2:4])

    return (
        mixed,
        tokens_grad,
        attn_results[0],
        outs[0],
        attn_results[1],
        outs[1],
        outs[2],
        outs[3],
        ffn_results[0],
        outs[4],
        ffn_results[1],
        outs[5],
    )


def solution(mesh):
    return jax.shard_map(
        per_device,
        mesh=mesh,
        in_specs=(
            P("items", "stream", None),
            P("items", "stream", None),
            P("items"),
            P(),
            P(),
            P(),
            P(),
            P(),
            P(),
            P(),
            P(),
            P(),
            P(),
        ),
        out_specs=(
            P("items", "stream", None),
            P("items", "stream", None),
            P(None, "items", None),
            P(None, None, "items"),
            P(None, "items", None),
            P(None, "items"),
            P(None, None, "items"),
            P(None, None, "items"),
            P(None, "items", None),
            P(None, "items"),
            P(None, "items", None),
            P(None, "items"),
        ),
        check_vma=False,
    )
```

```python
import functools
import jax
import jax.numpy as jnp
from jax import lax
from jax.experimental import pallas as pl
from jax.experimental.pallas import tpu as pltpu
from jax.sharding import PartitionSpec as P

HEADS = 12
PATCHES = 197
TEXT = 40
F32 = jnp.float32
BF = jnp.bfloat16
EPS = 1e-06
FILL = -1e30
MIB = 1 << 20
PAD = 80
TILE = 1024


def dot(left, right, dims=((1,), (0,))):
    return lax.dot_general(left, right, (dims, ((), ())), preferred_element_type=F32)


NT = ((1,), (1,))
TN = ((0,), (0,))


def norm_stats(values):
    row_mean = jnp.mean(values, axis=-1, keepdims=True)
    centred = values - row_mean
    row_var = jnp.mean(centred * centred, axis=-1, keepdims=True)
    inv_std = lax.rsqrt(row_var + EPS)
    return centred * inv_std, inv_std


def norm_back(grad_out, values, gain):
    scaled, inv_std = norm_stats(values)
    grad_scaled = grad_out * gain
    mean_first = jnp.mean(grad_scaled, axis=-1, keepdims=True)
    mean_second = jnp.mean(grad_scaled * scaled, axis=-1, keepdims=True)
    grad_in = inv_std * (grad_scaled - mean_first - scaled * mean_second)
    gain_sum = jnp.sum(grad_out * scaled, axis=0, keepdims=True)
    offset_sum = jnp.sum(grad_out, axis=0, keepdims=True)
    return grad_in, gain_sum, offset_sum


def gelu_parts(pre):
    cumulative = 0.5 * (1.0 + lax.erf(pre * 0.7071067811865476))
    density = jnp.exp(-0.5 * pre * pre) * 0.3989422804014327
    return pre * cumulative, cumulative + pre * density


def params(limit_mib):
    return pltpu.CompilerParams(vmem_limit_bytes=limit_mib * MIB)


def cost():
    return pl.CostEstimate(flops=1, bytes_accessed=1, transcendentals=0)


ONCE = pl.Buffered(1)


def whole(shape):
    return pl.BlockSpec(shape, lambda *_: (0,) * len(shape), pipeline_mode=ONCE)


def layer_block(shape, index):
    return pl.BlockSpec((1,) + shape, lambda *_: (index,) + (0,) * len(shape), pipeline_mode=ONCE)


SMEM = pl.BlockSpec(memory_space=pltpu.SMEM)
ANY = pl.BlockSpec(memory_space=pl.ANY)
sds = jax.ShapeDtypeStruct


TOKENS = {}


def order_after(deps):
    return tuple(TOKENS[id(dep)][1] if id(dep) in TOKENS else dep for dep in deps)


def note(outs, token):
    for out in outs:
        TOKENS[id(out)] = (out, token)


def run(body, args, deps=(), *, in_specs, out_specs, out_shape, grid_spec=None, call=None, **rest):
    deps = order_after(deps)
    count, extra = len(args), len(deps)
    single = not isinstance(out_shape, (list, tuple))
    if single:
        out_specs, out_shape = [out_specs], [out_shape]
    number = len(out_shape)

    def wrapped(*refs):
        outs = refs[count + extra :]
        outs[number][...] = jnp.zeros_like(outs[number])
        body(*refs[:count], *outs[:number], *outs[number + 1 :])

    outs = pl.pallas_call(
        wrapped,
        in_specs=list(in_specs) + [ANY] * extra,
        out_specs=list(out_specs) + [whole((8, 128))],
        out_shape=list(out_shape) + [sds((8, 128), F32)],
        name=call or getattr(body, "func", body).__name__,
        **rest,
    )(*args, *deps)
    *outs, token = outs
    note(outs, token)
    return outs[0] if single else outs


def hbm(value):
    return pltpu.with_memory_space_constraint(value, pltpu.HBM)


def first(shape):
    return lax.broadcasted_iota(jnp.int32, shape, 0)


def second(shape):
    return lax.broadcasted_iota(jnp.int32, shape, 1)


class Dims:
    def __init__(self, slots, streams, width, hidden, item_devs):
        self.slots = slots
        self.text_at = slots * (streams - 1)
        self.rows = slots * streams
        self.full = -(-self.rows // 16) * 16
        self.live = -(-(self.text_at + TEXT) // 16) * 16
        self.keys = -(-self.live // 128) * 128
        self.vis = -(-self.text_at // 16) * 16
        self.lang = self.text_at // 16 * 16
        self.width = width
        self.hidden = hidden
        self.streams = streams
        self.item_devs = item_devs
        self.share = width // item_devs
        self.bits = item_devs.bit_length() - 1
        self.order_a = list(range(self.bits))
        self.order_b = self.order_a[1:] + self.order_a[:1]
        self.tiled = self.share % 16 == 0

    def place(self, index, order):
        out = index * 0
        for k, bit in enumerate(order):
            out = out | (((index >> bit) & 1) << (self.bits - 1 - k))
        return out


def put_stage(dm, stage, pieces):
    stage[...] = jnp.zeros_like(stage)
    for r, piece in enumerate(pieces):
        stage[r * PAD : r * PAD + dm.slots] = piece


def slot_select(dm, rows, stream):
    shape = (rows, 4 * PAD)
    slot = first(shape)
    shard = jnp.zeros(shape, jnp.int32)
    for k in range(1, dm.streams):
        shard = shard + (slot >= k * dm.slots).astype(jnp.int32)
    place = slot - shard * dm.slots
    return second(shape) == ((shard ^ stream) * PAD + place), slot


def shard_rows(dm, rows, shard):
    shape = (-(-dm.slots // 8) * 8, rows)
    return ((second(shape) == first(shape) + shard * dm.slots) & (first(shape) < dm.slots)).astype(BF)


def split_shards(dm, value, stream, refs):
    for r, ref in enumerate(refs):
        ref[...] = dot(shard_rows(dm, value.shape[0], stream ^ r), value)[: dm.slots].astype(BF)


def cot_prep_body(dm, sc, c0, c1, c2, c3, out, stage):
    stream = sc[1]
    pick, slot = slot_select(dm, dm.live, stream)
    for r in range(4):
        put_stage(dm, stage, [c[stream ^ r] for c in (c0, c1, c2, c3)])
        alive = (slot < PATCHES) | ((slot >= dm.text_at) & (slot < dm.text_at + sc[4 + (stream ^ r)]))
        out[r] = dot((pick & alive).astype(BF), stage[...]).astype(BF)


def cot_prep(dm, sc, pieces, deps):
    shape = pieces[0].shape
    return run(
        functools.partial(cot_prep_body, dm),
        (sc, *pieces),
        deps,
        grid=(1,),
        in_specs=[SMEM] + [whole(shape)] * 4,
        out_specs=whole((4, dm.live, dm.width)),
        out_shape=sds((4, dm.live, dm.width), BF),
        scratch_shapes=[pltpu.VMEM((4 * PAD, dm.width), BF)],
        compiler_params=params(12),
        cost_estimate=cost(),
    )


def join_shards_body(sc, own, near, far, mixed, grad):
    stream = sc[1]
    for k, out in enumerate((mixed, grad)):
        for r, value in enumerate((own[k], near[k], far[2 * k], near[2 + k])):
            out[stream ^ r] = value.astype(out.dtype)


def join_shards(dm, sc, own, near, far, *deps):
    shape = (4, dm.slots, dm.width)
    return run(
        join_shards_body,
        (sc, own, near, far),
        deps,
        grid=(1,),
        in_specs=[SMEM, whole(own.shape), whole(near.shape), whole(far.shape)],
        out_specs=[whole(shape)] * 2,
        out_shape=[sds(shape, BF), sds(shape, F32)],
        compiler_params=params(8),
        cost_estimate=cost(),
    )


def select_body(dm, sc, w, b, wo, bo):
    part = dm.hidden // (dm.item_devs * dm.streams)
    for s in range(dm.streams):

        @pl.when(sc[1] == s)
        def _(s=s):
            count = w.shape[2] // (part * dm.streams)
            starts = [i * part * dm.streams + s * part for i in range(count)]
            wo[0] = jnp.concatenate([w[0, :, at : at + part] for at in starts], axis=1)
            bo[0] = jnp.concatenate([b[0, :, at : at + part].astype(F32) for at in starts], axis=1)


def select_quarter(dm, sc, ffn_in, ffn_in_bias):
    d, streams = dm.width, dm.streams
    count = ffn_in.shape[0]
    wide = dm.hidden // 2
    return run(
        functools.partial(select_body, dm),
        (sc, hbm(ffn_in), ffn_in_bias[:, None]),
        grid=(count, 2),
        in_specs=[
            SMEM,
            pl.BlockSpec((1, d, wide), lambda e, t: (e, 0, t)),
            pl.BlockSpec((1, 1, wide), lambda e, t: (e, 0, t)),
        ],
        out_specs=[
            pl.BlockSpec((1, d, wide // streams), lambda e, t: (e, 0, t)),
            pl.BlockSpec((1, 1, wide // streams), lambda e, t: (e, 0, t)),
        ],
        out_shape=[sds((count, d, d), BF), sds((count, 1, d), F32)],
        compiler_params=params(60),
        cost_estimate=cost(),
    )

def fwd_attn_body(dm, sc, xv, gain, offset, win, bias, wout, obias, nco, qo, ko, vo, po, x1o, n2o, n2live, ctx_s):
    width = dm.width
    scaled, _ = norm_stats(xv)
    n1 = (scaled * gain[0, 0:1].astype(F32) + offset[0, 0:1].astype(F32)).astype(BF)
    nco[0] = n1[: dm.live]
    w = win.at[0]
    q = (dot(n1, w[:, 0:width]) + bias[0, 0:1].astype(F32)).astype(BF) * 0.125
    q = q.astype(BF)
    k = dot(n1[: dm.keys], w[:, width : 2 * width]).astype(BF)
    v = (dot(n1[: dm.keys], w[:, 2 * width :]) + bias[0, 1:2].astype(F32)).astype(BF)
    qo[...] = q[: dm.live]
    ko[...] = k
    vo[...] = v
    col = lax.broadcasted_iota(jnp.int32, (1, dm.keys), 1)
    valid = (col < PATCHES) | ((col >= dm.text_at) & (col < dm.text_at + sc[0]))
    low_lane = lax.broadcasted_iota(jnp.int32, (1, 128), 1) < 64
    for pair in range(HEADS // 2):
        lanes = slice(pair * 128, pair * 128 + 128)
        qp, kp, vp = q[:, lanes], k[:, lanes], v[:, lanes]
        outs = []
        for j in range(2):
            qm = jnp.where(low_lane if j == 0 else ~low_lane, qp, jnp.zeros_like(qp))
            scores = jnp.where(valid, dot(qm, kp, NT), FILL)
            top = jnp.max(scores, axis=-1, keepdims=True)
            expo = jnp.exp(scores - top)
            probs = (expo / jnp.sum(expo, axis=-1, keepdims=True)).astype(BF)
            po[2 * pair + j] = probs[: dm.live]
            outs.append(dot(probs, vp))
        ctx_s[:, lanes] = jnp.where(low_lane, outs[0], outs[1]).astype(BF)
    ctx = ctx_s[...]
    nco[1] = ctx[: dm.live]
    x1 = xv + (dot(ctx, wout[0]) + obias[0].astype(F32))
    x1o[...] = x1
    scaled, _ = norm_stats(x1)
    n2 = (scaled * gain[0, 1:2].astype(F32) + offset[0, 1:2].astype(F32)).astype(BF)
    n2o[...] = n2
    n2live[...] = n2[: dm.live]


def fwd_attn_next_body(dm, sc, x, *refs):
    fwd_attn_body(dm, sc, x[...], *refs)


def fwd_attn_first_body(dm, sc, tokens, near, far, *refs):
    stream = sc[1]
    *refs, x0, ctx_s, stage = refs
    put_stage(dm, stage, [tokens[stream], near[0], far[stream & 1], near[1]])
    pick, _ = slot_select(dm, dm.full, stream)
    xv = dot(pick.astype(BF), stage[...])
    x0[...] = xv.astype(BF)
    fwd_attn_body(dm, sc, xv, *refs, ctx_s)


def fwd_attn(dm, layer, sc, inputs, norm_gain, norm_bias, attn_in, attn_bias, attn_out, out_bias, deps=()):
    d, full, live, keys = dm.width, dm.full, dm.live, dm.keys
    shapes = [
        sds((2, live, d), BF),
        sds((live, d), BF),
        sds((keys, d), BF),
        sds((keys, d), BF),
        sds((HEADS, live, keys), BF),
        sds((full, d), F32),
        sds((full, d), BF),
        sds((live, d), BF),
    ]
    scratch = [pltpu.VMEM((full, d), BF)]
    body = fwd_attn_next_body
    if len(inputs) > 1:
        body = fwd_attn_first_body
        shapes.append(sds((full, d), BF))
        scratch.append(pltpu.VMEM((4 * PAD, d), BF))
    return run(
        functools.partial(body, dm),
        (sc, *inputs, norm_gain, norm_bias, hbm(attn_in), attn_bias, hbm(attn_out), out_bias[:, None]),
        deps,
        grid=(1,),
        in_specs=[SMEM]
        + [whole(value.shape) for value in inputs]
        + [
            layer_block((2, d), layer),
            layer_block((2, d), layer),
            layer_block((d, 3 * d), layer),
            layer_block((2, d), layer),
            layer_block((d, d), layer),
            layer_block((1, d), layer),
        ],
        out_specs=[whole(s.shape) for s in shapes],
        out_shape=shapes,
        scratch_shapes=scratch,
        compiler_params=params(16),
        cost_estimate=cost(),
    )


def fwd_ff_two_body(dm, n2, x1, wv, wl, bi, wov, wol, bo, slope_v, slope_l, x2, acc):
    t = pl.program_id(0)
    vis, lang, text_at = dm.vis, dm.lang, dm.text_at
    rows_v = lax.broadcasted_iota(jnp.int32, (vis, 1), 0) < text_at
    rows_l = lax.broadcasted_iota(jnp.int32, (dm.full - lang, 1), 0) + lang >= text_at
    act_v, sv = gelu_parts(dot(n2[0:vis], wv[0]) + bi[0, 0:1].astype(F32))
    act_l, sl = gelu_parts(dot(n2[lang:], wl[0]) + bi[1, 0:1].astype(F32))
    slope_v[...] = sv.astype(BF)
    slope_l[...] = sl[: dm.live - lang].astype(BF)
    part_v = dot(act_v.astype(BF), wov[0])
    part_l = dot(act_l.astype(BF), wol[0])

    @pl.when(t == 0)
    def _():
        acc[...] = x1[...]
        part_vb = part_v + bo[0, 0:1].astype(F32)
        part_lb = part_l + bo[1, 0:1].astype(F32)
        acc[0:vis] += jnp.where(rows_v, part_vb, 0.0)
        acc[lang:] += jnp.where(rows_l, part_lb, 0.0)

    @pl.when(t > 0)
    def _():
        acc[0:vis] += jnp.where(rows_v, part_v, 0.0)
        acc[lang:] += jnp.where(rows_l, part_l, 0.0)

    @pl.when(t == pl.num_programs(0) - 1)
    def _():
        x2[...] = acc[...]


def fwd_ff_two(dm, n2, x1, ffn_in, ffn_in_bias, ffn_out, ffn_out_bias, deps=()):
    d, full, hid = dm.width, dm.full, dm.hidden
    count = ffn_in.shape[0]
    return run(
        functools.partial(fwd_ff_two_body, dm),
        (n2, x1, hbm(ffn_in), hbm(ffn_in), ffn_in_bias[:, None], hbm(ffn_out), hbm(ffn_out), ffn_out_bias[:, None]),
        deps,
        grid=(hid // TILE,),
        in_specs=[
            whole((full, d)),
            whole((full, d)),
            pl.BlockSpec((1, d, TILE), lambda t: (0, 0, t)),
            pl.BlockSpec((1, d, TILE), lambda t: (1, 0, t)),
            pl.BlockSpec((count, 1, TILE), lambda t: (0, 0, t)),
            pl.BlockSpec((1, TILE, d), lambda t: (0, t, 0)),
            pl.BlockSpec((1, TILE, d), lambda t: (1, t, 0)),
            whole((count, 1, d)),
        ],
        out_specs=[
            pl.BlockSpec((dm.vis, TILE), lambda t: (0, t)),
            pl.BlockSpec((dm.live - dm.lang, TILE), lambda t: (0, t)),
            whole((full, d)),
        ],
        out_shape=[sds((dm.vis, hid), BF), sds((dm.live - dm.lang, hid), BF), sds((full, d), F32)],
        scratch_shapes=[pltpu.VMEM((full, d), F32)],
        compiler_params=params(20),
        cost_estimate=cost(),
    )


def finish_ff_back(dm, g, gn, x1, gain, go, ga, sums):
    grad_in, gain_sum, offset_sum = norm_back(gn, x1[0 : dm.live], gain[0, 1:2].astype(F32))
    out = g + grad_in
    go[...] = out
    low = out.astype(BF)
    ga[...] = low
    sums[0:1] = gain_sum
    sums[1:2] = offset_sum
    sums[2:3] = jnp.sum(low.astype(F32), axis=0, keepdims=True)


def top_ff_body(dm, sc, n2, gf, x1, gain, wi, bi, wo, bo, mix, go, ga, sums, hsum, accm, accg):
    t = pl.program_id(0)
    act, slope = gelu_parts(dot(n2[...], wi[0]) + bi[0].astype(F32))
    gpre = (dot(gf[0], wo[0], NT) * slope[: dm.live]).astype(BF)
    hsum[...] = jnp.sum(gpre.astype(F32), axis=0, keepdims=True)
    part = dot(act.astype(BF), wo[0])
    back = dot(gpre, wi[0], NT)

    @pl.when(t == 0)
    def _():
        accm[...] = part + (x1[...] + bo[0].astype(F32))
        accg[...] = back

    @pl.when(t > 0)
    def _():
        accm[...] += part
        accg[...] += back

    @pl.when(t == pl.num_programs(0) - 1)
    def _():
        split_shards(dm, accm[...].astype(BF), sc[1], [mix.at[r] for r in range(4)])
        g = gf[0].astype(F32)
        sums[3:4] = jnp.sum(g, axis=0, keepdims=True)
        finish_ff_back(dm, g, accg[...], x1, gain, go, ga, sums)


def top_ff(dm, layer, expert, sc, n2, gf, x1, norm_gain, ffn_in, ffn_in_bias, ffn_out, ffn_out_bias, deps=()):
    d, full, live, hid, slots = dm.width, dm.full, dm.live, dm.hidden, dm.slots
    shapes = [
        sds((4, slots, d), BF),
        sds((live, d), F32),
        sds((live, d), BF),
        sds((4, d), F32),
    ]
    return run(
        functools.partial(top_ff_body, dm),
        (sc, n2, gf, x1, norm_gain, hbm(ffn_in), ffn_in_bias[:, None], hbm(ffn_out), ffn_out_bias[:, None]),
        deps,
        grid=(hid // TILE,),
        in_specs=[
            SMEM,
            whole((full, d)),
            layer_block((live, d), 0),
            whole((full, d)),
            layer_block((2, d), layer),
            pl.BlockSpec((1, d, TILE), lambda t: (expert, 0, t)),
            pl.BlockSpec((1, 1, TILE), lambda t: (expert, 0, t)),
            pl.BlockSpec((1, TILE, d), lambda t: (expert, t, 0)),
            layer_block((1, d), expert),
        ],
        out_specs=[whole(s.shape) for s in shapes] + [pl.BlockSpec((1, TILE), lambda t: (0, t))],
        out_shape=shapes + [sds((1, hid), F32)],
        scratch_shapes=[pltpu.VMEM((full, d), F32), pltpu.VMEM((live, d), F32)],
        compiler_params=params(20),
        cost_estimate=cost(),
    )


def back_ff_two_body(dm, g, gf, x1, gain, slv, sll, wov, wol, wv, wl, go, ga, sums, hsum, acc):
    t = pl.program_id(0)
    vis, lang, text_at, live = dm.vis, dm.lang, dm.text_at, dm.live
    rows_v = lax.broadcasted_iota(jnp.int32, (vis, 1), 0) < text_at
    rows_l = lax.broadcasted_iota(jnp.int32, (live - lang, 1), 0) + lang >= text_at
    gv = jnp.where(rows_v, gf[0:vis].astype(F32), 0.0)
    gl = jnp.where(rows_l, gf[lang:].astype(F32), 0.0)
    pre_v = (dot(gv.astype(BF), wov[0], NT) * slv[...].astype(F32)).astype(BF)
    pre_l = (dot(gl.astype(BF), wol[0], NT) * sll[...].astype(F32)).astype(BF)
    hsum[0:1] = jnp.sum(pre_v.astype(F32), axis=0, keepdims=True)
    hsum[1:2] = jnp.sum(pre_l.astype(F32), axis=0, keepdims=True)
    part_v = dot(pre_v, wv[0], NT)
    part_l = dot(pre_l, wl[0], NT)

    @pl.when(t == 0)
    def _():
        acc[...] = jnp.zeros_like(acc)

    acc[0:vis] += part_v
    acc[lang:] += part_l

    @pl.when(t == pl.num_programs(0) - 1)
    def _():
        sums[3:4] = jnp.sum(gv, axis=0, keepdims=True)
        sums[4:5] = jnp.sum(gl, axis=0, keepdims=True)
        finish_ff_back(dm, g[...], acc[...], x1, gain, go, ga, sums)


def back_ff_two(dm, layer, g, gf, x1, norm_gain, slope_v, slope_l, ffn_in, ffn_out, deps=()):
    d, live, hid = dm.width, dm.live, dm.hidden
    return run(
        functools.partial(back_ff_two_body, dm),
        (g, gf, x1, norm_gain, slope_v, slope_l, hbm(ffn_out), hbm(ffn_out), hbm(ffn_in), hbm(ffn_in)),
        deps,
        grid=(hid // TILE,),
        in_specs=[
            whole((live, d)),
            whole((live, d)),
            whole((dm.full, d)),
            layer_block((2, d), layer),
            pl.BlockSpec((dm.vis, TILE), lambda t: (0, t)),
            pl.BlockSpec((live - dm.lang, TILE), lambda t: (0, t)),
            pl.BlockSpec((1, TILE, d), lambda t: (0, t, 0)),
            pl.BlockSpec((1, TILE, d), lambda t: (1, t, 0)),
            pl.BlockSpec((1, d, TILE), lambda t: (0, 0, t)),
            pl.BlockSpec((1, d, TILE), lambda t: (1, 0, t)),
        ],
        out_specs=[
            whole((live, d)),
            whole((live, d)),
            whole((5, d)),
            pl.BlockSpec((2, TILE), lambda t: (0, t)),
        ],
        out_shape=[sds((live, d), F32), sds((live, d), BF), sds((5, d), F32), sds((2, hid), F32)],
        scratch_shapes=[pltpu.VMEM((live, d), F32)],
        compiler_params=params(20),
        cost_estimate=cost(),
    )


def back_attn_body(dm, bottom, sc, g, ga, q, k, v, p, x, gain, win, wout, *refs):
    width, live = dm.width, dm.live
    *refs, parts = refs
    mine, other_near, other_far, sums, *outs = refs[1:] if bottom else refs
    gc = dot(ga[...], wout[0], NT).astype(BF)
    low_lane = lax.broadcasted_iota(jnp.int32, (1, 128), 1) < 64
    for pair in range(HEADS // 2):
        lanes = slice(pair * 128, pair * 128 + 128)
        gp, qp, kp, vp = gc[:, lanes], q[:, lanes], k[:, lanes], v[:, lanes]
        dqs, dks, dvs = [], [], []
        for j in range(2):
            gm = jnp.where(low_lane if j == 0 else ~low_lane, gp, jnp.zeros_like(gp))
            dprob = dot(gm, vp, NT)
            prob_low = p[2 * pair + j]
            prob = prob_low.astype(F32)
            inner = jnp.sum(prob * dprob, axis=-1, keepdims=True)
            ds = (prob * (dprob - inner)).astype(BF)
            dqs.append(dot(ds, kp))
            dks.append(dot(ds, qp, TN))
            dvs.append(dot(prob_low, gp, TN))
        dq = jnp.where(low_lane, dqs[0], dqs[1]) * 0.125
        dk = jnp.where(low_lane, dks[0], dks[1])
        dv = jnp.where(low_lane, dvs[0], dvs[1])
        parts[0, :, lanes] = dq.astype(BF)
        parts[1, :, lanes] = dk[:live].astype(BF)
        parts[2, :, lanes] = dv[:live].astype(BF)
    parts[3] = ga[...]
    mine[0] = parts[sc[1]]
    mine[1] = parts[sc[1] ^ 2]
    other_near[...] = parts[sc[1] ^ 1]
    other_far[...] = parts[sc[1] ^ 3]
    gn = sum(dot(parts[k], win[0, :, k * width : (k + 1) * width], NT) for k in range(3))
    grad_in, gain_sum, offset_sum = norm_back(gn, x[0:live].astype(F32), gain[0, 0:1].astype(F32))
    out = g[...] + grad_in
    if bottom:
        own, near, far = outs
        split_shards(dm, out.astype(BF), sc[1], (own.at[1], near.at[1], far.at[2], far.at[3]))
        for r, ref in enumerate((own.at[0], near.at[0], far.at[0], far.at[1])):
            ref[...] = refs[0][r]
    else:
        outs[0][...] = out
        outs[1][...] = out.astype(BF)
    sums[0:1] = gain_sum
    sums[1:2] = offset_sum
    sums[2:3] = jnp.sum(parts[0].astype(F32), axis=0, keepdims=True)
    sums[3:4] = jnp.sum(parts[2].astype(F32), axis=0, keepdims=True)


def back_attn(dm, layer, sc, g, ga, q, k, v, p, x, norm_gain, attn_in, attn_out, mix=None, deps=()):
    d, live, keys, slots = dm.width, dm.live, dm.keys, dm.slots
    bottom = layer == 0
    shapes = [sds((2, live, d), BF), sds((live, d), BF), sds((live, d), BF), sds((4, d), F32)]
    if bottom:
        shapes += [sds((2, slots, d), BF), sds((2, slots, d), BF), sds((4, slots, d), BF)]
    else:
        shapes += [sds((live, d), F32), sds((live, d), BF)]
    return run(
        functools.partial(back_attn_body, dm, bottom),
        (sc, g, ga, q, k, v, p, x, norm_gain, hbm(attn_in), hbm(attn_out)) + ((mix,) if bottom else ()),
        deps,
        grid=(1,),
        in_specs=[
            SMEM,
            whole((live, d)),
            whole((live, d)),
            whole((live, d)),
            whole((keys, d)),
            whole((keys, d)),
            whole((HEADS, live, keys)),
            whole((dm.full, d)),
            layer_block((2, d), layer),
            layer_block((d, 3 * d), layer),
            layer_block((d, d), layer),
        ]
        + ([whole(mix.shape)] if bottom else []),
        out_specs=[whole(s.shape) for s in shapes],
        out_shape=shapes,
        scratch_shapes=[pltpu.VMEM((4, live, d), BF)],
        compiler_params=params(16),
        cost_estimate=cost(),
    )


def store_shares(dm, refs, row, value, order, flip, stage):
    keep, send = refs
    n, share = dm.item_devs, dm.share
    half = n // 2
    for i in range(n):
        stage[i] = value[i * share : (i + 1) * share]
    for p in range(n):
        ref = keep if p < half else send
        index = unplace(dm, p ^ flip, order)
        ref[p % half, row : row + share] = stage[index]


def unplace(dm, place, order):
    out = place * 0
    for k, bit in enumerate(order):
        out = out | (((place >> (dm.bits - 1 - k)) & 1) << bit)
    return out


def wgrad_attn_body(dm, sc, nc, nc_near, mine, got_near, got_far, keep, send, left, right):
    n, live = dm.item_devs, dm.live
    for k, (got, ref) in enumerate(((got_near, keep), (got_far, send))):
        side = jnp.where((sc[1] ^ (2 * k)) == 3, 1, 0)
        left[0:live] = nc[side]
        left[live:] = nc_near[side]
        right[0:live] = mine[k]
        right[live:] = got[...]
        value = dot(left[...], right[...], TN).astype(BF)
        if dm.tiled:
            for i in range(n):
                ref[dm.place(i, dm.order_a) ^ sc[2]] = value[i * dm.share : (i + 1) * dm.share]
        else:
            ref[...] = value


def wgrad_attn(dm, sc, nc, nc_near, mine, got_near, got_far, deps=()):
    d, live, n, share = dm.width, dm.live, dm.item_devs, dm.share
    shape = (n, share, d) if dm.tiled else (d, d)
    args = (sc, nc, nc_near, mine, got_near, got_far)
    return run(
        functools.partial(wgrad_attn_body, dm),
        args,
        deps,
        grid=(1,),
        in_specs=[SMEM] + [whole(value.shape) for value in args[1:]],
        out_specs=[whole(shape)] * 2,
        out_shape=[sds(shape, BF)] * 2,
        scratch_shapes=[pltpu.VMEM((2 * live, d), BF)] * 2,
        compiler_params=params(12),
        cost_estimate=cost(),
    )


def ff_layout(dm, experts):
    rows, where = [], {}
    for index, (*_, orders) in enumerate(experts):
        for side in range(2):
            if side and orders[0] is orders[1] and dm.tiled:
                rows[-1] += dm.share
            else:
                rows.append(dm.share)
            where[index, side] = (len(rows) - 1, rows[-1] - dm.share)
    return rows, where


def wgrad_ff_body(dm, experts, stacked, sc, *refs):
    d, streams = dm.width, dm.streams
    n2s = refs[0:streams]
    gfs, refs = ([refs[streams].at[r] for r in range(streams)], refs[streams + 1 :]) if stacked else (refs[streams : 2 * streams], refs[2 * streams :])
    count = len(experts)
    wi, wo, bi = refs[:3]
    outs = refs[3:-5]
    n2a, gfa, acta, gpa, stage = refs[-5:]
    _, where = ff_layout(dm, experts)
    for index, (expert, start, stop, low, high, orders) in enumerate(experts):
        size = stop - start
        total = size * streams
        rows = first((size, 1)) + start
        keep = (rows >= low) & (rows < high)
        for r in range(streams):
            n2a[r * size : (r + 1) * size] = n2s[r][start:stop]
            gpart = gfs[r][start:stop]
            if low > start or high < stop:
                gpart = jnp.where(keep, gpart.astype(F32), 0.0).astype(BF)
            gfa[r * size : (r + 1) * size] = gpart
        chunk = size if size >= 128 else total
        wi_e = wi.at[index]
        wo_e = wo[index].reshape(d, d)

        def step(c, carry, chunk=chunk, wi_e=wi_e, wo_e=wo_e, index=index):
            at = pl.ds(pl.multiple_of(c * chunk, 16), chunk)
            act, slope = gelu_parts(dot(n2a[at], wi_e[...]) + bi[index])
            acta[at] = act.astype(BF)
            gpa[at] = (dot(gfa[at], wo_e, NT) * slope).astype(BF)
            return carry

        lax.fori_loop(0, total // chunk, step, 0)
        for side, (left, right) in enumerate(((n2a, gpa), (acta, gfa))):
            value = dot(left[0:total], right[0:total], TN).astype(BF)
            pair, row = where[index, side]
            if not dm.tiled:
                outs[pair][...] = value
                continue
            store_shares(dm, outs[2 * pair : 2 * pair + 2], row, value, orders[side], sc[2] if orders[side] == dm.order_a else sc[3], stage)


def wgrad_ff(dm, experts, sc, n2s, gfs, wi, wo, bi, deps=()):
    d, live, n, share, streams = dm.width, dm.live, dm.item_devs, dm.share, dm.streams
    count = len(experts)
    base = experts[0][0]
    part = d // n
    stacked = len(gfs) == 1
    pair_rows, _ = ff_layout(dm, experts)
    shapes = [(n // 2, rows, d) for rows in pair_rows for _ in range(2)] if dm.tiled else [(d, d)] * len(pair_rows)
    top = max(e[2] - e[1] for e in experts) * streams
    if dm.tiled:
        wo = wo.reshape(wo.shape[0], n, streams, part, d)
        wo_spec = pl.BlockSpec((count, n, None, part, d), lambda t, s: (base // count, 0, s[1], 0, 0), pipeline_mode=ONCE)
    else:
        wo_spec = pl.BlockSpec((count, d, d), lambda t, s: (base // count, 0, 0), pipeline_mode=ONCE)

    body = functools.partial(wgrad_ff_body, dm, experts, stacked)
    deps = order_after(deps)
    extra = len(deps)
    args = (*n2s, *gfs, wi, hbm(wo), bi)
    number = len(shapes)

    def wrapped(*refs):
        outs = refs[1 + len(args) + extra :]
        outs[number][...] = jnp.zeros_like(outs[number])
        body(*refs[: 1 + len(args)], *outs[:number], *outs[number + 1 :])

    gf_specs = [pl.BlockSpec((streams, live, d), lambda t, s: (0, 0, 0), pipeline_mode=ONCE)] if stacked else [pl.BlockSpec((live, d), lambda t, s: (0, 0), pipeline_mode=ONCE)] * streams
    *outs, token = pl.pallas_call(
        wrapped,
        grid_spec=pltpu.PrefetchScalarGridSpec(
            num_scalar_prefetch=1,
            grid=(1,),
            in_specs=[pl.BlockSpec((live, d), lambda t, s: (0, 0), pipeline_mode=ONCE)] * streams
            + gf_specs
            + [
                pl.BlockSpec((count, d, d), lambda t, s: (base // count, 0, 0), pipeline_mode=ONCE),
                wo_spec,
                pl.BlockSpec((count, 1, d), lambda t, s: (base // count, 0, 0), pipeline_mode=ONCE),
            ]
            + [ANY] * extra,
            out_specs=[pl.BlockSpec(shape, lambda t, s, shape=shape: (0,) * len(shape), pipeline_mode=ONCE) for shape in [*shapes, (8, 128)]],
            scratch_shapes=[pltpu.VMEM((top, d), BF)] * 4 + [pltpu.VMEM((n, share, d), BF)],
        ),
        out_shape=[sds(shape, BF) for shape in shapes] + [sds((8, 128), F32)],
        compiler_params=params(24),
        cost_estimate=cost(),
        name="wgrad_ff_body",
    )(sc, *args, *deps)
    note(outs, token)
    return outs


def finish_body(dm, sc, *refs):
    *pieces, first_out, second_out, stage = refs
    share, part = dm.share, dm.hidden // (dm.item_devs * dm.streams)
    expert = len(pieces) == 8
    for k, piece in enumerate(pieces):
        stage[k // 4, sc[1] ^ (k % 4)] = piece[...]
    if expert:
        for i in range(dm.item_devs):
            block = [stage[0, q, :, i * part : (i + 1) * part].astype(F32) for q in range(4)]
            first_out[0, :, i * 4 * part : (i + 1) * 4 * part] = jnp.concatenate(block, axis=1)
        for q in range(4):
            second_out[0, q * share : (q + 1) * share] = stage[1, q].astype(F32)
    else:
        for q in range(3):
            first_out[0, :, q * dm.width : (q + 1) * dm.width] = stage[0, q].astype(F32)
        second_out[0] = stage[0, 3].astype(F32)


def finish(dm, sc, sources, index, bases, *deps):
    share, d, hid = dm.share, dm.width, dm.hidden
    expert = len(sources) == 2
    if expert:
        shapes = [(3, share, hid), (3, 4 * share, d)]
    else:
        shapes = [(2, share, 3 * d), (2, share, d)]
    args, specs = [sc], [SMEM]
    for arrays, block in sources:
        args += arrays
        if dm.tiled:
            specs += [pl.BlockSpec((share, d), lambda t, block=block: (block, 0), pipeline_mode=ONCE)] * 4
        else:
            args[-4:] = [value[block * share : (block + 1) * share] for value in arrays]
            specs += [whole((share, d))] * 4
    deps = order_after(deps)
    count, extra = len(args), len(bases)

    def body(*refs):
        outs = refs[count + extra + len(deps) :]
        outs[2][...] = jnp.zeros_like(outs[2])
        finish_body(dm, *refs[:count], *outs[:2], outs[3])

    *outs, token = pl.pallas_call(
        body,
        grid=(1,),
        in_specs=specs + [pl.BlockSpec(memory_space=pltpu.HBM)] * extra + [ANY] * len(deps),
        out_specs=[
            pl.BlockSpec((1,) + shape[1:], lambda t: (index, 0, 0), pipeline_mode=ONCE) for shape in shapes
        ]
        + [whole((8, 128))],
        out_shape=[pltpu.HBM(shape, F32) for shape in shapes] + [sds((8, 128), F32)],
        scratch_shapes=[pltpu.VMEM((len(sources), 4, share, d), BF)],
        input_output_aliases={count + k: k for k in range(extra)},
        compiler_params=params(12),
        cost_estimate=cost(),
        name="finish_body",
    )(*args, *bases, *deps)
    note(outs, token)
    return outs


SMALL_ROWS = 32


def small_body(dm, sc, a0, a1, f0, f1, h0, h1, out):
    out[...] = jnp.zeros_like(out)
    share = dm.share
    wide = jnp.concatenate(
        [
            a0[2:4], a1[2:4],
            f0[2:3], f1[2:3],
            a0[0:1], f0[0:1], a1[0:1], f1[0:1],
            a0[1:2], f0[1:2], a1[1:2], f1[1:2],
            f0[3:5], f1[3:4],
        ],
        axis=0,
    )
    hidden = jnp.concatenate([h0[...], h1[...]], axis=0)
    count = wide.shape[0]
    for i in range(dm.item_devs):
        place = dm.place(i, dm.order_a) ^ sc[2]
        out[place, 0:count, 0:share] = wide[:, i * share : (i + 1) * share]
        for q in range(4):
            at = (i * 4 + q) * share
            out[place, count + 3 * q : count + 3 * q + 3, 0:share] = hidden[:, at : at + share]


def small_pack(dm, sc, values, deps):
    shape = (dm.item_devs, SMALL_ROWS, 128)
    return run(
        functools.partial(small_body, dm),
        (sc, *values),
        deps,
        grid=(1,),
        in_specs=[SMEM] + [whole(value.shape) for value in values],
        out_specs=whole(shape),
        out_shape=sds(shape, F32),
        compiler_params=params(8),
        cost_estimate=cost(),
    )


def small_out_body(dm, near, far, attn_bias, out_bias, gain, offset, hidden, ffn_bias):
    share = dm.share
    total = near[:, 0:share] + far[:, 0:share]
    for l in range(2):
        attn_bias[l] = total[2 * l : 2 * l + 2]
        gain[l] = total[6 + 2 * l : 8 + 2 * l]
        offset[l] = total[10 + 2 * l : 12 + 2 * l]
    out_bias[...] = total[4:6]
    ffn_bias[...] = total[14:17]
    hidden[...] = jnp.concatenate([total[17 + 3 * q : 20 + 3 * q] for q in range(4)], axis=1)


def small_unpack(dm, near, far, *deps):
    share = dm.share
    shapes = [(2, 2, share), (2, share), (2, 2, share), (2, 2, share), (3, 4 * share), (3, share)]
    return run(
        functools.partial(small_out_body, dm),
        (near, far),
        deps,
        grid=(1,),
        in_specs=[whole(near.shape)] * 2,
        out_specs=[whole(shape) for shape in shapes],
        out_shape=[sds(shape, F32) for shape in shapes],
        compiler_params=params(8),
        cost_estimate=cost(),
    )


def swap(value, axis, bit):
    size = lax.axis_size(axis)
    return lax.ppermute(value, axis, [(i, i ^ bit) for i in range(size)])


def by_index(blocks, index):
    return lax.dynamic_index_in_dim(blocks, index, 0, keepdims=False)


def gather_start(value):
    return [value, swap(value, "stream", 1), swap(value, "stream", 2)]


def gather_end(parts, *later):
    far = after(parts[2], *later) if later else parts[2]
    return parts + [swap(far, "stream", 1)]


def gather_rel(value):
    return gather_end(gather_start(value))


def after(value, *others):
    return lax.optimization_barrier((value, *others))[0]


def add_up(values):
    total = values[0].astype(F32)
    for value in values[1:]:
        total = total + value.astype(F32)
    return total


def add_body(count, *refs):
    refs[count][...] = add_up([ref[...] for ref in refs[:count]]).astype(refs[count].dtype)


def add_part(terms, size, index, deps=()):
    shape = (size,) + terms[0].shape[1:]
    return run(
        functools.partial(add_body, len(terms)),
        terms,
        deps,
        grid=(1,),
        in_specs=[pl.BlockSpec(shape, lambda t: (index, 0, 0))] * len(terms),
        out_specs=whole(shape),
        out_shape=sds(shape, terms[0].dtype),
        compiler_params=params(8),
        cost_estimate=cost(),
    )


def pieces_body(counts, *refs):
    out = refs[-1]
    row = at = 0
    for count in counts:
        terms = refs[at : at + count]
        rows = terms[0].shape[1]
        out[row : row + rows] = add_up([term[0] for term in terms]).astype(out.dtype)
        at += count
        row += rows


def add_pieces(sums, deps=()):
    terms = [term for value in sums for term in value.terms]
    rows = sum(value.terms[0].shape[1] for value in sums)
    shape = (rows, terms[0].shape[2])
    return run(
        functools.partial(pieces_body, [len(value.terms) for value in sums]),
        terms,
        deps,
        grid=(1,),
        in_specs=[pl.BlockSpec((1,) + term.shape[1:], lambda t: (0, 0, 0)) for term in terms],
        out_specs=whole(shape),
        out_shape=sds(shape, terms[0].dtype),
        compiler_params=params(8),
        cost_estimate=cost(),
    )


class Halving:
    def __init__(self, order, terms, size, send=None, deps=()):
        self.order = list(order)
        self.terms = list(terms)
        self.size = size
        if send is None:
            self.more(deps)
        else:
            self.send(send)

    def send(self, value):
        self.size //= 2
        self.last = value
        self.terms.append(swap(value, "items", 1 << self.order.pop(0)))

    def more(self, deps=()):
        if self.order:
            self.send(add_part(self.terms, self.size // 2, 1, deps))
        return self.last

    def drain(self):
        while self.order:
            self.more()
        return self


def per_device(
    tokens,
    cotangent,
    text_len,
    attn_in,
    attn_bias,
    attn_out,
    out_bias,
    norm_gain,
    norm_bias,
    ffn_in,
    ffn_in_bias,
    ffn_out,
    ffn_out_bias,
):
    streams = lax.axis_size("stream")
    item_devs = lax.axis_size("items")
    stream = lax.axis_index("stream")
    item = lax.axis_index("items")
    _, slots, width = tokens.shape
    hidden = ffn_in.shape[2]
    dm = Dims(slots, streams, width, hidden, item_devs)
    share = dm.share
    sc = jnp.stack([by_index(text_len, stream), stream, dm.place(item, dm.order_a), dm.place(item, dm.order_b)])
    sc = jnp.concatenate([sc, text_len]).astype(jnp.int32)

    part = hidden // (item_devs * streams)
    if dm.tiled:
        wi_q, bi_q = select_quarter(dm, sc, ffn_in, ffn_in_bias)
        wo_q = ffn_out
    else:
        wi_q = by_index(jnp.moveaxis(ffn_in.reshape(3, width, item_devs, streams, part), 3, 0), stream).reshape(3, width, width)
        wo_q = by_index(jnp.moveaxis(ffn_out.reshape(3, item_devs, streams, part, width), 2, 0), stream).reshape(3, width, width)
        bi_q = by_index(jnp.moveaxis(ffn_in_bias.reshape(3, item_devs, streams, part), 2, 0), stream).reshape(3, 1, width).astype(F32)

    far = swap(lax.dynamic_slice_in_dim(tokens, 2 * (1 - stream // 2), 2, 0), "stream", 2)
    far = after(far, bi_q)
    near = swap(jnp.stack([by_index(tokens, stream ^ 1), by_index(far, 1 - stream % 2)]), "stream", 1)
    cots = gather_start(after(cotangent, near))

    layer_params = (norm_gain, norm_bias, attn_in, attn_bias, attn_out, out_bias)
    a0 = fwd_attn(dm, 0, sc, (tokens, near, far), *layer_params)
    nc_0, q_0, k_0, v_0, p_0, x1_0, n2_0, n2l_0, x_0 = a0
    nc_near_0 = swap(nc_0, "stream", 1)
    cots = gather_end(cots, n2l_0)
    n2_all_0 = gather_start(n2l_0)
    sv_0, sl_0, x_1 = fwd_ff_two(dm, n2_0, x1_0, ffn_in, ffn_in_bias, ffn_out, ffn_out_bias)
    gf_all_1 = cot_prep(dm, sc, cots, (sv_0,))
    n2_all_0 = gather_end(n2_all_0, sv_0)
    a1 = fwd_attn(dm, 1, sc, (x_1,), *layer_params, deps=(gf_all_1, n2_all_0[3]))
    nc_1, q_1, k_1, v_1, p_1, x1_1, n2_1, n2l_1 = a1
    nc_near_1 = swap(nc_1, "stream", 1)
    n2_all_1 = gather_start(n2l_1)
    mix, g, ga_1, fs_1, hs_1 = top_ff(
        dm, 1, 2, sc, n2_1, gf_all_1, x1_1, norm_gain, ffn_in, ffn_in_bias, ffn_out, ffn_out_bias
    )
    n2_all_1 = gather_end(n2_all_1, fs_1)

    live, vis, lang, text_at = dm.live, dm.vis, dm.lang, dm.text_at
    half = item_devs // 2
    a, b = dm.order_a, dm.order_b

    def reorder(value, order):
        places = jnp.stack([dm.place(jnp.int32(i), order) for i in range(item_devs)])
        source = jnp.zeros((item_devs,), jnp.int32).at[places ^ dm.place(item, order)].set(jnp.arange(item_devs, dtype=jnp.int32))
        value = value.reshape(value.shape[:-2] + (item_devs, share, width))
        return jnp.take(value, source, axis=value.ndim - 3)

    def pairs(values, experts):
        if dm.tiled:
            return [values[2 * k : 2 * k + 2] for k in range(len(values) // 2)]
        out = []
        for index, (*_, orders) in enumerate(experts):
            sides = [reorder(values[2 * index + side], orders[side]) for side in range(2)]
            if orders[0] is orders[1]:
                sides = [jnp.concatenate(sides, axis=1)]
            out += [(value[:half], value[half:]) for value in sides]
        return out

    def halving(pair, order, *later):
        return Halving(order, [pair[0]], item_devs, after(pair[1], *later) if later else pair[1])

    def attn_sum(keep, send):
        if not dm.tiled:
            keep, send = reorder(keep, a), reorder(send, a)
        return [keep, swap(send, "stream", 2)]

    mine_1, near_1, far_1, as_1, g, gf_0 = back_attn(dm, 1, sc, g, ga_1, q_1, k_1, v_1, p_1, x_1, norm_gain, attn_in, attn_out)
    gf_all_0 = gather_start(gf_0)
    near_1, far_1 = swap(near_1, "stream", 1), swap(far_1, "stream", 1)
    experts = ((2, 0, live, 0, live, (a, a)),)
    join = wgrad_ff(dm, experts, sc, n2_all_1, (gf_all_1,), wi_q, wo_q, bi_q, deps=(as_1,))
    join_sum = halving(pairs(join, experts)[0], a)
    gf_all_0 = gather_end(gf_all_0, join[0])
    att_1 = wgrad_attn(dm, sc, nc_1, nc_near_1, mine_1, near_1, far_1, deps=(join[0],))
    att_1_terms = attn_sum(*att_1)
    experts = ((0, 0, vis, 0, text_at, (a, list(a))), (1, lang, live, text_at, live, (a, b)))
    two = wgrad_ff(dm, experts, sc, n2_all_0, gf_all_0, wi_q, wo_q, bi_q, deps=(att_1[0],))
    va, vb, la, lb = pairs(two, experts)
    va_sum = halving(va, a)
    lb_sum = halving(lb, b)
    g, ga_0, fs_0, hs_0 = back_ff_two(
        dm, 0, g, gf_0, x1_0, norm_gain, sv_0, sl_0, ffn_in, ffn_out, deps=(two[0],)
    )
    last = join_sum.more((fs_0,))
    last = lb_sum.more((last,))
    mine_0, near_0, far_0, as_0, tg_own, tg_near, tg_far = back_attn(
        dm, 0, sc, g, ga_0, q_0, k_0, v_0, p_0, x_0, norm_gain, attn_in, attn_out, mix=mix, deps=(last,)
    )
    near_0, far_0 = swap(near_0, "stream", 1), swap(far_0, "stream", 1)
    small = small_pack(dm, sc, (as_0, as_1, fs_0, fs_1, hs_0, hs_1), ())
    last = lb_sum.more((small,))
    last = join_sum.more((last,))
    last = va_sum.more((last,))
    att_1_sum = Halving(a, att_1_terms, item_devs, deps=(last,))
    att_0 = wgrad_attn(dm, sc, nc_0, nc_near_0, mine_0, near_0, far_0, deps=(att_1_sum.last,))
    att_0_terms = attn_sum(*att_0)
    last = va_sum.more((att_0[0],))
    join_piece = add_pieces([join_sum.drain()], deps=(last,))
    last = att_1_sum.more((join_piece,))
    lb_piece = add_pieces([lb_sum.drain()], deps=(last,))
    vb_sum = halving(vb, a, lb_piece)

    va_piece = add_pieces([va_sum.drain()], deps=(lb_piece,))
    last = att_1_sum.more((va_piece,))
    last = vb_sum.more((last,))
    att_0_sum = Halving(a, att_0_terms, item_devs, deps=(last,))
    last = att_0_sum.last
    all_1 = gather_start(jnp.concatenate([join_piece, after(va_piece, last)]))
    small_sum = Halving(a, [small[:half]], item_devs, after(small[half:], last))

    att_1_piece = add_pieces([att_1_sum.drain()], deps=(last,))
    last = vb_sum.more((att_1_piece,))
    last = small_sum.more((last,))
    last = att_0_sum.more((last,))
    tg_far = swap(after(tg_far, all_1[2], last), "stream", 2)
    la_sum = halving(la, a, last)

    vb_piece = add_pieces([vb_sum.drain()], deps=(last,))
    last = small_sum.more((vb_piece,))
    last = att_0_sum.more((last,))
    last = la_sum.more((last,))
    all_1 = gather_end(all_1, last)
    all_2 = gather_start(after(jnp.concatenate([vb_piece, lb_piece, att_1_piece]), tg_far))

    results = finish(dm, sc, [(all_1, 0), (all_1, 1)], 2, (), last)
    small_own = add_pieces([small_sum.drain()], deps=(results[0],))
    small_near = small_own + swap(small_own, "stream", 1)
    att_0_piece = add_pieces([att_0_sum.drain()], deps=(small_own,))
    last = la_sum.more((att_0_piece,))
    all_4 = gather_start(after(att_0_piece, all_2[2]))
    tg_near = swap(jnp.concatenate([tg_near, after(tg_far, last)[1::2]]), "stream", 1)
    all_2 = gather_end(all_2, last)
    mixed, tokens_grad = join_shards(dm, sc, tg_own, tg_near, tg_far, last)
    results = finish(dm, sc, [(all_1, 2), (all_2, 0)], 0, results, mixed)
    la_piece = add_pieces([la_sum.drain()], deps=(results[0],))
    all_3 = gather_start(after(la_piece, all_4[2]))
    small_all = swap(after(small_near, la_piece), "stream", 2)
    attn_results = finish(dm, sc, [(all_2, 2)], 1, (), la_piece)
    all_4 = gather_end(all_4, la_piece)
    attn_results = finish(dm, sc, [(all_4, 0)], 0, attn_results)
    outs = small_unpack(dm, small_near, small_all, attn_results[0])
    all_3 = gather_end(all_3)
    ffn_results = finish(dm, sc, [(all_3, 0), (all_2, 1)], 1, results, outs[0])

    return (
        mixed,
        tokens_grad,
        attn_results[0],
        outs[0],
        attn_results[1],
        outs[1],
        outs[2],
        outs[3],
        ffn_results[0],
        outs[4],
        ffn_results[1],
        outs[5],
    )


def solution(mesh):
    return jax.shard_map(
        per_device,
        mesh=mesh,
        in_specs=(
            P("items", "stream", None),
            P("items", "stream", None),
            P("items"),
            P(),
            P(),
            P(),
            P(),
            P(),
            P(),
            P(),
            P(),
            P(),
            P(),
        ),
        out_specs=(
            P("items", "stream", None),
            P("items", "stream", None),
            P(None, "items", None),
            P(None, None, "items"),
            P(None, "items", None),
            P(None, "items"),
            P(None, None, "items"),
            P(None, None, "items"),
            P(None, "items", None),
            P(None, "items"),
            P(None, "items", None),
            P(None, "items"),
        ),
        check_vma=False,
    )
```

```python
import functools
import jax
import jax.numpy as jnp
from jax import lax
from jax.experimental import pallas as pl
from jax.experimental.pallas import tpu as pltpu
from jax.sharding import PartitionSpec as P

HEADS = 12
PATCHES = 197
TEXT = 40
F32 = jnp.float32
BF = jnp.bfloat16
EPS = 1e-06
FILL = -1e30
MIB = 1 << 20
PAD = 80
TILE = 1024


def dot(left, right, dims=((1,), (0,))):
    return lax.dot_general(left, right, (dims, ((), ())), preferred_element_type=F32)


NT = ((1,), (1,))
TN = ((0,), (0,))


def norm_stats(values):
    row_mean = jnp.mean(values, axis=-1, keepdims=True)
    centred = values - row_mean
    row_var = jnp.mean(centred * centred, axis=-1, keepdims=True)
    inv_std = lax.rsqrt(row_var + EPS)
    return centred * inv_std, inv_std


def norm_back(grad_out, values, gain):
    scaled, inv_std = norm_stats(values)
    grad_scaled = grad_out * gain
    mean_first = jnp.mean(grad_scaled, axis=-1, keepdims=True)
    mean_second = jnp.mean(grad_scaled * scaled, axis=-1, keepdims=True)
    grad_in = inv_std * (grad_scaled - mean_first - scaled * mean_second)
    gain_sum = jnp.sum(grad_out * scaled, axis=0, keepdims=True)
    offset_sum = jnp.sum(grad_out, axis=0, keepdims=True)
    return grad_in, gain_sum, offset_sum


def gelu_parts(pre):
    cumulative = 0.5 * (1.0 + lax.erf(pre * 0.7071067811865476))
    density = jnp.exp(-0.5 * pre * pre) * 0.3989422804014327
    return pre * cumulative, cumulative + pre * density


def params(limit_mib):
    return pltpu.CompilerParams(vmem_limit_bytes=limit_mib * MIB)


def cost():
    return pl.CostEstimate(flops=1, bytes_accessed=1, transcendentals=0)


ONCE = pl.Buffered(1)


def whole(shape):
    return pl.BlockSpec(shape, lambda *_: (0,) * len(shape), pipeline_mode=ONCE)


def layer_block(shape, index):
    return pl.BlockSpec((1,) + shape, lambda *_: (index,) + (0,) * len(shape), pipeline_mode=ONCE)


SMEM = pl.BlockSpec(memory_space=pltpu.SMEM)
ANY = pl.BlockSpec(memory_space=pl.ANY)
sds = jax.ShapeDtypeStruct


TOKENS = {}


def order_after(deps):
    return tuple(TOKENS[id(dep)][1] if id(dep) in TOKENS else dep for dep in deps)


def note(outs, token):
    for out in outs:
        TOKENS[id(out)] = (out, token)


def run(body, args, deps=(), *, in_specs, out_specs, out_shape, grid_spec=None, call=None, **rest):
    deps = order_after(deps)
    count, extra = len(args), len(deps)
    single = not isinstance(out_shape, (list, tuple))
    if single:
        out_specs, out_shape = [out_specs], [out_shape]
    number = len(out_shape)

    def wrapped(*refs):
        outs = refs[count + extra :]
        outs[number][...] = jnp.zeros_like(outs[number])
        body(*refs[:count], *outs[:number], *outs[number + 1 :])

    outs = pl.pallas_call(
        wrapped,
        in_specs=list(in_specs) + [ANY] * extra,
        out_specs=list(out_specs) + [whole((8, 128))],
        out_shape=list(out_shape) + [sds((8, 128), F32)],
        name=call or getattr(body, "func", body).__name__,
        **rest,
    )(*args, *deps)
    *outs, token = outs
    note(outs, token)
    return outs[0] if single else outs


def hbm(value):
    return pltpu.with_memory_space_constraint(value, pltpu.HBM)


def first(shape):
    return lax.broadcasted_iota(jnp.int32, shape, 0)


def second(shape):
    return lax.broadcasted_iota(jnp.int32, shape, 1)


class Dims:
    def __init__(self, slots, streams, width, hidden, item_devs):
        self.slots = slots
        self.text_at = slots * (streams - 1)
        self.rows = slots * streams
        self.full = -(-self.rows // 16) * 16
        self.live = -(-(self.text_at + TEXT) // 16) * 16
        self.keys = -(-self.live // 128) * 128
        self.vis = -(-self.text_at // 16) * 16
        self.lang = self.text_at // 16 * 16
        self.width = width
        self.hidden = hidden
        self.streams = streams
        self.item_devs = item_devs
        self.share = width // item_devs
        self.bits = item_devs.bit_length() - 1
        self.order_a = list(range(self.bits))
        self.order_b = self.order_a[1:] + self.order_a[:1]
        self.tiled = self.share % 16 == 0

    def place(self, index, order):
        out = index * 0
        for k, bit in enumerate(order):
            out = out | (((index >> bit) & 1) << (self.bits - 1 - k))
        return out


def put_stage(dm, stage, pieces):
    stage[...] = jnp.zeros_like(stage)
    for r, piece in enumerate(pieces):
        stage[r * PAD : r * PAD + dm.slots] = piece


def slot_select(dm, rows, stream):
    shape = (rows, 4 * PAD)
    slot = first(shape)
    shard = jnp.zeros(shape, jnp.int32)
    for k in range(1, dm.streams):
        shard = shard + (slot >= k * dm.slots).astype(jnp.int32)
    place = slot - shard * dm.slots
    return second(shape) == ((shard ^ stream) * PAD + place), slot


def shard_rows(dm, rows, shard):
    shape = (-(-dm.slots // 8) * 8, rows)
    return ((second(shape) == first(shape) + shard * dm.slots) & (first(shape) < dm.slots)).astype(BF)


def split_shards(dm, value, stream, refs):
    for r, ref in enumerate(refs):
        ref[...] = dot(shard_rows(dm, value.shape[0], stream ^ r), value)[: dm.slots].astype(BF)


def cot_prep_body(dm, sc, c0, c1, c2, c3, out, stage):
    stream = sc[1]
    pick, slot = slot_select(dm, dm.live, stream)
    for r in range(4):
        put_stage(dm, stage, [c[stream ^ r] for c in (c0, c1, c2, c3)])
        alive = (slot < PATCHES) | ((slot >= dm.text_at) & (slot < dm.text_at + sc[4 + (stream ^ r)]))
        out[r] = dot((pick & alive).astype(BF), stage[...]).astype(BF)


def cot_prep(dm, sc, pieces, deps):
    shape = pieces[0].shape
    return run(
        functools.partial(cot_prep_body, dm),
        (sc, *pieces),
        deps,
        grid=(1,),
        in_specs=[SMEM] + [whole(shape)] * 4,
        out_specs=whole((4, dm.live, dm.width)),
        out_shape=sds((4, dm.live, dm.width), BF),
        scratch_shapes=[pltpu.VMEM((4 * PAD, dm.width), BF)],
        compiler_params=params(12),
        cost_estimate=cost(),
    )


def join_shards_body(sc, own, near, far, mixed, grad):
    stream = sc[1]
    for k, out in enumerate((mixed, grad)):
        for r, value in enumerate((own[k], near[k], far[2 * k], near[2 + k])):
            out[stream ^ r] = value.astype(out.dtype)


def join_shards(dm, sc, own, near, far, *deps):
    shape = (4, dm.slots, dm.width)
    return run(
        join_shards_body,
        (sc, own, near, far),
        deps,
        grid=(1,),
        in_specs=[SMEM, whole(own.shape), whole(near.shape), whole(far.shape)],
        out_specs=[whole(shape)] * 2,
        out_shape=[pltpu.HBM(shape, BF), pltpu.HBM(shape, F32)],
        compiler_params=params(8),
        cost_estimate=cost(),
    )


def select_body(dm, sc, *refs):
    *parts, b, wo, bo = refs
    part = dm.hidden // (dm.item_devs * dm.streams)
    rows = parts[0].shape[1]
    for s in range(dm.streams):

        @pl.when(sc[1] == s)
        def _(s=s):
            starts = [i * part * dm.streams + s * part for i in range(dm.item_devs)]
            for k, w in enumerate(parts):
                wo[0, k * rows : (k + 1) * rows] = jnp.concatenate([w[0, :, at : at + part] for at in starts], axis=1)
            bo[0] = jnp.concatenate([b[0, :, at : at + part].astype(F32) for at in starts], axis=1)


def select_quarter(dm, sc, ffn_in, ffn_in_bias):
    d, hid = dm.width, dm.hidden
    count = ffn_in.shape[0]
    pieces = 4
    return run(
        functools.partial(select_body, dm),
        (sc, *[hbm(ffn_in)] * pieces, ffn_in_bias[:, None]),
        grid=(count,),
        in_specs=[SMEM]
        + [pl.BlockSpec((1, d // pieces, hid), lambda e, k=k: (e, k, 0)) for k in range(pieces)]
        + [pl.BlockSpec((1, 1, hid), lambda e: (e, 0, 0))],
        out_specs=[
            pl.BlockSpec((1, d, d), lambda e: (e, 0, 0)),
            pl.BlockSpec((1, 1, d), lambda e: (e, 0, 0)),
        ],
        out_shape=[sds((count, d, d), BF), sds((count, 1, d), F32)],
        compiler_params=params(60),
        cost_estimate=cost(),
    )


def fwd_attn_body(dm, sc, xv, gain, offset, win, bias, wout, obias, nco, qo, ko, vo, po, x1o, n2o, n2live, ctx_s):
    width = dm.width
    scaled, _ = norm_stats(xv)
    n1 = (scaled * gain[0, 0:1].astype(F32) + offset[0, 0:1].astype(F32)).astype(BF)
    nco[0] = n1[: dm.live]
    w = win.at[0]
    q = (dot(n1, w[:, 0:width]) + bias[0, 0:1].astype(F32)).astype(BF) * 0.125
    q = q.astype(BF)
    k = dot(n1[: dm.keys], w[:, width : 2 * width]).astype(BF)
    v = (dot(n1[: dm.keys], w[:, 2 * width :]) + bias[0, 1:2].astype(F32)).astype(BF)
    qo[...] = q[: dm.live]
    ko[...] = k
    vo[...] = v
    col = lax.broadcasted_iota(jnp.int32, (1, dm.keys), 1)
    valid = (col < PATCHES) | ((col >= dm.text_at) & (col < dm.text_at + sc[0]))
    low_lane = lax.broadcasted_iota(jnp.int32, (1, 128), 1) < 64
    for pair in range(HEADS // 2):
        lanes = slice(pair * 128, pair * 128 + 128)
        qp, kp, vp = q[:, lanes], k[:, lanes], v[:, lanes]
        outs = []
        for j in range(2):
            qm = jnp.where(low_lane if j == 0 else ~low_lane, qp, jnp.zeros_like(qp))
            scores = jnp.where(valid, dot(qm, kp, NT), FILL)
            top = jnp.max(scores, axis=-1, keepdims=True)
            expo = jnp.exp(scores - top)
            probs = (expo / jnp.sum(expo, axis=-1, keepdims=True)).astype(BF)
            po[2 * pair + j] = probs[: dm.live]
            outs.append(dot(probs, vp))
        ctx_s[:, lanes] = jnp.where(low_lane, outs[0], outs[1]).astype(BF)
    ctx = ctx_s[...]
    nco[1] = ctx[: dm.live]
    x1 = xv + (dot(ctx, wout[0]) + obias[0].astype(F32))
    x1o[...] = x1
    scaled, _ = norm_stats(x1)
    n2 = (scaled * gain[0, 1:2].astype(F32) + offset[0, 1:2].astype(F32)).astype(BF)
    n2o[...] = n2
    n2live[...] = n2[: dm.live]


def fwd_attn_next_body(dm, sc, x, *refs):
    fwd_attn_body(dm, sc, x[...], *refs)


def fwd_attn_first_body(dm, sc, tokens, near, far, *refs):
    stream = sc[1]
    *refs, x0, ctx_s, stage = refs
    put_stage(dm, stage, [tokens[stream], near[0], far[stream & 1], near[1]])
    pick, _ = slot_select(dm, dm.full, stream)
    xv = dot(pick.astype(BF), stage[...])
    x0[...] = xv.astype(BF)
    fwd_attn_body(dm, sc, xv, *refs, ctx_s)


def fwd_attn(dm, layer, sc, inputs, norm_gain, norm_bias, attn_in, attn_bias, attn_out, out_bias, deps=()):
    d, full, live, keys = dm.width, dm.full, dm.live, dm.keys
    shapes = [
        sds((2, live, d), BF),
        sds((live, d), BF),
        sds((keys, d), BF),
        sds((keys, d), BF),
        sds((HEADS, live, keys), BF),
        sds((full, d), F32),
        sds((full, d), BF),
        sds((live, d), BF),
    ]
    scratch = [pltpu.VMEM((full, d), BF)]
    body = fwd_attn_next_body
    if len(inputs) > 1:
        body = fwd_attn_first_body
        shapes.append(sds((full, d), BF))
        scratch.append(pltpu.VMEM((4 * PAD, d), BF))
    return run(
        functools.partial(body, dm),
        (sc, *inputs, norm_gain, norm_bias, hbm(attn_in), attn_bias, hbm(attn_out), out_bias[:, None]),
        deps,
        grid=(1,),
        in_specs=[SMEM]
        + [whole(value.shape) for value in inputs]
        + [
            layer_block((2, d), layer),
            layer_block((2, d), layer),
            layer_block((d, 3 * d), layer),
            layer_block((2, d), layer),
            layer_block((d, d), layer),
            layer_block((1, d), layer),
        ],
        out_specs=[whole(s.shape) for s in shapes],
        out_shape=shapes,
        scratch_shapes=scratch,
        compiler_params=params(16),
        cost_estimate=cost(),
    )


def fwd_ff_two_body(dm, n2, x1, wv, wl, bi, wov, wol, bo, slope_v, slope_l, x2, acc):
    t = pl.program_id(0)
    vis, lang, text_at = dm.vis, dm.lang, dm.text_at
    rows_v = lax.broadcasted_iota(jnp.int32, (vis, 1), 0) < text_at
    rows_l = lax.broadcasted_iota(jnp.int32, (dm.full - lang, 1), 0) + lang >= text_at
    act_v, sv = gelu_parts(dot(n2[0:vis], wv[0]) + bi[0, 0:1].astype(F32))
    act_l, sl = gelu_parts(dot(n2[lang:], wl[0]) + bi[1, 0:1].astype(F32))
    slope_v[...] = sv.astype(BF)
    slope_l[...] = sl[: dm.live - lang].astype(BF)
    part_v = dot(act_v.astype(BF), wov[0])
    part_l = dot(act_l.astype(BF), wol[0])

    @pl.when(t == 0)
    def _():
        acc[...] = x1[...]
        part_vb = part_v + bo[0, 0:1].astype(F32)
        part_lb = part_l + bo[1, 0:1].astype(F32)
        acc[0:vis] += jnp.where(rows_v, part_vb, 0.0)
        acc[lang:] += jnp.where(rows_l, part_lb, 0.0)

    @pl.when(t > 0)
    def _():
        acc[0:vis] += jnp.where(rows_v, part_v, 0.0)
        acc[lang:] += jnp.where(rows_l, part_l, 0.0)

    @pl.when(t == pl.num_programs(0) - 1)
    def _():
        x2[...] = acc[...]


def fwd_ff_two(dm, n2, x1, ffn_in, ffn_in_bias, ffn_out, ffn_out_bias, deps=()):
    d, full, hid = dm.width, dm.full, dm.hidden
    count = ffn_in.shape[0]
    return run(
        functools.partial(fwd_ff_two_body, dm),
        (n2, x1, hbm(ffn_in), hbm(ffn_in), ffn_in_bias[:, None], hbm(ffn_out), hbm(ffn_out), ffn_out_bias[:, None]),
        deps,
        grid=(hid // TILE,),
        in_specs=[
            whole((full, d)),
            whole((full, d)),
            pl.BlockSpec((1, d, TILE), lambda t: (0, 0, t)),
            pl.BlockSpec((1, d, TILE), lambda t: (1, 0, t)),
            pl.BlockSpec((count, 1, TILE), lambda t: (0, 0, t)),
            pl.BlockSpec((1, TILE, d), lambda t: (0, t, 0)),
            pl.BlockSpec((1, TILE, d), lambda t: (1, t, 0)),
            whole((count, 1, d)),
        ],
        out_specs=[
            pl.BlockSpec((dm.vis, TILE), lambda t: (0, t)),
            pl.BlockSpec((dm.live - dm.lang, TILE), lambda t: (0, t)),
            whole((full, d)),
        ],
        out_shape=[sds((dm.vis, hid), BF), sds((dm.live - dm.lang, hid), BF), sds((full, d), F32)],
        scratch_shapes=[pltpu.VMEM((full, d), F32)],
        compiler_params=params(36),
        cost_estimate=cost(),
    )


def finish_ff_back(dm, g, gn, x1, gain, go, ga, sums):
    grad_in, gain_sum, offset_sum = norm_back(gn, x1[0 : dm.live], gain[0, 1:2].astype(F32))
    out = g + grad_in
    go[...] = out
    low = out.astype(BF)
    ga[...] = low
    sums[0:1] = gain_sum
    sums[1:2] = offset_sum
    sums[2:3] = jnp.sum(low.astype(F32), axis=0, keepdims=True)


def top_ff_body(dm, sc, n2, gf, x1, gain, wi, bi, wo, bo, mix, go, ga, sums, hsum, accm, accg):
    t = pl.program_id(0)
    act, slope = gelu_parts(dot(n2[...], wi[0]) + bi[0].astype(F32))
    gpre = (dot(gf[0], wo[0], NT) * slope[: dm.live]).astype(BF)
    hsum[...] = jnp.sum(gpre.astype(F32), axis=0, keepdims=True)
    part = dot(act.astype(BF), wo[0])
    back = dot(gpre, wi[0], NT)

    @pl.when(t == 0)
    def _():
        accm[...] = part + (x1[...] + bo[0].astype(F32))
        accg[...] = back

    @pl.when(t > 0)
    def _():
        accm[...] += part
        accg[...] += back

    @pl.when(t == pl.num_programs(0) - 1)
    def _():
        split_shards(dm, accm[...].astype(BF), sc[1], [mix.at[r] for r in range(4)])
        g = gf[0].astype(F32)
        sums[3:4] = jnp.sum(g, axis=0, keepdims=True)
        finish_ff_back(dm, g, accg[...], x1, gain, go, ga, sums)


def top_ff(dm, layer, expert, sc, n2, gf, x1, norm_gain, ffn_in, ffn_in_bias, ffn_out, ffn_out_bias, deps=()):
    d, full, live, hid, slots = dm.width, dm.full, dm.live, dm.hidden, dm.slots
    shapes = [
        sds((4, slots, d), BF),
        sds((live, d), F32),
        sds((live, d), BF),
        sds((4, d), F32),
    ]
    return run(
        functools.partial(top_ff_body, dm),
        (sc, n2, gf, x1, norm_gain, hbm(ffn_in), ffn_in_bias[:, None], hbm(ffn_out), ffn_out_bias[:, None]),
        deps,
        grid=(hid // TILE,),
        in_specs=[
            SMEM,
            whole((full, d)),
            layer_block((live, d), 0),
            whole((full, d)),
            layer_block((2, d), layer),
            pl.BlockSpec((1, d, TILE), lambda t: (expert, 0, t)),
            pl.BlockSpec((1, 1, TILE), lambda t: (expert, 0, t)),
            pl.BlockSpec((1, TILE, d), lambda t: (expert, t, 0)),
            layer_block((1, d), expert),
        ],
        out_specs=[whole(s.shape) for s in shapes] + [pl.BlockSpec((1, TILE), lambda t: (0, t))],
        out_shape=shapes + [sds((1, hid), F32)],
        scratch_shapes=[pltpu.VMEM((full, d), F32), pltpu.VMEM((live, d), F32)],
        compiler_params=params(36),
        cost_estimate=cost(),
    )


def back_ff_two_body(dm, g, gf, x1, gain, slv, sll, wov, wol, wv, wl, go, ga, sums, hsum, acc):
    t = pl.program_id(0)
    vis, lang, text_at, live = dm.vis, dm.lang, dm.text_at, dm.live
    rows_v = lax.broadcasted_iota(jnp.int32, (vis, 1), 0) < text_at
    rows_l = lax.broadcasted_iota(jnp.int32, (live - lang, 1), 0) + lang >= text_at
    gv = jnp.where(rows_v, gf[0:vis].astype(F32), 0.0)
    gl = jnp.where(rows_l, gf[lang:].astype(F32), 0.0)
    pre_v = (dot(gv.astype(BF), wov[0], NT) * slv[...].astype(F32)).astype(BF)
    pre_l = (dot(gl.astype(BF), wol[0], NT) * sll[...].astype(F32)).astype(BF)
    hsum[0:1] = jnp.sum(pre_v.astype(F32), axis=0, keepdims=True)
    hsum[1:2] = jnp.sum(pre_l.astype(F32), axis=0, keepdims=True)
    part_v = dot(pre_v, wv[0], NT)
    part_l = dot(pre_l, wl[0], NT)

    @pl.when(t == 0)
    def _():
        acc[...] = jnp.zeros_like(acc)

    acc[0:vis] += part_v
    acc[lang:] += part_l

    @pl.when(t == pl.num_programs(0) - 1)
    def _():
        sums[3:4] = jnp.sum(gv, axis=0, keepdims=True)
        sums[4:5] = jnp.sum(gl, axis=0, keepdims=True)
        finish_ff_back(dm, g[...], acc[...], x1, gain, go, ga, sums)


def back_ff_two(dm, layer, g, gf, x1, norm_gain, slope_v, slope_l, ffn_in, ffn_out, deps=()):
    d, live, hid = dm.width, dm.live, dm.hidden
    return run(
        functools.partial(back_ff_two_body, dm),
        (g, gf, x1, norm_gain, slope_v, slope_l, hbm(ffn_out), hbm(ffn_out), hbm(ffn_in), hbm(ffn_in)),
        deps,
        grid=(hid // TILE,),
        in_specs=[
            whole((live, d)),
            whole((live, d)),
            whole((dm.full, d)),
            layer_block((2, d), layer),
            pl.BlockSpec((dm.vis, TILE), lambda t: (0, t)),
            pl.BlockSpec((live - dm.lang, TILE), lambda t: (0, t)),
            pl.BlockSpec((1, TILE, d), lambda t: (0, t, 0)),
            pl.BlockSpec((1, TILE, d), lambda t: (1, t, 0)),
            pl.BlockSpec((1, d, TILE), lambda t: (0, 0, t)),
            pl.BlockSpec((1, d, TILE), lambda t: (1, 0, t)),
        ],
        out_specs=[
            whole((live, d)),
            whole((live, d)),
            whole((5, d)),
            pl.BlockSpec((2, TILE), lambda t: (0, t)),
        ],
        out_shape=[sds((live, d), F32), sds((live, d), BF), sds((5, d), F32), sds((2, hid), F32)],
        scratch_shapes=[pltpu.VMEM((live, d), F32)],
        compiler_params=params(36),
        cost_estimate=cost(),
    )


def back_attn_body(dm, bottom, sc, g, ga, q, k, v, p, x, gain, win, wout, *refs):
    width, live = dm.width, dm.live
    *refs, parts = refs
    mine, other_near, other_far, sums, *outs = refs[1:] if bottom else refs
    gc = dot(ga[...], wout[0], NT).astype(BF)
    low_lane = lax.broadcasted_iota(jnp.int32, (1, 128), 1) < 64
    for pair in range(HEADS // 2):
        lanes = slice(pair * 128, pair * 128 + 128)
        gp, qp, kp, vp = gc[:, lanes], q[:, lanes], k[:, lanes], v[:, lanes]
        dqs, dks, dvs = [], [], []
        for j in range(2):
            gm = jnp.where(low_lane if j == 0 else ~low_lane, gp, jnp.zeros_like(gp))
            dprob = dot(gm, vp, NT)
            prob_low = p[2 * pair + j]
            prob = prob_low.astype(F32)
            inner = jnp.sum(prob * dprob, axis=-1, keepdims=True)
            ds = (prob * (dprob - inner)).astype(BF)
            dqs.append(dot(ds, kp))
            dks.append(dot(ds, qp, TN))
            dvs.append(dot(prob_low, gp, TN))
        dq = jnp.where(low_lane, dqs[0], dqs[1]) * 0.125
        dk = jnp.where(low_lane, dks[0], dks[1])
        dv = jnp.where(low_lane, dvs[0], dvs[1])
        parts[0, :, lanes] = dq.astype(BF)
        parts[1, :, lanes] = dk[:live].astype(BF)
        parts[2, :, lanes] = dv[:live].astype(BF)
    parts[3] = ga[...]
    mine[0] = parts[sc[1]]
    mine[1] = parts[sc[1] ^ 2]
    other_near[...] = parts[sc[1] ^ 1]
    other_far[...] = parts[sc[1] ^ 3]
    gn = sum(dot(parts[k], win[0, :, k * width : (k + 1) * width], NT) for k in range(3))
    grad_in, gain_sum, offset_sum = norm_back(gn, x[0:live].astype(F32), gain[0, 0:1].astype(F32))
    out = g[...] + grad_in
    if bottom:
        own, near, far = outs
        split_shards(dm, out.astype(BF), sc[1], (own.at[1], near.at[1], far.at[2], far.at[3]))
        for r, ref in enumerate((own.at[0], near.at[0], far.at[0], far.at[1])):
            ref[...] = refs[0][r]
    else:
        outs[0][...] = out
        outs[1][...] = out.astype(BF)
    sums[0:1] = gain_sum
    sums[1:2] = offset_sum
    sums[2:3] = jnp.sum(parts[0].astype(F32), axis=0, keepdims=True)
    sums[3:4] = jnp.sum(parts[2].astype(F32), axis=0, keepdims=True)


def back_attn(dm, layer, sc, g, ga, q, k, v, p, x, norm_gain, attn_in, attn_out, mix=None, deps=()):
    d, live, keys, slots = dm.width, dm.live, dm.keys, dm.slots
    bottom = layer == 0
    shapes = [sds((2, live, d), BF), sds((live, d), BF), sds((live, d), BF), sds((4, d), F32)]
    if bottom:
        shapes += [sds((2, slots, d), BF), sds((2, slots, d), BF), sds((4, slots, d), BF)]
    else:
        shapes += [sds((live, d), F32), sds((live, d), BF)]
    return run(
        functools.partial(back_attn_body, dm, bottom),
        (sc, g, ga, q, k, v, p, x, norm_gain, hbm(attn_in), hbm(attn_out)) + ((mix,) if bottom else ()),
        deps,
        grid=(1,),
        in_specs=[
            SMEM,
            whole((live, d)),
            whole((live, d)),
            whole((live, d)),
            whole((keys, d)),
            whole((keys, d)),
            whole((HEADS, live, keys)),
            whole((dm.full, d)),
            layer_block((2, d), layer),
            layer_block((d, 3 * d), layer),
            layer_block((d, d), layer),
        ]
        + ([whole(mix.shape)] if bottom else []),
        out_specs=[whole(s.shape) for s in shapes],
        out_shape=shapes,
        scratch_shapes=[pltpu.VMEM((4, live, d), BF)],
        compiler_params=params(16),
        cost_estimate=cost(),
    )


def store_shares(dm, refs, row, value, order, flip, stage):
    keep, send = refs
    n, share = dm.item_devs, dm.share
    half = n // 2
    for i in range(n):
        stage[i] = value[i * share : (i + 1) * share]
    for p in range(n):
        ref = keep if p < half else send
        index = unplace(dm, p ^ flip, order)
        ref[p % half, row : row + share] = stage[index]


def unplace(dm, place, order):
    out = place * 0
    for k, bit in enumerate(order):
        out = out | (((place >> (dm.bits - 1 - k)) & 1) << bit)
    return out


def wgrad_attn_body(dm, sc, nc, nc_near, mine, got_near, got_far, keep, send, left, right):
    n, live = dm.item_devs, dm.live
    for k, (got, ref) in enumerate(((got_near, keep), (got_far, send))):
        side = jnp.where((sc[1] ^ (2 * k)) == 3, 1, 0)
        left[0:live] = nc[side]
        left[live:] = nc_near[side]
        right[0:live] = mine[k]
        right[live:] = got[...]
        value = dot(left[...], right[...], TN).astype(BF)
        if dm.tiled:
            for i in range(n):
                ref[dm.place(i, dm.order_a) ^ sc[2]] = value[i * dm.share : (i + 1) * dm.share]
        else:
            ref[...] = value


def wgrad_attn(dm, sc, nc, nc_near, mine, got_near, got_far, deps=()):
    d, live, n, share = dm.width, dm.live, dm.item_devs, dm.share
    shape = (n, share, d) if dm.tiled else (d, d)
    args = (sc, nc, nc_near, mine, got_near, got_far)
    return run(
        functools.partial(wgrad_attn_body, dm),
        args,
        deps,
        grid=(1,),
        in_specs=[SMEM] + [whole(value.shape) for value in args[1:]],
        out_specs=[whole(shape)] * 2,
        out_shape=[sds(shape, BF)] * 2,
        scratch_shapes=[pltpu.VMEM((2 * live, d), BF)] * 2,
        compiler_params=params(12),
        cost_estimate=cost(),
    )


def ff_layout(dm, experts):
    rows, where = [], {}
    for index, (*_, orders) in enumerate(experts):
        for side in range(2):
            if side and orders[0] is orders[1] and dm.tiled:
                rows[-1] += dm.share
            else:
                rows.append(dm.share)
            where[index, side] = (len(rows) - 1, rows[-1] - dm.share)
    return rows, where


def wgrad_ff_body(dm, experts, stacked, sc, *refs):
    d, streams = dm.width, dm.streams
    n2s = refs[0:streams]
    gfs, refs = ([refs[streams].at[r] for r in range(streams)], refs[streams + 1 :]) if stacked else (refs[streams : 2 * streams], refs[2 * streams :])
    count = len(experts)
    wi, wo, bi = refs[:3]
    outs = refs[3:-5]
    n2a, gfa, acta, gpa, stage = refs[-5:]
    _, where = ff_layout(dm, experts)
    for index, (expert, start, stop, low, high, orders) in enumerate(experts):
        size = stop - start
        total = size * streams
        rows = first((size, 1)) + start
        keep = (rows >= low) & (rows < high)
        for r in range(streams):
            n2a[r * size : (r + 1) * size] = n2s[r][start:stop]
            gpart = gfs[r][start:stop]
            if low > start or high < stop:
                gpart = jnp.where(keep, gpart.astype(F32), 0.0).astype(BF)
            gfa[r * size : (r + 1) * size] = gpart
        chunk = size if size >= 128 else total
        wi_e = wi.at[index]
        wo_e = wo[index].reshape(d, d)

        def step(c, carry, chunk=chunk, wi_e=wi_e, wo_e=wo_e, index=index):
            at = pl.ds(pl.multiple_of(c * chunk, 16), chunk)
            act, slope = gelu_parts(dot(n2a[at], wi_e[...]) + bi[index])
            acta[at] = act.astype(BF)
            gpa[at] = (dot(gfa[at], wo_e, NT) * slope).astype(BF)
            return carry

        lax.fori_loop(0, total // chunk, step, 0)
        for side, (left, right) in enumerate(((n2a, gpa), (acta, gfa))):
            value = dot(left[0:total], right[0:total], TN).astype(BF)
            pair, row = where[index, side]
            if not dm.tiled:
                outs[pair][...] = value
                continue
            store_shares(dm, outs[2 * pair : 2 * pair + 2], row, value, orders[side], sc[2] if orders[side] == dm.order_a else sc[3], stage)


def wgrad_ff(dm, experts, sc, n2s, gfs, wi, wo, bi, deps=()):
    d, live, n, share, streams = dm.width, dm.live, dm.item_devs, dm.share, dm.streams
    count = len(experts)
    base = experts[0][0]
    part = d // n
    stacked = len(gfs) == 1
    pair_rows, _ = ff_layout(dm, experts)
    shapes = [(n // 2, rows, d) for rows in pair_rows for _ in range(2)] if dm.tiled else [(d, d)] * len(pair_rows)
    top = max(e[2] - e[1] for e in experts) * streams
    if dm.tiled:
        wo = wo.reshape(wo.shape[0], n, streams, part, d)
        wo_spec = pl.BlockSpec((count, n, None, part, d), lambda t, s: (base // count, 0, s[1], 0, 0), pipeline_mode=ONCE)
    else:
        wo_spec = pl.BlockSpec((count, d, d), lambda t, s: (base // count, 0, 0), pipeline_mode=ONCE)

    body = functools.partial(wgrad_ff_body, dm, experts, stacked)
    deps = order_after(deps)
    extra = len(deps)
    args = (*n2s, *gfs, wi, hbm(wo), bi)
    number = len(shapes)

    def wrapped(*refs):
        outs = refs[1 + len(args) + extra :]
        outs[number][...] = jnp.zeros_like(outs[number])
        body(*refs[: 1 + len(args)], *outs[:number], *outs[number + 1 :])

    gf_specs = [pl.BlockSpec((streams, live, d), lambda t, s: (0, 0, 0), pipeline_mode=ONCE)] if stacked else [pl.BlockSpec((live, d), lambda t, s: (0, 0), pipeline_mode=ONCE)] * streams
    *outs, token = pl.pallas_call(
        wrapped,
        grid_spec=pltpu.PrefetchScalarGridSpec(
            num_scalar_prefetch=1,
            grid=(1,),
            in_specs=[pl.BlockSpec((live, d), lambda t, s: (0, 0), pipeline_mode=ONCE)] * streams
            + gf_specs
            + [
                pl.BlockSpec((count, d, d), lambda t, s: (base // count, 0, 0), pipeline_mode=ONCE),
                wo_spec,
                pl.BlockSpec((count, 1, d), lambda t, s: (base // count, 0, 0), pipeline_mode=ONCE),
            ]
            + [ANY] * extra,
            out_specs=[pl.BlockSpec(shape, lambda t, s, shape=shape: (0,) * len(shape), pipeline_mode=ONCE) for shape in [*shapes, (8, 128)]],
            scratch_shapes=[pltpu.VMEM((top, d), BF)] * 4 + [pltpu.VMEM((n, share, d), BF)],
        ),
        out_shape=[sds(shape, BF) for shape in shapes] + [sds((8, 128), F32)],
        compiler_params=params(24),
        cost_estimate=cost(),
        name="wgrad_ff_body",
    )(sc, *args, *deps)
    note(outs, token)
    return outs


def finish_body(dm, sc, *refs):
    *pieces, first_out, second_out, stage = refs
    share, part = dm.share, dm.hidden // (dm.item_devs * dm.streams)
    expert = len(pieces) == 8
    for k, piece in enumerate(pieces):
        stage[k // 4, sc[1] ^ (k % 4)] = piece[...]
    if expert:
        for i in range(dm.item_devs):
            block = [stage[0, q, :, i * part : (i + 1) * part].astype(F32) for q in range(4)]
            first_out[0, :, i * 4 * part : (i + 1) * 4 * part] = jnp.concatenate(block, axis=1)
        for q in range(4):
            second_out[0, q * share : (q + 1) * share] = stage[1, q].astype(F32)
    else:
        for q in range(3):
            first_out[0, :, q * dm.width : (q + 1) * dm.width] = stage[0, q].astype(F32)
        second_out[0] = stage[0, 3].astype(F32)


def finish(dm, sc, sources, index, bases, *deps):
    share, d, hid = dm.share, dm.width, dm.hidden
    expert = len(sources) == 2
    if expert:
        shapes = [(3, share, hid), (3, 4 * share, d)]
    else:
        shapes = [(2, share, 3 * d), (2, share, d)]
    args, specs = [sc], [SMEM]
    for arrays, block in sources:
        args += arrays
        if dm.tiled:
            specs += [pl.BlockSpec((share, d), lambda t, block=block: (block, 0), pipeline_mode=ONCE)] * 4
        else:
            args[-4:] = [value[block * share : (block + 1) * share] for value in arrays]
            specs += [whole((share, d))] * 4
    deps = order_after(deps)
    count, extra = len(args), len(bases)

    def body(*refs):
        outs = refs[count + extra + len(deps) :]
        outs[2][...] = jnp.zeros_like(outs[2])
        finish_body(dm, *refs[:count], *outs[:2], outs[3])

    *outs, token = pl.pallas_call(
        body,
        grid=(1,),
        in_specs=specs + [pl.BlockSpec(memory_space=pltpu.HBM)] * extra + [ANY] * len(deps),
        out_specs=[
            pl.BlockSpec((1,) + shape[1:], lambda t: (index, 0, 0), pipeline_mode=ONCE) for shape in shapes
        ]
        + [whole((8, 128))],
        out_shape=[pltpu.HBM(shape, F32) for shape in shapes] + [sds((8, 128), F32)],
        scratch_shapes=[pltpu.VMEM((len(sources), 4, share, d), BF)],
        input_output_aliases={count + k: k for k in range(extra)},
        compiler_params=params(12),
        cost_estimate=cost(),
        name="finish_body",
    )(*args, *bases, *deps)
    note(outs, token)
    return outs


SMALL_ROWS = 32


def small_body(dm, sc, a0, a1, f0, f1, h0, h1, out):
    out[...] = jnp.zeros_like(out)
    share = dm.share
    wide = jnp.concatenate(
        [
            a0[2:4], a1[2:4],
            f0[2:3], f1[2:3],
            a0[0:1], f0[0:1], a1[0:1], f1[0:1],
            a0[1:2], f0[1:2], a1[1:2], f1[1:2],
            f0[3:5], f1[3:4],
        ],
        axis=0,
    )
    hidden = jnp.concatenate([h0[...], h1[...]], axis=0)
    count = wide.shape[0]
    for i in range(dm.item_devs):
        place = dm.place(i, dm.order_a) ^ sc[2]
        out[place, 0:count, 0:share] = wide[:, i * share : (i + 1) * share]
        for q in range(4):
            at = (i * 4 + q) * share
            out[place, count + 3 * q : count + 3 * q + 3, 0:share] = hidden[:, at : at + share]


def small_pack(dm, sc, values, deps):
    shape = (dm.item_devs, SMALL_ROWS, 128)
    return run(
        functools.partial(small_body, dm),
        (sc, *values),
        deps,
        grid=(1,),
        in_specs=[SMEM] + [whole(value.shape) for value in values],
        out_specs=whole(shape),
        out_shape=sds(shape, F32),
        compiler_params=params(8),
        cost_estimate=cost(),
    )


def small_out_body(dm, near, far, attn_bias, out_bias, gain, offset, hidden, ffn_bias):
    share = dm.share
    total = near[:, 0:share] + far[:, 0:share]
    for l in range(2):
        attn_bias[l] = total[2 * l : 2 * l + 2]
        gain[l] = total[6 + 2 * l : 8 + 2 * l]
        offset[l] = total[10 + 2 * l : 12 + 2 * l]
    out_bias[...] = total[4:6]
    ffn_bias[...] = total[14:17]
    hidden[...] = jnp.concatenate([total[17 + 3 * q : 20 + 3 * q] for q in range(4)], axis=1)


def small_unpack(dm, near, far, *deps):
    share = dm.share
    shapes = [(2, 2, share), (2, share), (2, 2, share), (2, 2, share), (3, 4 * share), (3, share)]
    return run(
        functools.partial(small_out_body, dm),
        (near, far),
        deps,
        grid=(1,),
        in_specs=[whole(near.shape)] * 2,
        out_specs=[whole(shape) for shape in shapes],
        out_shape=[sds(shape, F32) for shape in shapes],
        compiler_params=params(8),
        cost_estimate=cost(),
    )


def swap(value, axis, bit):
    size = lax.axis_size(axis)
    return lax.ppermute(value, axis, [(i, i ^ bit) for i in range(size)])


def by_index(blocks, index):
    return lax.dynamic_index_in_dim(blocks, index, 0, keepdims=False)


def gather_start(value):
    return [value, swap(value, "stream", 1), swap(value, "stream", 2)]


def gather_end(parts, *later):
    far = after(parts[2], *later) if later else parts[2]
    return parts + [swap(far, "stream", 1)]


def gather_rel(value):
    return gather_end(gather_start(value))


def after(value, *others):
    return lax.optimization_barrier((value, *others))[0]


def add_up(values):
    total = values[0].astype(F32)
    for value in values[1:]:
        total = total + value.astype(F32)
    return total


def add_body(count, *refs):
    refs[count][...] = add_up([ref[...] for ref in refs[:count]]).astype(refs[count].dtype)


def add_part(terms, size, index, deps=()):
    shape = (size,) + terms[0].shape[1:]
    return run(
        functools.partial(add_body, len(terms)),
        terms,
        deps,
        grid=(1,),
        in_specs=[pl.BlockSpec(shape, lambda t: (index, 0, 0))] * len(terms),
        out_specs=whole(shape),
        out_shape=sds(shape, terms[0].dtype),
        compiler_params=params(8),
        cost_estimate=cost(),
    )


def pieces_body(counts, *refs):
    out = refs[-1]
    row = at = 0
    for count in counts:
        terms = refs[at : at + count]
        rows = terms[0].shape[1]
        out[row : row + rows] = add_up([term[0] for term in terms]).astype(out.dtype)
        at += count
        row += rows


def add_pieces(sums, deps=()):
    terms = [term for value in sums for term in value.terms]
    rows = sum(value.terms[0].shape[1] for value in sums)
    shape = (rows, terms[0].shape[2])
    return run(
        functools.partial(pieces_body, [len(value.terms) for value in sums]),
        terms,
        deps,
        grid=(1,),
        in_specs=[pl.BlockSpec((1,) + term.shape[1:], lambda t: (0, 0, 0)) for term in terms],
        out_specs=whole(shape),
        out_shape=sds(shape, terms[0].dtype),
        compiler_params=params(8),
        cost_estimate=cost(),
    )


class Halving:
    def __init__(self, order, terms, size, send=None, deps=()):
        self.order = list(order)
        self.terms = list(terms)
        self.size = size
        if send is None:
            self.more(deps)
        else:
            self.send(send)

    def send(self, value):
        self.size //= 2
        self.last = value
        self.terms.append(swap(value, "items", 1 << self.order.pop(0)))

    def more(self, deps=()):
        if self.order:
            self.send(add_part(self.terms, self.size // 2, 1, deps))
        return self.last

    def drain(self):
        while self.order:
            self.more()
        return self


def per_device(
    tokens,
    cotangent,
    text_len,
    attn_in,
    attn_bias,
    attn_out,
    out_bias,
    norm_gain,
    norm_bias,
    ffn_in,
    ffn_in_bias,
    ffn_out,
    ffn_out_bias,
):
    streams = lax.axis_size("stream")
    item_devs = lax.axis_size("items")
    stream = lax.axis_index("stream")
    item = lax.axis_index("items")
    _, slots, width = tokens.shape
    hidden = ffn_in.shape[2]
    dm = Dims(slots, streams, width, hidden, item_devs)
    share = dm.share
    sc = jnp.stack([by_index(text_len, stream), stream, dm.place(item, dm.order_a), dm.place(item, dm.order_b)])
    sc = jnp.concatenate([sc, text_len]).astype(jnp.int32)

    part = hidden // (item_devs * streams)
    if dm.tiled:
        wi_q, bi_q = select_quarter(dm, sc, ffn_in, ffn_in_bias)
        wo_q = ffn_out
    else:
        wi_q = by_index(jnp.moveaxis(ffn_in.reshape(3, width, item_devs, streams, part), 3, 0), stream).reshape(3, width, width)
        wo_q = by_index(jnp.moveaxis(ffn_out.reshape(3, item_devs, streams, part, width), 2, 0), stream).reshape(3, width, width)
        bi_q = by_index(jnp.moveaxis(ffn_in_bias.reshape(3, item_devs, streams, part), 2, 0), stream).reshape(3, 1, width).astype(F32)

    far = swap(lax.dynamic_slice_in_dim(tokens, 2 * (1 - stream // 2), 2, 0), "stream", 2)
    far = after(far, bi_q)
    near = swap(jnp.stack([by_index(tokens, stream ^ 1), by_index(far, 1 - stream % 2)]), "stream", 1)
    cots = gather_start(after(cotangent, near))

    layer_params = (norm_gain, norm_bias, attn_in, attn_bias, attn_out, out_bias)
    a0 = fwd_attn(dm, 0, sc, (tokens, near, far), *layer_params)
    nc_0, q_0, k_0, v_0, p_0, x1_0, n2_0, n2l_0, x_0 = a0
    nc_near_0 = swap(nc_0, "stream", 1)
    n2_all_0 = gather_start(n2l_0)
    sv_0, sl_0, x_1 = fwd_ff_two(dm, n2_0, x1_0, ffn_in, ffn_in_bias, ffn_out, ffn_out_bias)
    cots = gather_end(cots, sv_0)
    n2_all_0 = gather_end(n2_all_0, sv_0)
    a1 = fwd_attn(dm, 1, sc, (x_1,), *layer_params)
    nc_1, q_1, k_1, v_1, p_1, x1_1, n2_1, n2l_1 = a1
    nc_near_1 = swap(nc_1, "stream", 1)
    n2_all_1 = gather_start(n2l_1)
    gf_all_1 = cot_prep(dm, sc, cots, (n2l_1, n2_all_0[3]))
    mix, g, ga_1, fs_1, hs_1 = top_ff(
        dm, 1, 2, sc, n2_1, gf_all_1, x1_1, norm_gain, ffn_in, ffn_in_bias, ffn_out, ffn_out_bias
    )
    n2_all_1 = gather_end(n2_all_1, fs_1)

    live, vis, lang, text_at = dm.live, dm.vis, dm.lang, dm.text_at
    half = item_devs // 2
    a, b = dm.order_a, dm.order_b

    def reorder(value, order):
        places = jnp.stack([dm.place(jnp.int32(i), order) for i in range(item_devs)])
        source = jnp.zeros((item_devs,), jnp.int32).at[places ^ dm.place(item, order)].set(jnp.arange(item_devs, dtype=jnp.int32))
        value = value.reshape(value.shape[:-2] + (item_devs, share, width))
        return jnp.take(value, source, axis=value.ndim - 3)

    def pairs(values, experts):
        if dm.tiled:
            return [values[2 * k : 2 * k + 2] for k in range(len(values) // 2)]
        out = []
        for index, (*_, orders) in enumerate(experts):
            sides = [reorder(values[2 * index + side], orders[side]) for side in range(2)]
            if orders[0] is orders[1]:
                sides = [jnp.concatenate(sides, axis=1)]
            out += [(value[:half], value[half:]) for value in sides]
        return out

    def halving(pair, order, *later):
        return Halving(order, [pair[0]], item_devs, after(pair[1], *later) if later else pair[1])

    def attn_sum(keep, send, *later):
        if not dm.tiled:
            keep, send = reorder(keep, a), reorder(send, a)
        return [keep, swap(after(send, *later) if later else send, "stream", 2)]

    experts = ((2, 0, live, 0, live, (a, a)),)
    join = wgrad_ff(dm, experts, sc, n2_all_1, (gf_all_1,), wi_q, wo_q, bi_q, deps=(fs_1,))
    join_sum = halving(pairs(join, experts)[0], a)
    mine_1, near_1, far_1, as_1, g, gf_0 = back_attn(
        dm, 1, sc, g, ga_1, q_1, k_1, v_1, p_1, x_1, norm_gain, attn_in, attn_out, deps=(join[0],)
    )
    gf_all_0 = gather_start(gf_0)
    near_1, far_1 = swap(near_1, "stream", 1), swap(far_1, "stream", 1)
    g, ga_0, fs_0, hs_0 = back_ff_two(dm, 0, g, gf_0, x1_0, norm_gain, sv_0, sl_0, ffn_in, ffn_out)
    gf_all_0 = gather_end(gf_all_0, fs_0)
    att_1 = wgrad_attn(dm, sc, nc_1, nc_near_1, mine_1, near_1, far_1, deps=(fs_0,))
    att_1_terms = attn_sum(*att_1)
    experts = ((0, 0, vis, 0, text_at, (a, list(a))), (1, lang, live, text_at, live, (a, b)))
    last = join_sum.more((att_1[0],))
    two = wgrad_ff(dm, experts, sc, n2_all_0, gf_all_0, wi_q, wo_q, bi_q, deps=(last,))
    va, vb, la, lb = pairs(two, experts)
    va_sum = halving(va, a)
    lb_sum = halving(lb, b)
    last = join_sum.more((two[0],))
    mine_0, near_0, far_0, as_0, tg_own, tg_near, tg_far = back_attn(
        dm, 0, sc, g, ga_0, q_0, k_0, v_0, p_0, x_0, norm_gain, attn_in, attn_out, mix=mix, deps=(last,)
    )
    near_0, far_0 = swap(near_0, "stream", 1), swap(far_0, "stream", 1)
    small = small_pack(dm, sc, (as_0, as_1, fs_0, fs_1, hs_0, hs_1), ())
    last = va_sum.more((small,))
    vb_sum = halving(vb, a, last)
    att_1_sum = Halving(a, att_1_terms, item_devs, deps=(last,))
    last = lb_sum.more((att_1_sum.last,))
    att_0 = wgrad_attn(dm, sc, nc_0, nc_near_0, mine_0, near_0, far_0, deps=(last,))
    att_0_terms = attn_sum(*att_0)
    last = va_sum.more((att_0[0],))
    last = vb_sum.more((last,))
    join_piece = add_pieces([join_sum.drain()], deps=(last,))
    last = vb_sum.more((join_piece,))
    att_0_sum = Halving(a, att_0_terms, item_devs, deps=(last,))
    last = att_1_sum.more((att_0_sum.last,))
    va_piece = add_pieces([va_sum.drain()], deps=(last,))
    last = lb_sum.more((va_piece,))
    la_sum = halving(la, a, last)
    last = att_1_sum.more((last,))
    lb_piece = add_pieces([lb_sum.drain()], deps=(last,))
    vb_piece = add_pieces([vb_sum.drain()], deps=(lb_piece,))
    all_1 = gather_start(jnp.concatenate([join_piece, va_piece, vb_piece, lb_piece]))
    last = att_0_sum.more((vb_piece,))
    small_sum = Halving(a, [small[:half]], item_devs, after(small[half:], last))
    att_1_piece = add_pieces([att_1_sum.drain()], deps=(last,))
    last = att_0_sum.more((att_1_piece,))
    last = small_sum.more((last,))
    last = la_sum.more((last,))
    att_0_piece = add_pieces([att_0_sum.drain()], deps=(last,))
    all_1 = gather_end(all_1, att_0_piece)
    all_2 = gather_start(after(jnp.concatenate([att_0_piece, att_1_piece]), all_1[2]))
    results = finish(dm, sc, [(all_1, 0), (all_1, 1)], 2, (), att_0_piece)
    last = small_sum.more((results[0],))
    last = la_sum.more((last,))
    all_2 = gather_end(all_2, last)
    tg_far = swap(after(tg_far, all_2[2], last), "stream", 2)
    results = finish(dm, sc, [(all_1, 2), (all_1, 3)], 0, results, last)
    small_own = add_pieces([small_sum.drain()], deps=(results[0],))
    small_near = small_own + swap(small_own, "stream", 1)
    la_piece = add_pieces([la_sum.drain()], deps=(small_own,))
    all_3 = gather_start(after(la_piece, tg_far))
    small_all = swap(after(small_near, la_piece), "stream", 2)
    tg_near = swap(jnp.concatenate([tg_near, after(tg_far, la_piece)[1::2]]), "stream", 1)
    attn_results = finish(dm, sc, [(all_2, 1)], 1, (), la_piece)
    attn_results = finish(dm, sc, [(all_2, 0)], 0, attn_results)
    mixed, tokens_grad = join_shards(dm, sc, tg_own, tg_near, tg_far, attn_results[0])
    outs = small_unpack(dm, small_near, small_all, mixed)
    all_3 = gather_end(all_3, outs[0])
    ffn_results = finish(dm, sc, [(all_3, 0), (all_1, 4)], 1, results, outs[0])

    return (
        mixed,
        tokens_grad,
        attn_results[0],
        outs[0],
        attn_results[1],
        outs[1],
        outs[2],
        outs[3],
        ffn_results[0],
        outs[4],
        ffn_results[1],
        outs[5],
    )


def solution(mesh):
    return jax.shard_map(
        per_device,
        mesh=mesh,
        in_specs=(
            P("items", "stream", None),
            P("items", "stream", None),
            P("items"),
            P(),
            P(),
            P(),
            P(),
            P(),
            P(),
            P(),
            P(),
            P(),
            P(),
        ),
        out_specs=(
            P("items", "stream", None),
            P("items", "stream", None),
            P(None, "items", None),
            P(None, None, "items"),
            P(None, "items", None),
            P(None, "items"),
            P(None, None, "items"),
            P(None, None, "items"),
            P(None, "items", None),
            P(None, "items"),
            P(None, "items", None),
            P(None, "items"),
        ),
        check_vma=False,
    )
```

```python
import functools
import jax
import jax.numpy as jnp
from jax import lax
from jax.experimental import pallas as pl
from jax.experimental.pallas import tpu as pltpu
from jax.sharding import PartitionSpec as P

HEADS = 12
PATCHES = 197
TEXT = 40
F32 = jnp.float32
BF = jnp.bfloat16
EPS = 1e-06
FILL = -1e30
MIB = 1 << 20
PAD = 80
TILE = 1024


def dot(left, right, dims=((1,), (0,))):
    return lax.dot_general(left, right, (dims, ((), ())), preferred_element_type=F32)


NT = ((1,), (1,))
TN = ((0,), (0,))


def norm_stats(values):
    row_mean = jnp.mean(values, axis=-1, keepdims=True)
    centred = values - row_mean
    row_var = jnp.mean(centred * centred, axis=-1, keepdims=True)
    inv_std = lax.rsqrt(row_var + EPS)
    return centred * inv_std, inv_std


def norm_back(grad_out, values, gain):
    scaled, inv_std = norm_stats(values)
    grad_scaled = grad_out * gain
    mean_first = jnp.mean(grad_scaled, axis=-1, keepdims=True)
    mean_second = jnp.mean(grad_scaled * scaled, axis=-1, keepdims=True)
    grad_in = inv_std * (grad_scaled - mean_first - scaled * mean_second)
    gain_sum = jnp.sum(grad_out * scaled, axis=0, keepdims=True)
    offset_sum = jnp.sum(grad_out, axis=0, keepdims=True)
    return grad_in, gain_sum, offset_sum


def gelu_parts(pre):
    cumulative = 0.5 * (1.0 + lax.erf(pre * 0.7071067811865476))
    density = jnp.exp(-0.5 * pre * pre) * 0.3989422804014327
    return pre * cumulative, cumulative + pre * density


def params(limit_mib):
    return pltpu.CompilerParams(vmem_limit_bytes=limit_mib * MIB)


def cost():
    return pl.CostEstimate(flops=1, bytes_accessed=1, transcendentals=0)


ONCE = pl.Buffered(1)


def whole(shape):
    return pl.BlockSpec(shape, lambda *_: (0,) * len(shape), pipeline_mode=ONCE)


def layer_block(shape, index):
    return pl.BlockSpec((1,) + shape, lambda *_: (index,) + (0,) * len(shape), pipeline_mode=ONCE)


SMEM = pl.BlockSpec(memory_space=pltpu.SMEM)
ANY = pl.BlockSpec(memory_space=pl.ANY)
sds = jax.ShapeDtypeStruct


TOKENS = {}


def order_after(deps):
    return tuple(TOKENS[id(dep)][1] if id(dep) in TOKENS else dep for dep in deps)


def note(outs, token):
    for out in outs:
        TOKENS[id(out)] = (out, token)


def run(body, args, deps=(), *, in_specs, out_specs, out_shape, grid_spec=None, call=None, **rest):
    deps = order_after(deps)
    count, extra = len(args), len(deps)
    single = not isinstance(out_shape, (list, tuple))
    if single:
        out_specs, out_shape = [out_specs], [out_shape]
    number = len(out_shape)

    def wrapped(*refs):
        outs = refs[count + extra :]
        outs[number][...] = jnp.zeros_like(outs[number])
        body(*refs[:count], *outs[:number], *outs[number + 1 :])

    outs = pl.pallas_call(
        wrapped,
        in_specs=list(in_specs) + [ANY] * extra,
        out_specs=list(out_specs) + [whole((8, 128))],
        out_shape=list(out_shape) + [sds((8, 128), F32)],
        name=call or getattr(body, "func", body).__name__,
        **rest,
    )(*args, *deps)
    *outs, token = outs
    note(outs, token)
    return outs[0] if single else outs


def hbm(value):
    return pltpu.with_memory_space_constraint(value, pltpu.HBM)


def first(shape):
    return lax.broadcasted_iota(jnp.int32, shape, 0)


def second(shape):
    return lax.broadcasted_iota(jnp.int32, shape, 1)


class Dims:
    def __init__(self, slots, streams, width, hidden, item_devs):
        self.slots = slots
        self.text_at = slots * (streams - 1)
        self.rows = slots * streams
        self.full = -(-self.rows // 16) * 16
        self.live = -(-(self.text_at + TEXT) // 16) * 16
        self.keys = -(-self.live // 128) * 128
        self.vis = -(-self.text_at // 16) * 16
        self.lang = self.text_at // 16 * 16
        self.width = width
        self.hidden = hidden
        self.streams = streams
        self.item_devs = item_devs
        self.share = width // item_devs
        self.bits = item_devs.bit_length() - 1
        self.order_a = list(range(self.bits))
        self.order_b = self.order_a[1:] + self.order_a[:1]
        self.tiled = self.share % 16 == 0

    def place(self, index, order):
        out = index * 0
        for k, bit in enumerate(order):
            out = out | (((index >> bit) & 1) << (self.bits - 1 - k))
        return out


def put_stage(dm, stage, pieces):
    stage[...] = jnp.zeros_like(stage)
    for r, piece in enumerate(pieces):
        stage[r * PAD : r * PAD + dm.slots] = piece


def slot_select(dm, rows, stream):
    shape = (rows, 4 * PAD)
    slot = first(shape)
    shard = jnp.zeros(shape, jnp.int32)
    for k in range(1, dm.streams):
        shard = shard + (slot >= k * dm.slots).astype(jnp.int32)
    place = slot - shard * dm.slots
    return second(shape) == ((shard ^ stream) * PAD + place), slot


def shard_rows(dm, rows, shard):
    shape = (-(-dm.slots // 8) * 8, rows)
    return ((second(shape) == first(shape) + shard * dm.slots) & (first(shape) < dm.slots)).astype(BF)


def split_shards(dm, value, stream, refs):
    for r, ref in enumerate(refs):
        ref[...] = dot(shard_rows(dm, value.shape[0], stream ^ r), value)[: dm.slots].astype(BF)


def cot_prep_body(dm, sc, lens, c0, c1, c2, c3, out, stage):
    stream = sc[1]
    pick, slot = slot_select(dm, dm.live, stream)
    for r in range(4):
        put_stage(dm, stage, [c[stream ^ r] for c in (c0, c1, c2, c3)])
        alive = (slot < PATCHES) | ((slot >= dm.text_at) & (slot < dm.text_at + lens[stream ^ r]))
        out[r] = dot((pick & alive).astype(BF), stage[...]).astype(BF)


def cot_prep(dm, sc, lens, pieces, deps):
    shape = pieces[0].shape
    return run(
        functools.partial(cot_prep_body, dm),
        (sc, lens, *pieces),
        deps,
        grid=(1,),
        in_specs=[SMEM, SMEM] + [whole(shape)] * 4,
        out_specs=whole((4, dm.live, dm.width)),
        out_shape=sds((4, dm.live, dm.width), BF),
        scratch_shapes=[pltpu.VMEM((4 * PAD, dm.width), BF)],
        compiler_params=params(12),
        cost_estimate=cost(),
    )


def join_shards_body(sc, own, near, far, mixed, grad):
    stream = sc[1]
    for k, out in enumerate((mixed, grad)):
        for r, value in enumerate((own[k], near[k], far[2 * k], near[2 + k])):
            out[stream ^ r] = value.astype(out.dtype)


def join_shards(dm, sc, own, near, far, *deps):
    shape = (4, dm.slots, dm.width)
    return run(
        join_shards_body,
        (sc, own, near, far),
        deps,
        grid=(1,),
        in_specs=[SMEM, whole(own.shape), whole(near.shape), whole(far.shape)],
        out_specs=[whole(shape)] * 2,
        out_shape=[sds(shape, BF), sds(shape, F32)],
        compiler_params=params(8),
        cost_estimate=cost(),
    )


def select_body(dm, sc, *refs):
    *parts, b, wo, bo = refs
    part = dm.hidden // (dm.item_devs * dm.streams)
    rows = parts[0].shape[1]
    for s in range(dm.streams):

        @pl.when(sc[1] == s)
        def _(s=s):
            starts = [i * part * dm.streams + s * part for i in range(dm.item_devs)]
            for k, w in enumerate(parts):
                wo[0, k * rows : (k + 1) * rows] = jnp.concatenate([w[0, :, at : at + part] for at in starts], axis=1)
            bo[0] = jnp.concatenate([b[0, :, at : at + part].astype(F32) for at in starts], axis=1)


def select_quarter(dm, sc, ffn_in, ffn_in_bias):
    d, hid = dm.width, dm.hidden
    count = ffn_in.shape[0]
    pieces = 4
    return run(
        functools.partial(select_body, dm),
        (sc, *[hbm(ffn_in)] * pieces, ffn_in_bias[:, None]),
        grid=(count,),
        in_specs=[SMEM]
        + [pl.BlockSpec((1, d // pieces, hid), lambda e, k=k: (e, k, 0)) for k in range(pieces)]
        + [pl.BlockSpec((1, 1, hid), lambda e: (e, 0, 0))],
        out_specs=[
            pl.BlockSpec((1, d, d), lambda e: (e, 0, 0)),
            pl.BlockSpec((1, 1, d), lambda e: (e, 0, 0)),
        ],
        out_shape=[sds((count, d, d), BF), sds((count, 1, d), F32)],
        compiler_params=params(60),
        cost_estimate=cost(),
    )


def fwd_attn_body(dm, own_len, xv, gain, offset, win, bias, wout, obias, nco, qo, ko, vo, po, x1o, n2o, n2live, ctx_s):
    width = dm.width
    scaled, _ = norm_stats(xv)
    n1 = (scaled * gain[0, 0:1].astype(F32) + offset[0, 0:1].astype(F32)).astype(BF)
    nco[0] = n1[: dm.live]
    w = win.at[0]
    q = (dot(n1, w[:, 0:width]) + bias[0, 0:1].astype(F32)).astype(BF) * 0.125
    q = q.astype(BF)
    k = dot(n1[: dm.keys], w[:, width : 2 * width]).astype(BF)
    v = (dot(n1[: dm.keys], w[:, 2 * width :]) + bias[0, 1:2].astype(F32)).astype(BF)
    qo[...] = q[: dm.live]
    ko[...] = k
    vo[...] = v
    col = lax.broadcasted_iota(jnp.int32, (1, dm.keys), 1)
    valid = (col < PATCHES) | ((col >= dm.text_at) & (col < dm.text_at + own_len))
    low_lane = lax.broadcasted_iota(jnp.int32, (1, 128), 1) < 64
    for pair in range(HEADS // 2):
        lanes = slice(pair * 128, pair * 128 + 128)
        qp, kp, vp = q[:, lanes], k[:, lanes], v[:, lanes]
        outs = []
        for j in range(2):
            qm = jnp.where(low_lane if j == 0 else ~low_lane, qp, jnp.zeros_like(qp))
            scores = jnp.where(valid, dot(qm, kp, NT), FILL)
            top = jnp.max(scores, axis=-1, keepdims=True)
            expo = jnp.exp(scores - top)
            probs = (expo / jnp.sum(expo, axis=-1, keepdims=True)).astype(BF)
            po[2 * pair + j] = probs[: dm.live]
            outs.append(dot(probs, vp))
        ctx_s[:, lanes] = jnp.where(low_lane, outs[0], outs[1]).astype(BF)
    ctx = ctx_s[...]
    nco[1] = ctx[: dm.live]
    x1 = xv + (dot(ctx, wout[0]) + obias[0].astype(F32))
    x1o[...] = x1
    scaled, _ = norm_stats(x1)
    n2 = (scaled * gain[0, 1:2].astype(F32) + offset[0, 1:2].astype(F32)).astype(BF)
    n2o[...] = n2
    n2live[...] = n2[: dm.live]


def fwd_attn_next_body(dm, sc, lens, x, *refs):
    fwd_attn_body(dm, lens[sc[1]], x[...], *refs)


def fwd_attn_first_body(dm, sc, lens, tokens, near, far, *refs):
    stream = sc[1]
    *refs, x0, ctx_s, stage = refs
    put_stage(dm, stage, [tokens[stream], near[0], far[stream & 1], near[1]])
    pick, _ = slot_select(dm, dm.full, stream)
    xv = dot(pick.astype(BF), stage[...])
    x0[...] = xv.astype(BF)
    fwd_attn_body(dm, lens[stream], xv, *refs, ctx_s)


def fwd_attn(dm, layer, sc, lens, inputs, norm_gain, norm_bias, attn_in, attn_bias, attn_out, out_bias, deps=()):
    d, full, live, keys = dm.width, dm.full, dm.live, dm.keys
    shapes = [
        sds((2, live, d), BF),
        sds((live, d), BF),
        sds((keys, d), BF),
        sds((keys, d), BF),
        sds((HEADS, live, keys), BF),
        sds((full, d), F32),
        sds((full, d), BF),
        sds((live, d), BF),
    ]
    scratch = [pltpu.VMEM((full, d), BF)]
    body = fwd_attn_next_body
    if len(inputs) > 1:
        body = fwd_attn_first_body
        shapes.append(sds((full, d), BF))
        scratch.append(pltpu.VMEM((4 * PAD, d), BF))
    return run(
        functools.partial(body, dm),
        (sc, lens, *inputs, norm_gain, norm_bias, hbm(attn_in), attn_bias, hbm(attn_out), out_bias[:, None]),
        deps,
        grid=(1,),
        in_specs=[SMEM, SMEM]
        + [whole(value.shape) for value in inputs]
        + [
            layer_block((2, d), layer),
            layer_block((2, d), layer),
            layer_block((d, 3 * d), layer),
            layer_block((2, d), layer),
            layer_block((d, d), layer),
            layer_block((1, d), layer),
        ],
        out_specs=[whole(s.shape) for s in shapes],
        out_shape=shapes,
        scratch_shapes=scratch,
        compiler_params=params(16),
        cost_estimate=cost(),
    )


def fwd_ff_two_body(dm, n2, x1, wv, wl, bi, wov, wol, bo, slope_v, slope_l, x2, acc):
    t = pl.program_id(0)
    vis, lang, text_at = dm.vis, dm.lang, dm.text_at
    rows_v = lax.broadcasted_iota(jnp.int32, (vis, 1), 0) < text_at
    rows_l = lax.broadcasted_iota(jnp.int32, (dm.full - lang, 1), 0) + lang >= text_at
    act_v, sv = gelu_parts(dot(n2[0:vis], wv[0]) + bi[0, 0:1].astype(F32))
    act_l, sl = gelu_parts(dot(n2[lang:], wl[0]) + bi[1, 0:1].astype(F32))
    slope_v[...] = sv.astype(BF)
    slope_l[...] = sl[: dm.live - lang].astype(BF)
    part_v = dot(act_v.astype(BF), wov[0])
    part_l = dot(act_l.astype(BF), wol[0])

    @pl.when(t == 0)
    def _():
        acc[...] = x1[...]
        part_vb = part_v + bo[0, 0:1].astype(F32)
        part_lb = part_l + bo[1, 0:1].astype(F32)
        acc[0:vis] += jnp.where(rows_v, part_vb, 0.0)
        acc[lang:] += jnp.where(rows_l, part_lb, 0.0)

    @pl.when(t > 0)
    def _():
        acc[0:vis] += jnp.where(rows_v, part_v, 0.0)
        acc[lang:] += jnp.where(rows_l, part_l, 0.0)

    @pl.when(t == pl.num_programs(0) - 1)
    def _():
        x2[...] = acc[...]


def fwd_ff_two(dm, n2, x1, ffn_in, ffn_in_bias, ffn_out, ffn_out_bias, deps=()):
    d, full, hid = dm.width, dm.full, dm.hidden
    count = ffn_in.shape[0]
    return run(
        functools.partial(fwd_ff_two_body, dm),
        (n2, x1, hbm(ffn_in), hbm(ffn_in), ffn_in_bias[:, None], hbm(ffn_out), hbm(ffn_out), ffn_out_bias[:, None]),
        deps,
        grid=(hid // TILE,),
        in_specs=[
            whole((full, d)),
            whole((full, d)),
            pl.BlockSpec((1, d, TILE), lambda t: (0, 0, t)),
            pl.BlockSpec((1, d, TILE), lambda t: (1, 0, t)),
            pl.BlockSpec((count, 1, TILE), lambda t: (0, 0, t)),
            pl.BlockSpec((1, TILE, d), lambda t: (0, t, 0)),
            pl.BlockSpec((1, TILE, d), lambda t: (1, t, 0)),
            whole((count, 1, d)),
        ],
        out_specs=[
            pl.BlockSpec((dm.vis, TILE), lambda t: (0, t)),
            pl.BlockSpec((dm.live - dm.lang, TILE), lambda t: (0, t)),
            whole((full, d)),
        ],
        out_shape=[sds((dm.vis, hid), BF), sds((dm.live - dm.lang, hid), BF), sds((full, d), F32)],
        scratch_shapes=[pltpu.VMEM((full, d), F32)],
        compiler_params=params(36),
        cost_estimate=cost(),
    )


def finish_ff_back(dm, g, gn, x1, gain, go, ga, sums):
    grad_in, gain_sum, offset_sum = norm_back(gn, x1[0 : dm.live], gain[0, 1:2].astype(F32))
    out = g + grad_in
    go[...] = out
    low = out.astype(BF)
    ga[...] = low
    sums[0:1] = gain_sum
    sums[1:2] = offset_sum
    sums[2:3] = jnp.sum(low.astype(F32), axis=0, keepdims=True)


def top_ff_body(dm, sc, n2, gf, x1, gain, wi, bi, wo, bo, mix, go, ga, sums, hsum, accm, accg):
    t = pl.program_id(0)
    act, slope = gelu_parts(dot(n2[...], wi[0]) + bi[0].astype(F32))
    gpre = (dot(gf[0], wo[0], NT) * slope[: dm.live]).astype(BF)
    hsum[...] = jnp.sum(gpre.astype(F32), axis=0, keepdims=True)
    part = dot(act.astype(BF), wo[0])
    back = dot(gpre, wi[0], NT)

    @pl.when(t == 0)
    def _():
        accm[...] = part + (x1[...] + bo[0].astype(F32))
        accg[...] = back

    @pl.when(t > 0)
    def _():
        accm[...] += part
        accg[...] += back

    @pl.when(t == pl.num_programs(0) - 1)
    def _():
        split_shards(dm, accm[...].astype(BF), sc[1], [mix.at[r] for r in range(4)])
        g = gf[0].astype(F32)
        sums[3:4] = jnp.sum(g, axis=0, keepdims=True)
        finish_ff_back(dm, g, accg[...], x1, gain, go, ga, sums)


def top_ff(dm, layer, expert, sc, n2, gf, x1, norm_gain, ffn_in, ffn_in_bias, ffn_out, ffn_out_bias, deps=()):
    d, full, live, hid, slots = dm.width, dm.full, dm.live, dm.hidden, dm.slots
    shapes = [
        sds((4, slots, d), BF),
        sds((live, d), F32),
        sds((live, d), BF),
        sds((4, d), F32),
    ]
    return run(
        functools.partial(top_ff_body, dm),
        (sc, n2, gf, x1, norm_gain, hbm(ffn_in), ffn_in_bias[:, None], hbm(ffn_out), ffn_out_bias[:, None]),
        deps,
        grid=(hid // TILE,),
        in_specs=[
            SMEM,
            whole((full, d)),
            layer_block((live, d), 0),
            whole((full, d)),
            layer_block((2, d), layer),
            pl.BlockSpec((1, d, TILE), lambda t: (expert, 0, t)),
            pl.BlockSpec((1, 1, TILE), lambda t: (expert, 0, t)),
            pl.BlockSpec((1, TILE, d), lambda t: (expert, t, 0)),
            layer_block((1, d), expert),
        ],
        out_specs=[whole(s.shape) for s in shapes] + [pl.BlockSpec((1, TILE), lambda t: (0, t))],
        out_shape=shapes + [sds((1, hid), F32)],
        scratch_shapes=[pltpu.VMEM((full, d), F32), pltpu.VMEM((live, d), F32)],
        compiler_params=params(36),
        cost_estimate=cost(),
    )


def back_ff_two_body(dm, g, gf, x1, gain, slv, sll, wov, wol, wv, wl, go, ga, sums, hsum, acc):
    t = pl.program_id(0)
    vis, lang, text_at, live = dm.vis, dm.lang, dm.text_at, dm.live
    rows_v = lax.broadcasted_iota(jnp.int32, (vis, 1), 0) < text_at
    rows_l = lax.broadcasted_iota(jnp.int32, (live - lang, 1), 0) + lang >= text_at
    gv = jnp.where(rows_v, gf[0:vis].astype(F32), 0.0)
    gl = jnp.where(rows_l, gf[lang:].astype(F32), 0.0)
    pre_v = (dot(gv.astype(BF), wov[0], NT) * slv[...].astype(F32)).astype(BF)
    pre_l = (dot(gl.astype(BF), wol[0], NT) * sll[...].astype(F32)).astype(BF)
    hsum[0:1] = jnp.sum(pre_v.astype(F32), axis=0, keepdims=True)
    hsum[1:2] = jnp.sum(pre_l.astype(F32), axis=0, keepdims=True)
    part_v = dot(pre_v, wv[0], NT)
    part_l = dot(pre_l, wl[0], NT)

    @pl.when(t == 0)
    def _():
        acc[...] = jnp.zeros_like(acc)

    acc[0:vis] += part_v
    acc[lang:] += part_l

    @pl.when(t == pl.num_programs(0) - 1)
    def _():
        sums[3:4] = jnp.sum(gv, axis=0, keepdims=True)
        sums[4:5] = jnp.sum(gl, axis=0, keepdims=True)
        finish_ff_back(dm, g[...], acc[...], x1, gain, go, ga, sums)


def back_ff_two(dm, layer, g, gf, x1, norm_gain, slope_v, slope_l, ffn_in, ffn_out, deps=()):
    d, live, hid = dm.width, dm.live, dm.hidden
    return run(
        functools.partial(back_ff_two_body, dm),
        (g, gf, x1, norm_gain, slope_v, slope_l, hbm(ffn_out), hbm(ffn_out), hbm(ffn_in), hbm(ffn_in)),
        deps,
        grid=(hid // TILE,),
        in_specs=[
            whole((live, d)),
            whole((live, d)),
            whole((dm.full, d)),
            layer_block((2, d), layer),
            pl.BlockSpec((dm.vis, TILE), lambda t: (0, t)),
            pl.BlockSpec((live - dm.lang, TILE), lambda t: (0, t)),
            pl.BlockSpec((1, TILE, d), lambda t: (0, t, 0)),
            pl.BlockSpec((1, TILE, d), lambda t: (1, t, 0)),
            pl.BlockSpec((1, d, TILE), lambda t: (0, 0, t)),
            pl.BlockSpec((1, d, TILE), lambda t: (1, 0, t)),
        ],
        out_specs=[
            whole((live, d)),
            whole((live, d)),
            whole((5, d)),
            pl.BlockSpec((2, TILE), lambda t: (0, t)),
        ],
        out_shape=[sds((live, d), F32), sds((live, d), BF), sds((5, d), F32), sds((2, hid), F32)],
        scratch_shapes=[pltpu.VMEM((live, d), F32)],
        compiler_params=params(36),
        cost_estimate=cost(),
    )


def back_attn_body(dm, bottom, sc, g, ga, q, k, v, p, x, gain, win, wout, *refs):
    width, live = dm.width, dm.live
    *refs, parts = refs
    mine, other_near, other_far, sums, *outs = refs[1:] if bottom else refs
    gc = dot(ga[...], wout[0], NT).astype(BF)
    low_lane = lax.broadcasted_iota(jnp.int32, (1, 128), 1) < 64
    for pair in range(HEADS // 2):
        lanes = slice(pair * 128, pair * 128 + 128)
        gp, qp, kp, vp = gc[:, lanes], q[:, lanes], k[:, lanes], v[:, lanes]
        dqs, dks, dvs = [], [], []
        for j in range(2):
            gm = jnp.where(low_lane if j == 0 else ~low_lane, gp, jnp.zeros_like(gp))
            dprob = dot(gm, vp, NT)
            prob_low = p[2 * pair + j]
            prob = prob_low.astype(F32)
            inner = jnp.sum(prob * dprob, axis=-1, keepdims=True)
            ds = (prob * (dprob - inner)).astype(BF)
            dqs.append(dot(ds, kp))
            dks.append(dot(ds, qp, TN))
            dvs.append(dot(prob_low, gp, TN))
        dq = jnp.where(low_lane, dqs[0], dqs[1]) * 0.125
        dk = jnp.where(low_lane, dks[0], dks[1])
        dv = jnp.where(low_lane, dvs[0], dvs[1])
        parts[0, :, lanes] = dq.astype(BF)
        parts[1, :, lanes] = dk[:live].astype(BF)
        parts[2, :, lanes] = dv[:live].astype(BF)
    parts[3] = ga[...]
    mine[0] = parts[sc[1]]
    mine[1] = parts[sc[1] ^ 2]
    other_near[...] = parts[sc[1] ^ 1]
    other_far[...] = parts[sc[1] ^ 3]
    gn = sum(dot(parts[k], win[0, :, k * width : (k + 1) * width], NT) for k in range(3))
    grad_in, gain_sum, offset_sum = norm_back(gn, x[0:live].astype(F32), gain[0, 0:1].astype(F32))
    out = g[...] + grad_in
    if bottom:
        own, near, far = outs
        split_shards(dm, out.astype(BF), sc[1], (own.at[1], near.at[1], far.at[2], far.at[3]))
        for r, ref in enumerate((own.at[0], near.at[0], far.at[0], far.at[1])):
            ref[...] = refs[0][r]
    else:
        outs[0][...] = out
        outs[1][...] = out.astype(BF)
    sums[0:1] = gain_sum
    sums[1:2] = offset_sum
    sums[2:3] = jnp.sum(parts[0].astype(F32), axis=0, keepdims=True)
    sums[3:4] = jnp.sum(parts[2].astype(F32), axis=0, keepdims=True)


def back_attn(dm, layer, sc, g, ga, q, k, v, p, x, norm_gain, attn_in, attn_out, mix=None, deps=()):
    d, live, keys, slots = dm.width, dm.live, dm.keys, dm.slots
    bottom = layer == 0
    shapes = [sds((2, live, d), BF), sds((live, d), BF), sds((live, d), BF), sds((4, d), F32)]
    if bottom:
        shapes += [sds((2, slots, d), BF), sds((2, slots, d), BF), sds((4, slots, d), BF)]
    else:
        shapes += [sds((live, d), F32), sds((live, d), BF)]
    return run(
        functools.partial(back_attn_body, dm, bottom),
        (sc, g, ga, q, k, v, p, x, norm_gain, hbm(attn_in), hbm(attn_out)) + ((mix,) if bottom else ()),
        deps,
        grid=(1,),
        in_specs=[
            SMEM,
            whole((live, d)),
            whole((live, d)),
            whole((live, d)),
            whole((keys, d)),
            whole((keys, d)),
            whole((HEADS, live, keys)),
            whole((dm.full, d)),
            layer_block((2, d), layer),
            layer_block((d, 3 * d), layer),
            layer_block((d, d), layer),
        ]
        + ([whole(mix.shape)] if bottom else []),
        out_specs=[whole(s.shape) for s in shapes],
        out_shape=shapes,
        scratch_shapes=[pltpu.VMEM((4, live, d), BF)],
        compiler_params=params(16),
        cost_estimate=cost(),
    )


def store_shares(dm, refs, row, value, order, flip, stage):
    keep, send = refs
    n, share = dm.item_devs, dm.share
    half = n // 2
    for i in range(n):
        stage[i] = value[i * share : (i + 1) * share]
    for p in range(n):
        ref = keep if p < half else send
        index = unplace(dm, p ^ flip, order)
        ref[p % half, row : row + share] = stage[index]


def unplace(dm, place, order):
    out = place * 0
    for k, bit in enumerate(order):
        out = out | (((place >> (dm.bits - 1 - k)) & 1) << bit)
    return out


def wgrad_attn_body(dm, sc, nc, nc_near, mine, got_near, got_far, keep, send, left, right):
    n, live = dm.item_devs, dm.live
    for k, (got, ref) in enumerate(((got_near, keep), (got_far, send))):
        side = jnp.where((sc[1] ^ (2 * k)) == 3, 1, 0)
        left[0:live] = nc[side]
        left[live:] = nc_near[side]
        right[0:live] = mine[k]
        right[live:] = got[...]
        value = dot(left[...], right[...], TN).astype(BF)
        if dm.tiled:
            for i in range(n):
                ref[dm.place(i, dm.order_a) ^ sc[2]] = value[i * dm.share : (i + 1) * dm.share]
        else:
            ref[...] = value


def wgrad_attn(dm, sc, nc, nc_near, mine, got_near, got_far, deps=()):
    d, live, n, share = dm.width, dm.live, dm.item_devs, dm.share
    shape = (n, share, d) if dm.tiled else (d, d)
    args = (sc, nc, nc_near, mine, got_near, got_far)
    return run(
        functools.partial(wgrad_attn_body, dm),
        args,
        deps,
        grid=(1,),
        in_specs=[SMEM] + [whole(value.shape) for value in args[1:]],
        out_specs=[whole(shape)] * 2,
        out_shape=[sds(shape, BF)] * 2,
        scratch_shapes=[pltpu.VMEM((2 * live, d), BF)] * 2,
        compiler_params=params(12),
        cost_estimate=cost(),
    )


def ff_layout(dm, experts):
    rows, where = [], {}
    for index, (*_, orders) in enumerate(experts):
        for side in range(2):
            if side and orders[0] is orders[1] and dm.tiled:
                rows[-1] += dm.share
            else:
                rows.append(dm.share)
            where[index, side] = (len(rows) - 1, rows[-1] - dm.share)
    return rows, where


def wgrad_ff_body(dm, experts, stacked, sc, *refs):
    d, streams = dm.width, dm.streams
    n2s = refs[0:streams]
    gfs, refs = ([refs[streams].at[r] for r in range(streams)], refs[streams + 1 :]) if stacked else (refs[streams : 2 * streams], refs[2 * streams :])
    count = len(experts)
    wi, wo, bi = refs[:3]
    outs = refs[3:-5]
    n2a, gfa, acta, gpa, stage = refs[-5:]
    _, where = ff_layout(dm, experts)
    for index, (expert, start, stop, low, high, orders) in enumerate(experts):
        size = stop - start
        total = size * streams
        rows = first((size, 1)) + start
        keep = (rows >= low) & (rows < high)
        for r in range(streams):
            n2a[r * size : (r + 1) * size] = n2s[r][start:stop]
            gpart = gfs[r][start:stop]
            if low > start or high < stop:
                gpart = jnp.where(keep, gpart.astype(F32), 0.0).astype(BF)
            gfa[r * size : (r + 1) * size] = gpart
        chunk = size if size >= 128 else total
        wi_e = wi.at[index]
        wo_e = wo[index].reshape(d, d)

        def step(c, carry, chunk=chunk, wi_e=wi_e, wo_e=wo_e, index=index):
            at = pl.ds(pl.multiple_of(c * chunk, 16), chunk)
            act, slope = gelu_parts(dot(n2a[at], wi_e[...]) + bi[index])
            acta[at] = act.astype(BF)
            gpa[at] = (dot(gfa[at], wo_e, NT) * slope).astype(BF)
            return carry

        lax.fori_loop(0, total // chunk, step, 0)
        for side, (left, right) in enumerate(((n2a, gpa), (acta, gfa))):
            value = dot(left[0:total], right[0:total], TN).astype(BF)
            pair, row = where[index, side]
            if not dm.tiled:
                outs[pair][...] = value
                continue
            store_shares(dm, outs[2 * pair : 2 * pair + 2], row, value, orders[side], sc[2] if orders[side] == dm.order_a else sc[3], stage)


def wgrad_ff(dm, experts, sc, n2s, gfs, wi, wo, bi, deps=()):
    d, live, n, share, streams = dm.width, dm.live, dm.item_devs, dm.share, dm.streams
    count = len(experts)
    base = experts[0][0]
    part = d // n
    stacked = len(gfs) == 1
    pair_rows, _ = ff_layout(dm, experts)
    shapes = [(n // 2, rows, d) for rows in pair_rows for _ in range(2)] if dm.tiled else [(d, d)] * len(pair_rows)
    top = max(e[2] - e[1] for e in experts) * streams
    if dm.tiled:
        wo = wo.reshape(wo.shape[0], n, streams, part, d)
        wo_spec = pl.BlockSpec((count, n, None, part, d), lambda t, s: (base // count, 0, s[1], 0, 0), pipeline_mode=ONCE)
    else:
        wo_spec = pl.BlockSpec((count, d, d), lambda t, s: (base // count, 0, 0), pipeline_mode=ONCE)

    body = functools.partial(wgrad_ff_body, dm, experts, stacked)
    deps = order_after(deps)
    extra = len(deps)
    args = (*n2s, *gfs, wi, hbm(wo), bi)
    number = len(shapes)

    def wrapped(*refs):
        outs = refs[1 + len(args) + extra :]
        outs[number][...] = jnp.zeros_like(outs[number])
        body(*refs[: 1 + len(args)], *outs[:number], *outs[number + 1 :])

    gf_specs = [pl.BlockSpec((streams, live, d), lambda t, s: (0, 0, 0), pipeline_mode=ONCE)] if stacked else [pl.BlockSpec((live, d), lambda t, s: (0, 0), pipeline_mode=ONCE)] * streams
    *outs, token = pl.pallas_call(
        wrapped,
        grid_spec=pltpu.PrefetchScalarGridSpec(
            num_scalar_prefetch=1,
            grid=(1,),
            in_specs=[pl.BlockSpec((live, d), lambda t, s: (0, 0), pipeline_mode=ONCE)] * streams
            + gf_specs
            + [
                pl.BlockSpec((count, d, d), lambda t, s: (base // count, 0, 0), pipeline_mode=ONCE),
                wo_spec,
                pl.BlockSpec((count, 1, d), lambda t, s: (base // count, 0, 0), pipeline_mode=ONCE),
            ]
            + [ANY] * extra,
            out_specs=[pl.BlockSpec(shape, lambda t, s, shape=shape: (0,) * len(shape), pipeline_mode=ONCE) for shape in [*shapes, (8, 128)]],
            scratch_shapes=[pltpu.VMEM((top, d), BF)] * 4 + [pltpu.VMEM((n, share, d), BF)],
        ),
        out_shape=[sds(shape, BF) for shape in shapes] + [sds((8, 128), F32)],
        compiler_params=params(24),
        cost_estimate=cost(),
        name="wgrad_ff_body",
    )(sc, *args, *deps)
    note(outs, token)
    return outs


def finish_body(dm, sc, *refs):
    *pieces, first_out, second_out, stage = refs
    share, part = dm.share, dm.hidden // (dm.item_devs * dm.streams)
    expert = len(pieces) == 8
    for k, piece in enumerate(pieces):
        stage[k // 4, sc[1] ^ (k % 4)] = piece[...]
    if expert:
        for i in range(dm.item_devs):
            block = [stage[0, q, :, i * part : (i + 1) * part].astype(F32) for q in range(4)]
            first_out[0, :, i * 4 * part : (i + 1) * 4 * part] = jnp.concatenate(block, axis=1)
        for q in range(4):
            second_out[0, q * share : (q + 1) * share] = stage[1, q].astype(F32)
    else:
        for q in range(3):
            first_out[0, :, q * dm.width : (q + 1) * dm.width] = stage[0, q].astype(F32)
        second_out[0] = stage[0, 3].astype(F32)


def finish(dm, sc, sources, index, bases, *deps):
    share, d, hid = dm.share, dm.width, dm.hidden
    expert = len(sources) == 2
    if expert:
        shapes = [(3, share, hid), (3, 4 * share, d)]
    else:
        shapes = [(2, share, 3 * d), (2, share, d)]
    args, specs = [sc], [SMEM]
    for arrays, block in sources:
        args += arrays
        if dm.tiled:
            specs += [pl.BlockSpec((share, d), lambda t, block=block: (block, 0), pipeline_mode=ONCE)] * 4
        else:
            args[-4:] = [value[block * share : (block + 1) * share] for value in arrays]
            specs += [whole((share, d))] * 4
    deps = order_after(deps)
    count, extra = len(args), len(bases)

    def body(*refs):
        outs = refs[count + extra + len(deps) :]
        outs[2][...] = jnp.zeros_like(outs[2])
        finish_body(dm, *refs[:count], *outs[:2], outs[3])

    *outs, token = pl.pallas_call(
        body,
        grid=(1,),
        in_specs=specs + [pl.BlockSpec(memory_space=pltpu.HBM)] * extra + [ANY] * len(deps),
        out_specs=[
            pl.BlockSpec((1,) + shape[1:], lambda t: (index, 0, 0), pipeline_mode=ONCE) for shape in shapes
        ]
        + [whole((8, 128))],
        out_shape=[pltpu.HBM(shape, F32) for shape in shapes] + [sds((8, 128), F32)],
        scratch_shapes=[pltpu.VMEM((len(sources), 4, share, d), BF)],
        input_output_aliases={count + k: k for k in range(extra)},
        compiler_params=params(12),
        cost_estimate=cost(),
        name="finish_body",
    )(*args, *bases, *deps)
    note(outs, token)
    return outs


SMALL_ROWS = 32


def small_body(dm, sc, a0, a1, f0, f1, h0, h1, out):
    out[...] = jnp.zeros_like(out)
    share = dm.share
    wide = jnp.concatenate(
        [
            a0[2:4], a1[2:4],
            f0[2:3], f1[2:3],
            a0[0:1], f0[0:1], a1[0:1], f1[0:1],
            a0[1:2], f0[1:2], a1[1:2], f1[1:2],
            f0[3:5], f1[3:4],
        ],
        axis=0,
    )
    hidden = jnp.concatenate([h0[...], h1[...]], axis=0)
    count = wide.shape[0]
    for i in range(dm.item_devs):
        place = dm.place(i, dm.order_a) ^ sc[2]
        out[place, 0:count, 0:share] = wide[:, i * share : (i + 1) * share]
        for q in range(4):
            at = (i * 4 + q) * share
            out[place, count + 3 * q : count + 3 * q + 3, 0:share] = hidden[:, at : at + share]


def small_pack(dm, sc, values, deps):
    shape = (dm.item_devs, SMALL_ROWS, 128)
    return run(
        functools.partial(small_body, dm),
        (sc, *values),
        deps,
        grid=(1,),
        in_specs=[SMEM] + [whole(value.shape) for value in values],
        out_specs=whole(shape),
        out_shape=sds(shape, F32),
        compiler_params=params(8),
        cost_estimate=cost(),
    )


def small_out_body(dm, near, far, attn_bias, out_bias, gain, offset, hidden, ffn_bias):
    share = dm.share
    total = near[:, 0:share] + far[:, 0:share]
    for l in range(2):
        attn_bias[l] = total[2 * l : 2 * l + 2]
        gain[l] = total[6 + 2 * l : 8 + 2 * l]
        offset[l] = total[10 + 2 * l : 12 + 2 * l]
    out_bias[...] = total[4:6]
    ffn_bias[...] = total[14:17]
    hidden[...] = jnp.concatenate([total[17 + 3 * q : 20 + 3 * q] for q in range(4)], axis=1)


def small_unpack(dm, near, far, *deps):
    share = dm.share
    shapes = [(2, 2, share), (2, share), (2, 2, share), (2, 2, share), (3, 4 * share), (3, share)]
    return run(
        functools.partial(small_out_body, dm),
        (near, far),
        deps,
        grid=(1,),
        in_specs=[whole(near.shape)] * 2,
        out_specs=[whole(shape) for shape in shapes],
        out_shape=[sds(shape, F32) for shape in shapes],
        compiler_params=params(8),
        cost_estimate=cost(),
    )


def swap(value, axis, bit):
    size = lax.axis_size(axis)
    return lax.ppermute(value, axis, [(i, i ^ bit) for i in range(size)])


def by_index(blocks, index):
    return lax.dynamic_index_in_dim(blocks, index, 0, keepdims=False)


def gather_start(value):
    return [value, swap(value, "stream", 1), swap(value, "stream", 2)]


def gather_end(parts, *later):
    far = after(parts[2], *later) if later else parts[2]
    return parts + [swap(far, "stream", 1)]


def gather_rel(value):
    return gather_end(gather_start(value))


def after(value, *others):
    return lax.optimization_barrier((value, *others))[0]


def add_up(values):
    total = values[0].astype(F32)
    for value in values[1:]:
        total = total + value.astype(F32)
    return total


def add_body(count, *refs):
    refs[count][...] = add_up([ref[...] for ref in refs[:count]]).astype(refs[count].dtype)


def add_part(terms, size, index, deps=()):
    shape = (size,) + terms[0].shape[1:]
    return run(
        functools.partial(add_body, len(terms)),
        terms,
        deps,
        grid=(1,),
        in_specs=[pl.BlockSpec(shape, lambda t: (index, 0, 0))] * len(terms),
        out_specs=whole(shape),
        out_shape=sds(shape, terms[0].dtype),
        compiler_params=params(8),
        cost_estimate=cost(),
    )


def pieces_body(counts, *refs):
    out = refs[-1]
    row = at = 0
    for count in counts:
        terms = refs[at : at + count]
        rows = terms[0].shape[1]
        out[row : row + rows] = add_up([term[0] for term in terms]).astype(out.dtype)
        at += count
        row += rows


def add_pieces(sums, deps=()):
    terms = [term for value in sums for term in value.terms]
    rows = sum(value.terms[0].shape[1] for value in sums)
    shape = (rows, terms[0].shape[2])
    return run(
        functools.partial(pieces_body, [len(value.terms) for value in sums]),
        terms,
        deps,
        grid=(1,),
        in_specs=[pl.BlockSpec((1,) + term.shape[1:], lambda t: (0, 0, 0)) for term in terms],
        out_specs=whole(shape),
        out_shape=sds(shape, terms[0].dtype),
        compiler_params=params(8),
        cost_estimate=cost(),
    )


class Halving:
    def __init__(self, order, terms, size, send=None, deps=()):
        self.order = list(order)
        self.terms = list(terms)
        self.size = size
        if send is None:
            self.more(deps)
        else:
            self.send(send)

    def send(self, value):
        self.size //= 2
        self.last = value
        self.terms.append(swap(value, "items", 1 << self.order.pop(0)))

    def more(self, deps=()):
        if self.order:
            self.send(add_part(self.terms, self.size // 2, 1, deps))
        return self.last

    def drain(self):
        while self.order:
            self.more()
        return self


def per_device(
    tokens,
    cotangent,
    text_len,
    attn_in,
    attn_bias,
    attn_out,
    out_bias,
    norm_gain,
    norm_bias,
    ffn_in,
    ffn_in_bias,
    ffn_out,
    ffn_out_bias,
):
    streams = lax.axis_size("stream")
    item_devs = lax.axis_size("items")
    stream = lax.axis_index("stream")
    item = lax.axis_index("items")
    _, slots, width = tokens.shape
    hidden = ffn_in.shape[2]
    dm = Dims(slots, streams, width, hidden, item_devs)
    share = dm.share
    sc = jnp.stack([stream * 0, stream, dm.place(item, dm.order_a), dm.place(item, dm.order_b)]).astype(jnp.int32)

    part = hidden // (item_devs * streams)
    if dm.tiled:
        wi_q, bi_q = select_quarter(dm, sc, ffn_in, ffn_in_bias)
        wo_q = ffn_out
    else:
        wi_q = by_index(jnp.moveaxis(ffn_in.reshape(3, width, item_devs, streams, part), 3, 0), stream).reshape(3, width, width)
        wo_q = by_index(jnp.moveaxis(ffn_out.reshape(3, item_devs, streams, part, width), 2, 0), stream).reshape(3, width, width)
        bi_q = by_index(jnp.moveaxis(ffn_in_bias.reshape(3, item_devs, streams, part), 2, 0), stream).reshape(3, 1, width).astype(F32)

    far = swap(lax.dynamic_slice_in_dim(tokens, 2 * (1 - stream // 2), 2, 0), "stream", 2)
    far = after(far, bi_q)
    near = swap(jnp.stack([by_index(tokens, stream ^ 1), by_index(far, 1 - stream % 2)]), "stream", 1)
    cots = gather_start(after(cotangent, near))

    layer_params = (norm_gain, norm_bias, attn_in, attn_bias, attn_out, out_bias)
    a0 = fwd_attn(dm, 0, sc, text_len, (tokens, near, far), *layer_params)
    nc_0, q_0, k_0, v_0, p_0, x1_0, n2_0, n2l_0, x_0 = a0
    nc_near_0 = swap(nc_0, "stream", 1)
    n2_all_0 = gather_start(n2l_0)
    sv_0, sl_0, x_1 = fwd_ff_two(dm, n2_0, x1_0, ffn_in, ffn_in_bias, ffn_out, ffn_out_bias)
    cots = gather_end(cots, sv_0)
    n2_all_0 = gather_end(n2_all_0, sv_0)
    a1 = fwd_attn(dm, 1, sc, text_len, (x_1,), *layer_params)
    nc_1, q_1, k_1, v_1, p_1, x1_1, n2_1, n2l_1 = a1
    nc_near_1 = swap(nc_1, "stream", 1)
    n2_all_1 = gather_start(n2l_1)
    gf_all_1 = cot_prep(dm, sc, text_len, cots, (n2l_1, n2_all_0[3]))
    mix, g, ga_1, fs_1, hs_1 = top_ff(
        dm, 1, 2, sc, n2_1, gf_all_1, x1_1, norm_gain, ffn_in, ffn_in_bias, ffn_out, ffn_out_bias
    )
    n2_all_1 = gather_end(n2_all_1, fs_1)

    live, vis, lang, text_at = dm.live, dm.vis, dm.lang, dm.text_at
    half = item_devs // 2
    a, b = dm.order_a, dm.order_b

    def reorder(value, order):
        places = jnp.stack([dm.place(jnp.int32(i), order) for i in range(item_devs)])
        source = jnp.zeros((item_devs,), jnp.int32).at[places ^ dm.place(item, order)].set(jnp.arange(item_devs, dtype=jnp.int32))
        value = value.reshape(value.shape[:-2] + (item_devs, share, width))
        return jnp.take(value, source, axis=value.ndim - 3)

    def pairs(values, experts):
        if dm.tiled:
            return [values[2 * k : 2 * k + 2] for k in range(len(values) // 2)]
        out = []
        for index, (*_, orders) in enumerate(experts):
            sides = [reorder(values[2 * index + side], orders[side]) for side in range(2)]
            if orders[0] is orders[1]:
                sides = [jnp.concatenate(sides, axis=1)]
            out += [(value[:half], value[half:]) for value in sides]
        return out

    def halving(pair, order, *later):
        return Halving(order, [pair[0]], item_devs, after(pair[1], *later) if later else pair[1])

    def attn_sum(keep, send, *later):
        if not dm.tiled:
            keep, send = reorder(keep, a), reorder(send, a)
        return [keep, swap(after(send, *later) if later else send, "stream", 2)]

    experts = ((2, 0, live, 0, live, (a, a)),)
    join = wgrad_ff(dm, experts, sc, n2_all_1, (gf_all_1,), wi_q, wo_q, bi_q, deps=(fs_1,))
    join_sum = halving(pairs(join, experts)[0], a)
    mine_1, near_1, far_1, as_1, g, gf_0 = back_attn(
        dm, 1, sc, g, ga_1, q_1, k_1, v_1, p_1, x_1, norm_gain, attn_in, attn_out, deps=(join[0],)
    )
    gf_all_0 = gather_start(gf_0)
    near_1, far_1 = swap(near_1, "stream", 1), swap(far_1, "stream", 1)
    g, ga_0, fs_0, hs_0 = back_ff_two(dm, 0, g, gf_0, x1_0, norm_gain, sv_0, sl_0, ffn_in, ffn_out)
    gf_all_0 = gather_end(gf_all_0, fs_0)
    att_1 = wgrad_attn(dm, sc, nc_1, nc_near_1, mine_1, near_1, far_1, deps=(fs_0,))
    att_1_terms = attn_sum(*att_1)
    experts = ((0, 0, vis, 0, text_at, (a, list(a))), (1, lang, live, text_at, live, (a, b)))
    last = join_sum.more((att_1[0],))
    two = wgrad_ff(dm, experts, sc, n2_all_0, gf_all_0, wi_q, wo_q, bi_q, deps=(last,))
    va, vb, la, lb = pairs(two, experts)
    va_sum = halving(va, a)
    lb_sum = halving(lb, b)
    last = join_sum.more((two[0],))
    mine_0, near_0, far_0, as_0, tg_own, tg_near, tg_far = back_attn(
        dm, 0, sc, g, ga_0, q_0, k_0, v_0, p_0, x_0, norm_gain, attn_in, attn_out, mix=mix, deps=(last,)
    )
    near_0, far_0 = swap(near_0, "stream", 1), swap(far_0, "stream", 1)
    small = small_pack(dm, sc, (as_0, as_1, fs_0, fs_1, hs_0, hs_1), ())
    last = va_sum.more((small,))
    vb_sum = halving(vb, a, last)
    att_1_sum = Halving(a, att_1_terms, item_devs, deps=(last,))
    last = lb_sum.more((att_1_sum.last,))
    att_0 = wgrad_attn(dm, sc, nc_0, nc_near_0, mine_0, near_0, far_0, deps=(last,))
    att_0_terms = attn_sum(*att_0)
    last = va_sum.more((att_0[0],))
    last = vb_sum.more((last,))
    join_piece = add_pieces([join_sum.drain()], deps=(last,))
    last = vb_sum.more((join_piece,))
    att_0_sum = Halving(a, att_0_terms, item_devs, deps=(last,))
    last = att_1_sum.more((att_0_sum.last,))
    va_piece = add_pieces([va_sum.drain()], deps=(last,))
    last = lb_sum.more((va_piece,))
    la_sum = halving(la, a, last)
    last = att_1_sum.more((last,))
    tg_far = swap(after(tg_far, va_piece), "stream", 2)
    lb_piece = add_pieces([lb_sum.drain()], deps=(last,))
    vb_piece = add_pieces([vb_sum.drain()], deps=(lb_piece,))
    tg_near = swap(jnp.concatenate([tg_near, after(tg_far, vb_piece)[1::2]]), "stream", 1)
    all_1 = gather_start(jnp.concatenate([join_piece, va_piece, vb_piece, lb_piece]))
    last = att_0_sum.more((vb_piece,))
    small_sum = Halving(a, [small[:half]], item_devs, after(small[half:], last))
    att_1_piece = add_pieces([att_1_sum.drain()], deps=(last,))
    last = la_sum.more((att_1_piece,))
    last = att_0_sum.more((last,))
    last = small_sum.more((last,))
    att_0_piece = add_pieces([att_0_sum.drain()], deps=(last,))
    last = la_sum.more((att_0_piece,))
    all_1 = gather_end(all_1, last)
    all_2 = gather_start(after(jnp.concatenate([att_0_piece, att_1_piece]), all_1[2]))
    results = finish(dm, sc, [(all_1, 0), (all_1, 1)], 2, (), last)
    last = small_sum.more((results[0],))
    mixed, tokens_grad = join_shards(dm, sc, tg_own, tg_near, tg_far, last)
    results = finish(dm, sc, [(all_1, 2), (all_1, 3)], 0, results, mixed)
    la_piece = add_pieces([la_sum.drain()], deps=(results[0],))
    all_2 = gather_end(all_2, la_piece)
    all_3 = gather_start(after(la_piece, all_2[2]))
    attn_results = finish(dm, sc, [(all_2, 1)], 1, (), la_piece)
    attn_results = finish(dm, sc, [(all_2, 0)], 0, attn_results)
    small_own = add_pieces([small_sum.drain()], deps=(attn_results[0],))
    small_near = small_own + swap(small_own, "stream", 1)
    small_all = swap(small_near, "stream", 2)
    all_3 = gather_end(all_3, small_own)
    ffn_results = finish(dm, sc, [(all_3, 0), (all_1, 4)], 1, results, small_own)
    outs = small_unpack(dm, small_near, small_all, ffn_results[0])

    return (
        mixed,
        tokens_grad,
        attn_results[0],
        outs[0],
        attn_results[1],
        outs[1],
        outs[2],
        outs[3],
        ffn_results[0],
        outs[4],
        ffn_results[1],
        outs[5],
    )


def solution(mesh):
    return jax.shard_map(
        per_device,
        mesh=mesh,
        in_specs=(
            P("items", "stream", None),
            P("items", "stream", None),
            P("items"),
            P(),
            P(),
            P(),
            P(),
            P(),
            P(),
            P(),
            P(),
            P(),
            P(),
        ),
        out_specs=(
            P("items", "stream", None),
            P("items", "stream", None),
            P(None, "items", None),
            P(None, None, "items"),
            P(None, "items", None),
            P(None, "items"),
            P(None, None, "items"),
            P(None, None, "items"),
            P(None, "items", None),
            P(None, "items"),
            P(None, "items", None),
            P(None, "items"),
        ),
        check_vma=False,
    )
```

```python
import functools
import jax
import jax.numpy as jnp
from jax import lax
from jax.experimental import pallas as pl
from jax.experimental.pallas import tpu as pltpu
from jax.sharding import PartitionSpec as P

HEADS = 12
PATCHES = 197
TEXT = 40
F32 = jnp.float32
BF = jnp.bfloat16
EPS = 1e-06
FILL = -1e30
MIB = 1 << 20
PAD = 80
TILE = 1024


def dot(left, right, dims=((1,), (0,))):
    return lax.dot_general(left, right, (dims, ((), ())), preferred_element_type=F32)


NT = ((1,), (1,))
TN = ((0,), (0,))


def norm_stats(values):
    row_mean = jnp.mean(values, axis=-1, keepdims=True)
    centred = values - row_mean
    row_var = jnp.mean(centred * centred, axis=-1, keepdims=True)
    inv_std = lax.rsqrt(row_var + EPS)
    return centred * inv_std, inv_std


def norm_back(grad_out, values, gain):
    scaled, inv_std = norm_stats(values)
    grad_scaled = grad_out * gain
    mean_first = jnp.mean(grad_scaled, axis=-1, keepdims=True)
    mean_second = jnp.mean(grad_scaled * scaled, axis=-1, keepdims=True)
    grad_in = inv_std * (grad_scaled - mean_first - scaled * mean_second)
    gain_sum = jnp.sum(grad_out * scaled, axis=0, keepdims=True)
    offset_sum = jnp.sum(grad_out, axis=0, keepdims=True)
    return grad_in, gain_sum, offset_sum


def gelu_parts(pre):
    cumulative = 0.5 * (1.0 + lax.erf(pre * 0.7071067811865476))
    density = jnp.exp(-0.5 * pre * pre) * 0.3989422804014327
    return pre * cumulative, cumulative + pre * density


def params(limit_mib):
    return pltpu.CompilerParams(vmem_limit_bytes=limit_mib * MIB)


def cost():
    return pl.CostEstimate(flops=1, bytes_accessed=1, transcendentals=0)


ONCE = pl.Buffered(1)


def whole(shape):
    return pl.BlockSpec(shape, lambda *_: (0,) * len(shape), pipeline_mode=ONCE)


def layer_block(shape, index):
    return pl.BlockSpec((1,) + shape, lambda *_: (index,) + (0,) * len(shape), pipeline_mode=ONCE)


SMEM = pl.BlockSpec(memory_space=pltpu.SMEM)
ANY = pl.BlockSpec(memory_space=pl.ANY)
sds = jax.ShapeDtypeStruct


TOKENS = {}


def order_after(deps):
    return tuple(TOKENS[id(dep)][1] if id(dep) in TOKENS else dep for dep in deps)


def note(outs, token):
    for out in outs:
        TOKENS[id(out)] = (out, token)


def run(body, args, deps=(), *, in_specs, out_specs, out_shape, grid_spec=None, call=None, **rest):
    deps = order_after(deps)
    count, extra = len(args), len(deps)
    single = not isinstance(out_shape, (list, tuple))
    if single:
        out_specs, out_shape = [out_specs], [out_shape]
    number = len(out_shape)

    def wrapped(*refs):
        outs = refs[count + extra :]
        outs[number][...] = jnp.zeros_like(outs[number])
        body(*refs[:count], *outs[:number], *outs[number + 1 :])

    outs = pl.pallas_call(
        wrapped,
        in_specs=list(in_specs) + [ANY] * extra,
        out_specs=list(out_specs) + [whole((8, 128))],
        out_shape=list(out_shape) + [sds((8, 128), F32)],
        name=call or getattr(body, "func", body).__name__,
        **rest,
    )(*args, *deps)
    *outs, token = outs
    note(outs, token)
    return outs[0] if single else outs


def hbm(value):
    return pltpu.with_memory_space_constraint(value, pltpu.HBM)


def first(shape):
    return lax.broadcasted_iota(jnp.int32, shape, 0)


def second(shape):
    return lax.broadcasted_iota(jnp.int32, shape, 1)


class Dims:
    def __init__(self, slots, streams, width, hidden, item_devs):
        self.slots = slots
        self.text_at = slots * (streams - 1)
        self.rows = slots * streams
        self.full = -(-self.rows // 16) * 16
        self.live = -(-(self.text_at + TEXT) // 16) * 16
        self.keys = -(-self.live // 128) * 128
        self.vis = -(-self.text_at // 16) * 16
        self.lang = self.text_at // 16 * 16
        self.width = width
        self.hidden = hidden
        self.streams = streams
        self.item_devs = item_devs
        self.share = width // item_devs
        self.bits = item_devs.bit_length() - 1
        self.order_a = list(range(self.bits))
        self.order_b = self.order_a[1:] + self.order_a[:1]
        self.tiled = self.share % 16 == 0

    def place(self, index, order):
        out = index * 0
        for k, bit in enumerate(order):
            out = out | (((index >> bit) & 1) << (self.bits - 1 - k))
        return out


def put_stage(dm, stage, pieces):
    stage[...] = jnp.zeros_like(stage)
    for r, piece in enumerate(pieces):
        stage[r * PAD : r * PAD + dm.slots] = piece


def slot_select(dm, rows, stream):
    shape = (rows, 4 * PAD)
    slot = first(shape)
    shard = jnp.zeros(shape, jnp.int32)
    for k in range(1, dm.streams):
        shard = shard + (slot >= k * dm.slots).astype(jnp.int32)
    place = slot - shard * dm.slots
    return second(shape) == ((shard ^ stream) * PAD + place), slot


def shard_rows(dm, rows, shard):
    shape = (-(-dm.slots // 8) * 8, rows)
    return ((second(shape) == first(shape) + shard * dm.slots) & (first(shape) < dm.slots)).astype(BF)


def split_shards(dm, value, stream, refs):
    for r, ref in enumerate(refs):
        ref[...] = dot(shard_rows(dm, value.shape[0], stream ^ r), value)[: dm.slots].astype(BF)


def cot_prep_body(dm, sc, lens, c0, c1, c2, c3, out, stage):
    stream = sc[1]
    pick, slot = slot_select(dm, dm.live, stream)
    for r in range(4):
        put_stage(dm, stage, [c[stream ^ r] for c in (c0, c1, c2, c3)])
        alive = (slot < PATCHES) | ((slot >= dm.text_at) & (slot < dm.text_at + lens[stream ^ r]))
        out[r] = dot((pick & alive).astype(BF), stage[...]).astype(BF)


def cot_prep(dm, sc, lens, pieces, deps):
    shape = pieces[0].shape
    return run(
        functools.partial(cot_prep_body, dm),
        (sc, lens, *pieces),
        deps,
        grid=(1,),
        in_specs=[SMEM, SMEM] + [whole(shape)] * 4,
        out_specs=whole((4, dm.live, dm.width)),
        out_shape=sds((4, dm.live, dm.width), BF),
        scratch_shapes=[pltpu.VMEM((4 * PAD, dm.width), BF)],
        compiler_params=params(12),
        cost_estimate=cost(),
    )


def join_shards_body(sc, own, near, far, mixed, grad):
    stream = sc[1]
    for k, out in enumerate((mixed, grad)):
        for r, value in enumerate((own[k], near[k], far[2 * k], near[2 + k])):
            out[stream ^ r] = value.astype(out.dtype)


def join_shards(dm, sc, own, near, far, *deps):
    shape = (4, dm.slots, dm.width)
    return run(
        join_shards_body,
        (sc, own, near, far),
        deps,
        grid=(1,),
        in_specs=[SMEM, whole(own.shape), whole(near.shape), whole(far.shape)],
        out_specs=[whole(shape)] * 2,
        out_shape=[sds(shape, BF), sds(shape, F32)],
        compiler_params=params(8),
        cost_estimate=cost(),
    )


def select_body(dm, sc, *refs):
    *parts, b, wo, bo = refs
    part = dm.hidden // (dm.item_devs * dm.streams)
    rows = parts[0].shape[1]
    for s in range(dm.streams):

        @pl.when(sc[1] == s)
        def _(s=s):
            starts = [i * part * dm.streams + s * part for i in range(dm.item_devs)]
            for k, w in enumerate(parts):
                wo[0, k * rows : (k + 1) * rows] = jnp.concatenate([w[0, :, at : at + part] for at in starts], axis=1)
            bo[0] = jnp.concatenate([b[0, :, at : at + part].astype(F32) for at in starts], axis=1)


def select_quarter(dm, sc, ffn_in, ffn_in_bias):
    d, hid = dm.width, dm.hidden
    count = ffn_in.shape[0]
    pieces = 4
    return run(
        functools.partial(select_body, dm),
        (sc, *[hbm(ffn_in)] * pieces, ffn_in_bias[:, None]),
        grid=(count,),
        in_specs=[SMEM]
        + [pl.BlockSpec((1, d // pieces, hid), lambda e, k=k: (e, k, 0)) for k in range(pieces)]
        + [pl.BlockSpec((1, 1, hid), lambda e: (e, 0, 0))],
        out_specs=[
            pl.BlockSpec((1, d, d), lambda e: (e, 0, 0)),
            pl.BlockSpec((1, 1, d), lambda e: (e, 0, 0)),
        ],
        out_shape=[sds((count, d, d), BF), sds((count, 1, d), F32)],
        compiler_params=params(60),
        cost_estimate=cost(),
    )


def fwd_attn_body(dm, own_len, xv, gain, offset, win, bias, wout, obias, nco, qo, ko, vo, po, x1o, n2o, n2live, ctx_s):
    width = dm.width
    scaled, _ = norm_stats(xv)
    n1 = (scaled * gain[0, 0:1].astype(F32) + offset[0, 0:1].astype(F32)).astype(BF)
    nco[0] = n1[: dm.live]
    w = win.at[0]
    q = (dot(n1, w[:, 0:width]) + bias[0, 0:1].astype(F32)).astype(BF) * 0.125
    q = q.astype(BF)
    k = dot(n1[: dm.keys], w[:, width : 2 * width]).astype(BF)
    v = (dot(n1[: dm.keys], w[:, 2 * width :]) + bias[0, 1:2].astype(F32)).astype(BF)
    qo[...] = q[: dm.live]
    ko[...] = k
    vo[...] = v
    col = lax.broadcasted_iota(jnp.int32, (1, dm.keys), 1)
    valid = (col < PATCHES) | ((col >= dm.text_at) & (col < dm.text_at + own_len))
    low_lane = lax.broadcasted_iota(jnp.int32, (1, 128), 1) < 64
    for pair in range(HEADS // 2):
        lanes = slice(pair * 128, pair * 128 + 128)
        qp, kp, vp = q[:, lanes], k[:, lanes], v[:, lanes]
        outs = []
        for j in range(2):
            qm = jnp.where(low_lane if j == 0 else ~low_lane, qp, jnp.zeros_like(qp))
            scores = jnp.where(valid, dot(qm, kp, NT), FILL)
            top = jnp.max(scores, axis=-1, keepdims=True)
            expo = jnp.exp(scores - top)
            probs = (expo / jnp.sum(expo, axis=-1, keepdims=True)).astype(BF)
            po[2 * pair + j] = probs[: dm.live]
            outs.append(dot(probs, vp))
        ctx_s[:, lanes] = jnp.where(low_lane, outs[0], outs[1]).astype(BF)
    ctx = ctx_s[...]
    nco[1] = ctx[: dm.live]
    x1 = xv + (dot(ctx, wout[0]) + obias[0].astype(F32))
    x1o[...] = x1
    scaled, _ = norm_stats(x1)
    n2 = (scaled * gain[0, 1:2].astype(F32) + offset[0, 1:2].astype(F32)).astype(BF)
    n2o[...] = n2
    n2live[...] = n2[: dm.live]


def fwd_attn_next_body(dm, sc, lens, x, *refs):
    fwd_attn_body(dm, lens[sc[1]], x[...], *refs)


def fwd_attn_first_body(dm, sc, lens, tokens, near, far, *refs):
    stream = sc[1]
    *refs, x0, ctx_s, stage = refs
    put_stage(dm, stage, [tokens[stream], near[0], far[stream & 1], near[1]])
    pick, _ = slot_select(dm, dm.full, stream)
    xv = dot(pick.astype(BF), stage[...])
    x0[...] = xv.astype(BF)
    fwd_attn_body(dm, lens[stream], xv, *refs, ctx_s)


def fwd_attn(dm, layer, sc, lens, inputs, norm_gain, norm_bias, attn_in, attn_bias, attn_out, out_bias, deps=()):
    d, full, live, keys = dm.width, dm.full, dm.live, dm.keys
    shapes = [
        sds((2, live, d), BF),
        sds((live, d), BF),
        sds((keys, d), BF),
        sds((keys, d), BF),
        sds((HEADS, live, keys), BF),
        sds((full, d), F32),
        sds((full, d), BF),
        sds((live, d), BF),
    ]
    scratch = [pltpu.VMEM((full, d), BF)]
    body = fwd_attn_next_body
    if len(inputs) > 1:
        body = fwd_attn_first_body
        shapes.append(sds((full, d), BF))
        scratch.append(pltpu.VMEM((4 * PAD, d), BF))
    return run(
        functools.partial(body, dm),
        (sc, lens, *inputs, norm_gain, norm_bias, hbm(attn_in), attn_bias, hbm(attn_out), out_bias[:, None]),
        deps,
        grid=(1,),
        in_specs=[SMEM, SMEM]
        + [whole(value.shape) for value in inputs]
        + [
            layer_block((2, d), layer),
            layer_block((2, d), layer),
            layer_block((d, 3 * d), layer),
            layer_block((2, d), layer),
            layer_block((d, d), layer),
            layer_block((1, d), layer),
        ],
        out_specs=[whole(s.shape) for s in shapes],
        out_shape=shapes,
        scratch_shapes=scratch,
        compiler_params=params(16),
        cost_estimate=cost(),
    )


def fwd_ff_two_body(dm, n2, x1, wv, wl, bi, wov, wol, bo, slope_v, slope_l, x2, acc):
    t = pl.program_id(0)
    vis, lang, text_at = dm.vis, dm.lang, dm.text_at
    rows_v = lax.broadcasted_iota(jnp.int32, (vis, 1), 0) < text_at
    rows_l = lax.broadcasted_iota(jnp.int32, (dm.full - lang, 1), 0) + lang >= text_at
    act_v, sv = gelu_parts(dot(n2[0:vis], wv[0]) + bi[0, 0:1].astype(F32))
    act_l, sl = gelu_parts(dot(n2[lang:], wl[0]) + bi[1, 0:1].astype(F32))
    slope_v[...] = sv.astype(BF)
    slope_l[...] = sl[: dm.live - lang].astype(BF)
    part_v = dot(act_v.astype(BF), wov[0])
    part_l = dot(act_l.astype(BF), wol[0])

    @pl.when(t == 0)
    def _():
        acc[...] = x1[...]
        part_vb = part_v + bo[0, 0:1].astype(F32)
        part_lb = part_l + bo[1, 0:1].astype(F32)
        acc[0:vis] += jnp.where(rows_v, part_vb, 0.0)
        acc[lang:] += jnp.where(rows_l, part_lb, 0.0)

    @pl.when(t > 0)
    def _():
        acc[0:vis] += jnp.where(rows_v, part_v, 0.0)
        acc[lang:] += jnp.where(rows_l, part_l, 0.0)

    @pl.when(t == pl.num_programs(0) - 1)
    def _():
        x2[...] = acc[...]


def fwd_ff_two(dm, n2, x1, ffn_in, ffn_in_bias, ffn_out, ffn_out_bias, deps=()):
    d, full, hid = dm.width, dm.full, dm.hidden
    count = ffn_in.shape[0]
    return run(
        functools.partial(fwd_ff_two_body, dm),
        (n2, x1, hbm(ffn_in), hbm(ffn_in), ffn_in_bias[:, None], hbm(ffn_out), hbm(ffn_out), ffn_out_bias[:, None]),
        deps,
        grid=(hid // TILE,),
        in_specs=[
            whole((full, d)),
            whole((full, d)),
            pl.BlockSpec((1, d, TILE), lambda t: (0, 0, t)),
            pl.BlockSpec((1, d, TILE), lambda t: (1, 0, t)),
            pl.BlockSpec((count, 1, TILE), lambda t: (0, 0, t)),
            pl.BlockSpec((1, TILE, d), lambda t: (0, t, 0)),
            pl.BlockSpec((1, TILE, d), lambda t: (1, t, 0)),
            whole((count, 1, d)),
        ],
        out_specs=[
            pl.BlockSpec((dm.vis, TILE), lambda t: (0, t)),
            pl.BlockSpec((dm.live - dm.lang, TILE), lambda t: (0, t)),
            whole((full, d)),
        ],
        out_shape=[sds((dm.vis, hid), BF), sds((dm.live - dm.lang, hid), BF), sds((full, d), F32)],
        scratch_shapes=[pltpu.VMEM((full, d), F32)],
        compiler_params=params(36),
        cost_estimate=cost(),
    )


def finish_ff_back(dm, g, gn, x1, gain, go, ga, sums):
    grad_in, gain_sum, offset_sum = norm_back(gn, x1[0 : dm.live], gain[0, 1:2].astype(F32))
    out = g + grad_in
    go[...] = out
    low = out.astype(BF)
    ga[...] = low
    sums[0:1] = gain_sum
    sums[1:2] = offset_sum
    sums[2:3] = jnp.sum(low.astype(F32), axis=0, keepdims=True)


def top_ff_body(dm, sc, n2, gf, x1, gain, wi, bi, wo, bo, mix, go, ga, sums, hsum, accm, accg):
    t = pl.program_id(0)
    act, slope = gelu_parts(dot(n2[...], wi[0]) + bi[0].astype(F32))
    gpre = (dot(gf[0], wo[0], NT) * slope[: dm.live]).astype(BF)
    hsum[...] = jnp.sum(gpre.astype(F32), axis=0, keepdims=True)
    part = dot(act.astype(BF), wo[0])
    back = dot(gpre, wi[0], NT)

    @pl.when(t == 0)
    def _():
        accm[...] = part + (x1[...] + bo[0].astype(F32))
        accg[...] = back

    @pl.when(t > 0)
    def _():
        accm[...] += part
        accg[...] += back

    @pl.when(t == pl.num_programs(0) - 1)
    def _():
        split_shards(dm, accm[...].astype(BF), sc[1], [mix.at[r] for r in range(4)])
        g = gf[0].astype(F32)
        sums[3:4] = jnp.sum(g, axis=0, keepdims=True)
        finish_ff_back(dm, g, accg[...], x1, gain, go, ga, sums)


def top_ff(dm, layer, expert, sc, n2, gf, x1, norm_gain, ffn_in, ffn_in_bias, ffn_out, ffn_out_bias, deps=()):
    d, full, live, hid, slots = dm.width, dm.full, dm.live, dm.hidden, dm.slots
    shapes = [
        sds((4, slots, d), BF),
        sds((live, d), F32),
        sds((live, d), BF),
        sds((4, d), F32),
    ]
    return run(
        functools.partial(top_ff_body, dm),
        (sc, n2, gf, x1, norm_gain, hbm(ffn_in), ffn_in_bias[:, None], hbm(ffn_out), ffn_out_bias[:, None]),
        deps,
        grid=(hid // TILE,),
        in_specs=[
            SMEM,
            whole((full, d)),
            layer_block((live, d), 0),
            whole((full, d)),
            layer_block((2, d), layer),
            pl.BlockSpec((1, d, TILE), lambda t: (expert, 0, t)),
            pl.BlockSpec((1, 1, TILE), lambda t: (expert, 0, t)),
            pl.BlockSpec((1, TILE, d), lambda t: (expert, t, 0)),
            layer_block((1, d), expert),
        ],
        out_specs=[whole(s.shape) for s in shapes] + [pl.BlockSpec((1, TILE), lambda t: (0, t))],
        out_shape=shapes + [sds((1, hid), F32)],
        scratch_shapes=[pltpu.VMEM((full, d), F32), pltpu.VMEM((live, d), F32)],
        compiler_params=params(36),
        cost_estimate=cost(),
    )


def back_ff_two_body(dm, g, gf, x1, gain, slv, sll, wov, wol, wv, wl, go, ga, sums, hsum, acc):
    t = pl.program_id(0)
    vis, lang, text_at, live = dm.vis, dm.lang, dm.text_at, dm.live
    rows_v = lax.broadcasted_iota(jnp.int32, (vis, 1), 0) < text_at
    rows_l = lax.broadcasted_iota(jnp.int32, (live - lang, 1), 0) + lang >= text_at
    gv = jnp.where(rows_v, gf[0:vis].astype(F32), 0.0)
    gl = jnp.where(rows_l, gf[lang:].astype(F32), 0.0)
    pre_v = (dot(gv.astype(BF), wov[0], NT) * slv[...].astype(F32)).astype(BF)
    pre_l = (dot(gl.astype(BF), wol[0], NT) * sll[...].astype(F32)).astype(BF)
    hsum[0:1] = jnp.sum(pre_v.astype(F32), axis=0, keepdims=True)
    hsum[1:2] = jnp.sum(pre_l.astype(F32), axis=0, keepdims=True)
    part_v = dot(pre_v, wv[0], NT)
    part_l = dot(pre_l, wl[0], NT)

    @pl.when(t == 0)
    def _():
        acc[...] = jnp.zeros_like(acc)

    acc[0:vis] += part_v
    acc[lang:] += part_l

    @pl.when(t == pl.num_programs(0) - 1)
    def _():
        sums[3:4] = jnp.sum(gv, axis=0, keepdims=True)
        sums[4:5] = jnp.sum(gl, axis=0, keepdims=True)
        finish_ff_back(dm, g[...], acc[...], x1, gain, go, ga, sums)


def back_ff_two(dm, layer, g, gf, x1, norm_gain, slope_v, slope_l, ffn_in, ffn_out, deps=()):
    d, live, hid = dm.width, dm.live, dm.hidden
    return run(
        functools.partial(back_ff_two_body, dm),
        (g, gf, x1, norm_gain, slope_v, slope_l, hbm(ffn_out), hbm(ffn_out), hbm(ffn_in), hbm(ffn_in)),
        deps,
        grid=(hid // TILE,),
        in_specs=[
            whole((live, d)),
            whole((live, d)),
            whole((dm.full, d)),
            layer_block((2, d), layer),
            pl.BlockSpec((dm.vis, TILE), lambda t: (0, t)),
            pl.BlockSpec((live - dm.lang, TILE), lambda t: (0, t)),
            pl.BlockSpec((1, TILE, d), lambda t: (0, t, 0)),
            pl.BlockSpec((1, TILE, d), lambda t: (1, t, 0)),
            pl.BlockSpec((1, d, TILE), lambda t: (0, 0, t)),
            pl.BlockSpec((1, d, TILE), lambda t: (1, 0, t)),
        ],
        out_specs=[
            whole((live, d)),
            whole((live, d)),
            whole((5, d)),
            pl.BlockSpec((2, TILE), lambda t: (0, t)),
        ],
        out_shape=[sds((live, d), F32), sds((live, d), BF), sds((5, d), F32), sds((2, hid), F32)],
        scratch_shapes=[pltpu.VMEM((live, d), F32)],
        compiler_params=params(36),
        cost_estimate=cost(),
    )


def back_attn_body(dm, bottom, sc, g, ga, q, k, v, p, x, gain, win, wout, *refs):
    width, live = dm.width, dm.live
    *refs, parts = refs
    mine, other_near, other_far, sums, *outs = refs[1:] if bottom else refs
    gc = dot(ga[...], wout[0], NT).astype(BF)
    low_lane = lax.broadcasted_iota(jnp.int32, (1, 128), 1) < 64
    for pair in range(HEADS // 2):
        lanes = slice(pair * 128, pair * 128 + 128)
        gp, qp, kp, vp = gc[:, lanes], q[:, lanes], k[:, lanes], v[:, lanes]
        dqs, dks, dvs = [], [], []
        for j in range(2):
            gm = jnp.where(low_lane if j == 0 else ~low_lane, gp, jnp.zeros_like(gp))
            dprob = dot(gm, vp, NT)
            prob_low = p[2 * pair + j]
            prob = prob_low.astype(F32)
            inner = jnp.sum(prob * dprob, axis=-1, keepdims=True)
            ds = (prob * (dprob - inner)).astype(BF)
            dqs.append(dot(ds, kp))
            dks.append(dot(ds, qp, TN))
            dvs.append(dot(prob_low, gp, TN))
        dq = jnp.where(low_lane, dqs[0], dqs[1]) * 0.125
        dk = jnp.where(low_lane, dks[0], dks[1])
        dv = jnp.where(low_lane, dvs[0], dvs[1])
        parts[0, :, lanes] = dq.astype(BF)
        parts[1, :, lanes] = dk[:live].astype(BF)
        parts[2, :, lanes] = dv[:live].astype(BF)
    parts[3] = ga[...]
    mine[0] = parts[sc[1]]
    mine[1] = parts[sc[1] ^ 2]
    other_near[...] = parts[sc[1] ^ 1]
    other_far[...] = parts[sc[1] ^ 3]
    gn = sum(dot(parts[k], win[0, :, k * width : (k + 1) * width], NT) for k in range(3))
    grad_in, gain_sum, offset_sum = norm_back(gn, x[0:live].astype(F32), gain[0, 0:1].astype(F32))
    out = g[...] + grad_in
    if bottom:
        own, near, far = outs
        split_shards(dm, out.astype(BF), sc[1], (own.at[1], near.at[1], far.at[2], far.at[3]))
        for r, ref in enumerate((own.at[0], near.at[0], far.at[0], far.at[1])):
            ref[...] = refs[0][r]
    else:
        outs[0][...] = out
        outs[1][...] = out.astype(BF)
    sums[0:1] = gain_sum
    sums[1:2] = offset_sum
    sums[2:3] = jnp.sum(parts[0].astype(F32), axis=0, keepdims=True)
    sums[3:4] = jnp.sum(parts[2].astype(F32), axis=0, keepdims=True)


def back_attn(dm, layer, sc, g, ga, q, k, v, p, x, norm_gain, attn_in, attn_out, mix=None, deps=()):
    d, live, keys, slots = dm.width, dm.live, dm.keys, dm.slots
    bottom = layer == 0
    shapes = [sds((2, live, d), BF), sds((live, d), BF), sds((live, d), BF), sds((4, d), F32)]
    if bottom:
        shapes += [sds((2, slots, d), BF), sds((2, slots, d), BF), sds((4, slots, d), BF)]
    else:
        shapes += [sds((live, d), F32), sds((live, d), BF)]
    return run(
        functools.partial(back_attn_body, dm, bottom),
        (sc, g, ga, q, k, v, p, x, norm_gain, hbm(attn_in), hbm(attn_out)) + ((mix,) if bottom else ()),
        deps,
        grid=(1,),
        in_specs=[
            SMEM,
            whole((live, d)),
            whole((live, d)),
            whole((live, d)),
            whole((keys, d)),
            whole((keys, d)),
            whole((HEADS, live, keys)),
            whole((dm.full, d)),
            layer_block((2, d), layer),
            layer_block((d, 3 * d), layer),
            layer_block((d, d), layer),
        ]
        + ([whole(mix.shape)] if bottom else []),
        out_specs=[whole(s.shape) for s in shapes],
        out_shape=shapes,
        scratch_shapes=[pltpu.VMEM((4, live, d), BF)],
        compiler_params=params(16),
        cost_estimate=cost(),
    )


def store_shares(dm, refs, row, value, order, flip, stage):
    keep, send = refs
    n, share = dm.item_devs, dm.share
    half = n // 2
    for i in range(n):
        stage[i] = value[i * share : (i + 1) * share]
    for p in range(n):
        ref = keep if p < half else send
        index = unplace(dm, p ^ flip, order)
        ref[p % half, row : row + share] = stage[index]


def unplace(dm, place, order):
    out = place * 0
    for k, bit in enumerate(order):
        out = out | (((place >> (dm.bits - 1 - k)) & 1) << bit)
    return out


def wgrad_attn_body(dm, sc, nc, nc_near, mine, got_near, got_far, keep, send, left, right):
    n, live = dm.item_devs, dm.live
    for k, (got, ref) in enumerate(((got_near, keep), (got_far, send))):
        side = jnp.where((sc[1] ^ (2 * k)) == 3, 1, 0)
        left[0:live] = nc[side]
        left[live:] = nc_near[side]
        right[0:live] = mine[k]
        right[live:] = got[...]
        value = dot(left[...], right[...], TN).astype(BF)
        if dm.tiled:
            for i in range(n):
                ref[dm.place(i, dm.order_a) ^ sc[2]] = value[i * dm.share : (i + 1) * dm.share]
        else:
            ref[...] = value


def wgrad_attn(dm, sc, nc, nc_near, mine, got_near, got_far, deps=()):
    d, live, n, share = dm.width, dm.live, dm.item_devs, dm.share
    shape = (n, share, d) if dm.tiled else (d, d)
    args = (sc, nc, nc_near, mine, got_near, got_far)
    return run(
        functools.partial(wgrad_attn_body, dm),
        args,
        deps,
        grid=(1,),
        in_specs=[SMEM] + [whole(value.shape) for value in args[1:]],
        out_specs=[whole(shape)] * 2,
        out_shape=[sds(shape, BF)] * 2,
        scratch_shapes=[pltpu.VMEM((2 * live, d), BF)] * 2,
        compiler_params=params(12),
        cost_estimate=cost(),
    )


def ff_layout(dm, experts):
    rows, where = [], {}
    for index, (*_, orders) in enumerate(experts):
        for side in range(2):
            if side and orders[0] is orders[1] and dm.tiled:
                rows[-1] += dm.share
            else:
                rows.append(dm.share)
            where[index, side] = (len(rows) - 1, rows[-1] - dm.share)
    return rows, where


def wgrad_ff_body(dm, experts, stacked, sc, *refs):
    d, streams = dm.width, dm.streams
    n2s = refs[0:streams]
    gfs, refs = ([refs[streams].at[r] for r in range(streams)], refs[streams + 1 :]) if stacked else (refs[streams : 2 * streams], refs[2 * streams :])
    count = len(experts)
    wi, wo, bi = refs[:3]
    outs = refs[3:-5]
    n2a, gfa, acta, gpa, stage = refs[-5:]
    _, where = ff_layout(dm, experts)
    for index, (expert, start, stop, low, high, orders) in enumerate(experts):
        size = stop - start
        total = size * streams
        rows = first((size, 1)) + start
        keep = (rows >= low) & (rows < high)
        for r in range(streams):
            n2a[r * size : (r + 1) * size] = n2s[r][start:stop]
            gpart = gfs[r][start:stop]
            if low > start or high < stop:
                gpart = jnp.where(keep, gpart.astype(F32), 0.0).astype(BF)
            gfa[r * size : (r + 1) * size] = gpart
        chunk = size if size >= 128 else total
        wi_e = wi.at[index]
        wo_e = wo[index].reshape(d, d)

        def step(c, carry, chunk=chunk, wi_e=wi_e, wo_e=wo_e, index=index):
            at = slice(c * chunk, (c + 1) * chunk)
            act, slope = gelu_parts(dot(n2a[at], wi_e[...]) + bi[index])
            acta[at] = act.astype(BF)
            gpa[at] = (dot(gfa[at], wo_e, NT) * slope).astype(BF)
            return carry

        for c in range(total // chunk):
            step(c, 0)
        for side, (left, right) in enumerate(((n2a, gpa), (acta, gfa))):
            value = dot(left[0:total], right[0:total], TN).astype(BF)
            pair, row = where[index, side]
            if not dm.tiled:
                outs[pair][...] = value
                continue
            store_shares(dm, outs[2 * pair : 2 * pair + 2], row, value, orders[side], sc[2] if orders[side] == dm.order_a else sc[3], stage)


def wgrad_ff(dm, experts, sc, n2s, gfs, wi, wo, bi, deps=()):
    d, live, n, share, streams = dm.width, dm.live, dm.item_devs, dm.share, dm.streams
    count = len(experts)
    base = experts[0][0]
    part = d // n
    stacked = len(gfs) == 1
    pair_rows, _ = ff_layout(dm, experts)
    shapes = [(n // 2, rows, d) for rows in pair_rows for _ in range(2)] if dm.tiled else [(d, d)] * len(pair_rows)
    top = max(e[2] - e[1] for e in experts) * streams
    if dm.tiled:
        wo = wo.reshape(wo.shape[0], n, streams, part, d)
        wo_spec = pl.BlockSpec((count, n, None, part, d), lambda t, s: (base // count, 0, s[1], 0, 0), pipeline_mode=ONCE)
    else:
        wo_spec = pl.BlockSpec((count, d, d), lambda t, s: (base // count, 0, 0), pipeline_mode=ONCE)

    body = functools.partial(wgrad_ff_body, dm, experts, stacked)
    deps = order_after(deps)
    extra = len(deps)
    args = (*n2s, *gfs, wi, hbm(wo), bi)
    number = len(shapes)

    def wrapped(*refs):
        outs = refs[1 + len(args) + extra :]
        outs[number][...] = jnp.zeros_like(outs[number])
        body(*refs[: 1 + len(args)], *outs[:number], *outs[number + 1 :])

    gf_specs = [pl.BlockSpec((streams, live, d), lambda t, s: (0, 0, 0), pipeline_mode=ONCE)] if stacked else [pl.BlockSpec((live, d), lambda t, s: (0, 0), pipeline_mode=ONCE)] * streams
    *outs, token = pl.pallas_call(
        wrapped,
        grid_spec=pltpu.PrefetchScalarGridSpec(
            num_scalar_prefetch=1,
            grid=(1,),
            in_specs=[pl.BlockSpec((live, d), lambda t, s: (0, 0), pipeline_mode=ONCE)] * streams
            + gf_specs
            + [
                pl.BlockSpec((count, d, d), lambda t, s: (base // count, 0, 0), pipeline_mode=ONCE),
                wo_spec,
                pl.BlockSpec((count, 1, d), lambda t, s: (base // count, 0, 0), pipeline_mode=ONCE),
            ]
            + [ANY] * extra,
            out_specs=[pl.BlockSpec(shape, lambda t, s, shape=shape: (0,) * len(shape), pipeline_mode=ONCE) for shape in [*shapes, (8, 128)]],
            scratch_shapes=[pltpu.VMEM((top, d), BF)] * 4 + [pltpu.VMEM((n, share, d), BF)],
        ),
        out_shape=[sds(shape, BF) for shape in shapes] + [sds((8, 128), F32)],
        compiler_params=params(24),
        cost_estimate=cost(),
        name="wgrad_ff_body",
    )(sc, *args, *deps)
    note(outs, token)
    return outs


def finish_body(dm, sc, *refs):
    *pieces, first_out, second_out, stage = refs
    share, part = dm.share, dm.hidden // (dm.item_devs * dm.streams)
    expert = len(pieces) == 8
    for k, piece in enumerate(pieces):
        stage[k // 4, sc[1] ^ (k % 4)] = piece[...]
    if expert:
        for i in range(dm.item_devs):
            block = [stage[0, q, :, i * part : (i + 1) * part].astype(F32) for q in range(4)]
            first_out[0, :, i * 4 * part : (i + 1) * 4 * part] = jnp.concatenate(block, axis=1)
        for q in range(4):
            second_out[0, q * share : (q + 1) * share] = stage[1, q].astype(F32)
    else:
        for q in range(3):
            first_out[0, :, q * dm.width : (q + 1) * dm.width] = stage[0, q].astype(F32)
        second_out[0] = stage[0, 3].astype(F32)


def finish(dm, sc, sources, index, bases, *deps):
    share, d, hid = dm.share, dm.width, dm.hidden
    expert = len(sources) == 2
    if expert:
        shapes = [(3, share, hid), (3, 4 * share, d)]
    else:
        shapes = [(2, share, 3 * d), (2, share, d)]
    args, specs = [sc], [SMEM]
    for arrays, block in sources:
        args += arrays
        if dm.tiled:
            specs += [pl.BlockSpec((share, d), lambda t, block=block: (block, 0), pipeline_mode=ONCE)] * 4
        else:
            args[-4:] = [value[block * share : (block + 1) * share] for value in arrays]
            specs += [whole((share, d))] * 4
    deps = order_after(deps)
    count, extra = len(args), len(bases)

    def body(*refs):
        outs = refs[count + extra + len(deps) :]
        outs[2][...] = jnp.zeros_like(outs[2])
        finish_body(dm, *refs[:count], *outs[:2], outs[3])

    *outs, token = pl.pallas_call(
        body,
        grid=(1,),
        in_specs=specs + [pl.BlockSpec(memory_space=pltpu.HBM)] * extra + [ANY] * len(deps),
        out_specs=[
            pl.BlockSpec((1,) + shape[1:], lambda t: (index, 0, 0), pipeline_mode=ONCE) for shape in shapes
        ]
        + [whole((8, 128))],
        out_shape=[pltpu.HBM(shape, F32) for shape in shapes] + [sds((8, 128), F32)],
        scratch_shapes=[pltpu.VMEM((len(sources), 4, share, d), BF)],
        input_output_aliases={count + k: k for k in range(extra)},
        compiler_params=params(12),
        cost_estimate=cost(),
        name="finish_body",
    )(*args, *bases, *deps)
    note(outs, token)
    return outs


SMALL_ROWS = 32


def small_body(dm, sc, a0, a1, f0, f1, h0, h1, out):
    out[...] = jnp.zeros_like(out)
    share = dm.share
    wide = jnp.concatenate(
        [
            a0[2:4], a1[2:4],
            f0[2:3], f1[2:3],
            a0[0:1], f0[0:1], a1[0:1], f1[0:1],
            a0[1:2], f0[1:2], a1[1:2], f1[1:2],
            f0[3:5], f1[3:4],
        ],
        axis=0,
    )
    hidden = jnp.concatenate([h0[...], h1[...]], axis=0)
    count = wide.shape[0]
    for i in range(dm.item_devs):
        place = dm.place(i, dm.order_a) ^ sc[2]
        out[place, 0:count, 0:share] = wide[:, i * share : (i + 1) * share]
        for q in range(4):
            at = (i * 4 + q) * share
            out[place, count + 3 * q : count + 3 * q + 3, 0:share] = hidden[:, at : at + share]


def small_pack(dm, sc, values, deps):
    shape = (dm.item_devs, SMALL_ROWS, 128)
    return run(
        functools.partial(small_body, dm),
        (sc, *values),
        deps,
        grid=(1,),
        in_specs=[SMEM] + [whole(value.shape) for value in values],
        out_specs=whole(shape),
        out_shape=sds(shape, F32),
        compiler_params=params(8),
        cost_estimate=cost(),
    )


def small_out_body(dm, near, far, attn_bias, out_bias, gain, offset, hidden, ffn_bias):
    share = dm.share
    total = near[:, 0:share] + far[:, 0:share]
    for l in range(2):
        attn_bias[l] = total[2 * l : 2 * l + 2]
        gain[l] = total[6 + 2 * l : 8 + 2 * l]
        offset[l] = total[10 + 2 * l : 12 + 2 * l]
    out_bias[...] = total[4:6]
    ffn_bias[...] = total[14:17]
    hidden[...] = jnp.concatenate([total[17 + 3 * q : 20 + 3 * q] for q in range(4)], axis=1)


def small_unpack(dm, near, far, *deps):
    share = dm.share
    shapes = [(2, 2, share), (2, share), (2, 2, share), (2, 2, share), (3, 4 * share), (3, share)]
    return run(
        functools.partial(small_out_body, dm),
        (near, far),
        deps,
        grid=(1,),
        in_specs=[whole(near.shape)] * 2,
        out_specs=[whole(shape) for shape in shapes],
        out_shape=[sds(shape, F32) for shape in shapes],
        compiler_params=params(8),
        cost_estimate=cost(),
    )


def swap(value, axis, bit):
    size = lax.axis_size(axis)
    return lax.ppermute(value, axis, [(i, i ^ bit) for i in range(size)])


def by_index(blocks, index):
    return lax.dynamic_index_in_dim(blocks, index, 0, keepdims=False)


def gather_start(value):
    return [value, swap(value, "stream", 1), swap(value, "stream", 2)]


def gather_end(parts, *later):
    far = after(parts[2], *later) if later else parts[2]
    return parts + [swap(far, "stream", 1)]


def gather_rel(value):
    return gather_end(gather_start(value))


def after(value, *others):
    return lax.optimization_barrier((value, *others))[0]


def add_up(values):
    total = values[0].astype(F32)
    for value in values[1:]:
        total = total + value.astype(F32)
    return total


def add_body(count, *refs):
    refs[count][...] = add_up([ref[...] for ref in refs[:count]]).astype(refs[count].dtype)


def add_part(terms, size, index, deps=()):
    shape = (size,) + terms[0].shape[1:]
    return run(
        functools.partial(add_body, len(terms)),
        terms,
        deps,
        grid=(1,),
        in_specs=[pl.BlockSpec(shape, lambda t: (index, 0, 0))] * len(terms),
        out_specs=whole(shape),
        out_shape=sds(shape, terms[0].dtype),
        compiler_params=params(8),
        cost_estimate=cost(),
    )


def pieces_body(counts, *refs):
    out = refs[-1]
    row = at = 0
    for count in counts:
        terms = refs[at : at + count]
        rows = terms[0].shape[1]
        out[row : row + rows] = add_up([term[0] for term in terms]).astype(out.dtype)
        at += count
        row += rows


def add_pieces(sums, deps=()):
    terms = [term for value in sums for term in value.terms]
    rows = sum(value.terms[0].shape[1] for value in sums)
    shape = (rows, terms[0].shape[2])
    return run(
        functools.partial(pieces_body, [len(value.terms) for value in sums]),
        terms,
        deps,
        grid=(1,),
        in_specs=[pl.BlockSpec((1,) + term.shape[1:], lambda t: (0, 0, 0)) for term in terms],
        out_specs=whole(shape),
        out_shape=sds(shape, terms[0].dtype),
        compiler_params=params(8),
        cost_estimate=cost(),
    )


class Halving:
    def __init__(self, order, terms, size, send=None, deps=()):
        self.order = list(order)
        self.terms = list(terms)
        self.size = size
        if send is None:
            self.more(deps)
        else:
            self.send(send)

    def send(self, value):
        self.size //= 2
        self.last = value
        self.terms.append(swap(value, "items", 1 << self.order.pop(0)))

    def more(self, deps=()):
        if self.order:
            self.send(add_part(self.terms, self.size // 2, 1, deps))
        return self.last

    def drain(self):
        while self.order:
            self.more()
        return self


def per_device(
    tokens,
    cotangent,
    text_len,
    attn_in,
    attn_bias,
    attn_out,
    out_bias,
    norm_gain,
    norm_bias,
    ffn_in,
    ffn_in_bias,
    ffn_out,
    ffn_out_bias,
):
    streams = lax.axis_size("stream")
    item_devs = lax.axis_size("items")
    stream = lax.axis_index("stream")
    item = lax.axis_index("items")
    _, slots, width = tokens.shape
    hidden = ffn_in.shape[2]
    dm = Dims(slots, streams, width, hidden, item_devs)
    share = dm.share
    sc = jnp.stack([stream * 0, stream, dm.place(item, dm.order_a), dm.place(item, dm.order_b)]).astype(jnp.int32)

    part = hidden // (item_devs * streams)
    if dm.tiled:
        wi_q, bi_q = select_quarter(dm, sc, ffn_in, ffn_in_bias)
        wo_q = ffn_out
    else:
        wi_q = by_index(jnp.moveaxis(ffn_in.reshape(3, width, item_devs, streams, part), 3, 0), stream).reshape(3, width, width)
        wo_q = by_index(jnp.moveaxis(ffn_out.reshape(3, item_devs, streams, part, width), 2, 0), stream).reshape(3, width, width)
        bi_q = by_index(jnp.moveaxis(ffn_in_bias.reshape(3, item_devs, streams, part), 2, 0), stream).reshape(3, 1, width).astype(F32)

    far = swap(lax.dynamic_slice_in_dim(tokens, 2 * (1 - stream // 2), 2, 0), "stream", 2)
    far = after(far, bi_q)
    near = swap(jnp.stack([by_index(tokens, stream ^ 1), by_index(far, 1 - stream % 2)]), "stream", 1)
    cots = gather_start(after(cotangent, near))

    layer_params = (norm_gain, norm_bias, attn_in, attn_bias, attn_out, out_bias)
    a0 = fwd_attn(dm, 0, sc, text_len, (tokens, near, far), *layer_params)
    nc_0, q_0, k_0, v_0, p_0, x1_0, n2_0, n2l_0, x_0 = a0
    nc_near_0 = swap(nc_0, "stream", 1)
    n2_all_0 = gather_start(n2l_0)
    sv_0, sl_0, x_1 = fwd_ff_two(dm, n2_0, x1_0, ffn_in, ffn_in_bias, ffn_out, ffn_out_bias)
    cots = gather_end(cots, sv_0)
    n2_all_0 = gather_end(n2_all_0, sv_0)
    a1 = fwd_attn(dm, 1, sc, text_len, (x_1,), *layer_params)
    nc_1, q_1, k_1, v_1, p_1, x1_1, n2_1, n2l_1 = a1
    nc_near_1 = swap(nc_1, "stream", 1)
    n2_all_1 = gather_start(n2l_1)
    gf_all_1 = cot_prep(dm, sc, text_len, cots, (n2l_1, n2_all_0[3]))
    mix, g, ga_1, fs_1, hs_1 = top_ff(
        dm, 1, 2, sc, n2_1, gf_all_1, x1_1, norm_gain, ffn_in, ffn_in_bias, ffn_out, ffn_out_bias
    )
    n2_all_1 = gather_end(n2_all_1, fs_1)

    live, vis, lang, text_at = dm.live, dm.vis, dm.lang, dm.text_at
    half = item_devs // 2
    a, b = dm.order_a, dm.order_b

    def reorder(value, order):
        places = jnp.stack([dm.place(jnp.int32(i), order) for i in range(item_devs)])
        source = jnp.zeros((item_devs,), jnp.int32).at[places ^ dm.place(item, order)].set(jnp.arange(item_devs, dtype=jnp.int32))
        value = value.reshape(value.shape[:-2] + (item_devs, share, width))
        return jnp.take(value, source, axis=value.ndim - 3)

    def pairs(values, experts):
        if dm.tiled:
            return [values[2 * k : 2 * k + 2] for k in range(len(values) // 2)]
        out = []
        for index, (*_, orders) in enumerate(experts):
            sides = [reorder(values[2 * index + side], orders[side]) for side in range(2)]
            if orders[0] is orders[1]:
                sides = [jnp.concatenate(sides, axis=1)]
            out += [(value[:half], value[half:]) for value in sides]
        return out

    def halving(pair, order, *later):
        return Halving(order, [pair[0]], item_devs, after(pair[1], *later) if later else pair[1])

    def attn_sum(keep, send, *later):
        if not dm.tiled:
            keep, send = reorder(keep, a), reorder(send, a)
        return [keep, swap(after(send, *later) if later else send, "stream", 2)]

    experts = ((2, 0, live, 0, live, (a, a)),)
    join = wgrad_ff(dm, experts, sc, n2_all_1, (gf_all_1,), wi_q, wo_q, bi_q, deps=(fs_1,))
    join_sum = halving(pairs(join, experts)[0], a)
    mine_1, near_1, far_1, as_1, g, gf_0 = back_attn(
        dm, 1, sc, g, ga_1, q_1, k_1, v_1, p_1, x_1, norm_gain, attn_in, attn_out, deps=(join[0],)
    )
    gf_all_0 = gather_start(gf_0)
    near_1, far_1 = swap(near_1, "stream", 1), swap(far_1, "stream", 1)
    g, ga_0, fs_0, hs_0 = back_ff_two(dm, 0, g, gf_0, x1_0, norm_gain, sv_0, sl_0, ffn_in, ffn_out)
    gf_all_0 = gather_end(gf_all_0, fs_0)
    att_1 = wgrad_attn(dm, sc, nc_1, nc_near_1, mine_1, near_1, far_1, deps=(fs_0,))
    att_1_terms = attn_sum(*att_1)
    experts = ((0, 0, vis, 0, text_at, (a, list(a))), (1, lang, live, text_at, live, (a, b)))
    last = join_sum.more((att_1[0],))
    two = wgrad_ff(dm, experts, sc, n2_all_0, gf_all_0, wi_q, wo_q, bi_q, deps=(last,))
    va, vb, la, lb = pairs(two, experts)
    va_sum = halving(va, a)
    lb_sum = halving(lb, b)
    last = join_sum.more((two[0],))
    mine_0, near_0, far_0, as_0, tg_own, tg_near, tg_far = back_attn(
        dm, 0, sc, g, ga_0, q_0, k_0, v_0, p_0, x_0, norm_gain, attn_in, attn_out, mix=mix, deps=(last,)
    )
    near_0, far_0 = swap(near_0, "stream", 1), swap(far_0, "stream", 1)
    small = small_pack(dm, sc, (as_0, as_1, fs_0, fs_1, hs_0, hs_1), ())
    last = va_sum.more((small,))
    vb_sum = halving(vb, a, last)
    att_1_sum = Halving(a, att_1_terms, item_devs, deps=(last,))
    last = lb_sum.more((att_1_sum.last,))
    att_0 = wgrad_attn(dm, sc, nc_0, nc_near_0, mine_0, near_0, far_0, deps=(last,))
    att_0_terms = attn_sum(*att_0)
    last = va_sum.more((att_0[0],))
    last = vb_sum.more((last,))
    join_piece = add_pieces([join_sum.drain()], deps=(last,))
    last = vb_sum.more((join_piece,))
    att_0_sum = Halving(a, att_0_terms, item_devs, deps=(last,))
    last = att_1_sum.more((att_0_sum.last,))
    va_piece = add_pieces([va_sum.drain()], deps=(last,))
    last = lb_sum.more((va_piece,))
    la_sum = halving(la, a, last)
    last = att_1_sum.more((last,))
    tg_far = swap(after(tg_far, va_piece), "stream", 2)
    lb_piece = add_pieces([lb_sum.drain()], deps=(last,))
    vb_piece = add_pieces([vb_sum.drain()], deps=(lb_piece,))
    tg_near = swap(jnp.concatenate([tg_near, after(tg_far, vb_piece)[1::2]]), "stream", 1)
    all_1 = gather_start(jnp.concatenate([join_piece, va_piece, vb_piece, lb_piece]))
    last = att_0_sum.more((vb_piece,))
    small_sum = Halving(a, [small[:half]], item_devs, after(small[half:], last))
    att_1_piece = add_pieces([att_1_sum.drain()], deps=(last,))
    last = la_sum.more((att_1_piece,))
    last = att_0_sum.more((last,))
    last = small_sum.more((last,))
    att_0_piece = add_pieces([att_0_sum.drain()], deps=(last,))
    last = la_sum.more((att_0_piece,))
    all_1 = gather_end(all_1, last)
    all_2 = gather_start(after(jnp.concatenate([att_0_piece, att_1_piece]), all_1[2]))
    results = finish(dm, sc, [(all_1, 0), (all_1, 1)], 2, (), last)
    last = small_sum.more((results[0],))
    mixed, tokens_grad = join_shards(dm, sc, tg_own, tg_near, tg_far, last)
    results = finish(dm, sc, [(all_1, 2), (all_1, 3)], 0, results, mixed)
    la_piece = add_pieces([la_sum.drain()], deps=(results[0],))
    all_2 = gather_end(all_2, la_piece)
    all_3 = gather_start(after(la_piece, all_2[2]))
    attn_results = finish(dm, sc, [(all_2, 1)], 1, (), la_piece)
    attn_results = finish(dm, sc, [(all_2, 0)], 0, attn_results)
    small_own = add_pieces([small_sum.drain()], deps=(attn_results[0],))
    small_near = small_own + swap(small_own, "stream", 1)
    small_all = swap(small_near, "stream", 2)
    all_3 = gather_end(all_3, small_own)
    ffn_results = finish(dm, sc, [(all_3, 0), (all_1, 4)], 1, results, small_own)
    outs = small_unpack(dm, small_near, small_all, ffn_results[0])

    return (
        mixed,
        tokens_grad,
        attn_results[0],
        outs[0],
        attn_results[1],
        outs[1],
        outs[2],
        outs[3],
        ffn_results[0],
        outs[4],
        ffn_results[1],
        outs[5],
    )


def solution(mesh):
    return jax.shard_map(
        per_device,
        mesh=mesh,
        in_specs=(
            P("items", "stream", None),
            P("items", "stream", None),
            P("items"),
            P(),
            P(),
            P(),
            P(),
            P(),
            P(),
            P(),
            P(),
            P(),
            P(),
        ),
        out_specs=(
            P("items", "stream", None),
            P("items", "stream", None),
            P(None, "items", None),
            P(None, None, "items"),
            P(None, "items", None),
            P(None, "items"),
            P(None, None, "items"),
            P(None, None, "items"),
            P(None, "items", None),
            P(None, "items"),
            P(None, "items", None),
            P(None, "items"),
        ),
        check_vma=False,
    )
```

```python
import functools
import jax
import jax.numpy as jnp
from jax import lax
from jax.experimental import pallas as pl
from jax.experimental.pallas import tpu as pltpu
from jax.sharding import PartitionSpec as P

HEADS = 12
PATCHES = 197
TEXT = 40
F32 = jnp.float32
BF = jnp.bfloat16
EPS = 1e-06
FILL = -1e30
MIB = 1 << 20
PAD = 80
TILE = 1024


def dot(left, right, dims=((1,), (0,))):
    return lax.dot_general(left, right, (dims, ((), ())), preferred_element_type=F32)


NT = ((1,), (1,))
TN = ((0,), (0,))


def norm_stats(values):
    row_mean = jnp.mean(values, axis=-1, keepdims=True)
    centred = values - row_mean
    row_var = jnp.mean(centred * centred, axis=-1, keepdims=True)
    inv_std = lax.rsqrt(row_var + EPS)
    return centred * inv_std, inv_std


def norm_back(grad_out, values, gain):
    scaled, inv_std = norm_stats(values)
    grad_scaled = grad_out * gain
    mean_first = jnp.mean(grad_scaled, axis=-1, keepdims=True)
    mean_second = jnp.mean(grad_scaled * scaled, axis=-1, keepdims=True)
    grad_in = inv_std * (grad_scaled - mean_first - scaled * mean_second)
    gain_sum = jnp.sum(grad_out * scaled, axis=0, keepdims=True)
    offset_sum = jnp.sum(grad_out, axis=0, keepdims=True)
    return grad_in, gain_sum, offset_sum


def gelu_parts(pre):
    cumulative = 0.5 * (1.0 + lax.erf(pre * 0.7071067811865476))
    density = jnp.exp(-0.5 * pre * pre) * 0.3989422804014327
    return pre * cumulative, cumulative + pre * density


def params(limit_mib):
    return pltpu.CompilerParams(vmem_limit_bytes=limit_mib * MIB)


def cost():
    return pl.CostEstimate(flops=1, bytes_accessed=1, transcendentals=0)


ONCE = pl.Buffered(1)


def whole(shape):
    return pl.BlockSpec(shape, lambda *_: (0,) * len(shape), pipeline_mode=ONCE)


def layer_block(shape, index):
    return pl.BlockSpec((1,) + shape, lambda *_: (index,) + (0,) * len(shape), pipeline_mode=ONCE)


SMEM = pl.BlockSpec(memory_space=pltpu.SMEM)
ANY = pl.BlockSpec(memory_space=pl.ANY)
sds = jax.ShapeDtypeStruct


TOKENS = {}


def order_after(deps):
    return tuple(TOKENS[id(dep)][1] if id(dep) in TOKENS else dep for dep in deps)


def note(outs, token):
    for out in outs:
        TOKENS[id(out)] = (out, token)


def run(body, args, deps=(), *, in_specs, out_specs, out_shape, grid_spec=None, call=None, **rest):
    deps = order_after(deps)
    count, extra = len(args), len(deps)
    single = not isinstance(out_shape, (list, tuple))
    if single:
        out_specs, out_shape = [out_specs], [out_shape]
    number = len(out_shape)

    def wrapped(*refs):
        outs = refs[count + extra :]
        outs[number][...] = jnp.zeros_like(outs[number])
        body(*refs[:count], *outs[:number], *outs[number + 1 :])

    outs = pl.pallas_call(
        wrapped,
        in_specs=list(in_specs) + [ANY] * extra,
        out_specs=list(out_specs) + [whole((8, 128))],
        out_shape=list(out_shape) + [sds((8, 128), F32)],
        name=call or getattr(body, "func", body).__name__,
        **rest,
    )(*args, *deps)
    *outs, token = outs
    note(outs, token)
    return outs[0] if single else outs


def hbm(value):
    return pltpu.with_memory_space_constraint(value, pltpu.HBM)


def first(shape):
    return lax.broadcasted_iota(jnp.int32, shape, 0)


def second(shape):
    return lax.broadcasted_iota(jnp.int32, shape, 1)


class Dims:
    def __init__(self, slots, streams, width, hidden, item_devs):
        self.slots = slots
        self.text_at = slots * (streams - 1)
        self.rows = slots * streams
        self.full = -(-self.rows // 16) * 16
        self.live = -(-(self.text_at + TEXT) // 16) * 16
        self.keys = -(-self.live // 128) * 128
        self.vis = -(-self.text_at // 16) * 16
        self.lang = self.text_at // 16 * 16
        self.width = width
        self.hidden = hidden
        self.streams = streams
        self.item_devs = item_devs
        self.share = width // item_devs
        self.bits = item_devs.bit_length() - 1
        self.order_a = list(range(self.bits))
        self.order_b = self.order_a[1:] + self.order_a[:1]
        self.tiled = self.share % 16 == 0

    def place(self, index, order):
        out = index * 0
        for k, bit in enumerate(order):
            out = out | (((index >> bit) & 1) << (self.bits - 1 - k))
        return out


def put_stage(dm, stage, pieces):
    stage[...] = jnp.zeros_like(stage)
    for r, piece in enumerate(pieces):
        stage[r * PAD : r * PAD + dm.slots] = piece


def slot_select(dm, rows, stream):
    shape = (rows, 4 * PAD)
    slot = first(shape)
    shard = jnp.zeros(shape, jnp.int32)
    for k in range(1, dm.streams):
        shard = shard + (slot >= k * dm.slots).astype(jnp.int32)
    place = slot - shard * dm.slots
    return second(shape) == ((shard ^ stream) * PAD + place), slot


def shard_rows(dm, rows, shard):
    shape = (-(-dm.slots // 8) * 8, rows)
    return ((second(shape) == first(shape) + shard * dm.slots) & (first(shape) < dm.slots)).astype(BF)


def split_shards(dm, value, stream, refs):
    for r, ref in enumerate(refs):
        ref[...] = dot(shard_rows(dm, value.shape[0], stream ^ r), value)[: dm.slots].astype(BF)


def cot_prep_body(dm, sc, lens, c0, c1, c2, c3, out, stage):
    stream = sc[1]
    pick, slot = slot_select(dm, dm.live, stream)
    for r in range(4):
        put_stage(dm, stage, [c[stream ^ r] for c in (c0, c1, c2, c3)])
        alive = (slot < PATCHES) | ((slot >= dm.text_at) & (slot < dm.text_at + lens[stream ^ r]))
        out[r] = dot((pick & alive).astype(BF), stage[...]).astype(BF)


def cot_prep(dm, sc, lens, pieces, deps):
    shape = pieces[0].shape
    return run(
        functools.partial(cot_prep_body, dm),
        (sc, lens, *pieces),
        deps,
        grid=(1,),
        in_specs=[SMEM, SMEM] + [whole(shape)] * 4,
        out_specs=whole((4, dm.live, dm.width)),
        out_shape=sds((4, dm.live, dm.width), BF),
        scratch_shapes=[pltpu.VMEM((4 * PAD, dm.width), BF)],
        compiler_params=params(12),
        cost_estimate=cost(),
    )


def join_shards_body(sc, own, near, far, mixed, grad):
    stream = sc[1]
    for k, out in enumerate((mixed, grad)):
        for r, value in enumerate((own[k], near[k], far[2 * k], near[2 + k])):
            out[stream ^ r] = value.astype(out.dtype)


def join_shards(dm, sc, own, near, far, *deps):
    shape = (4, dm.slots, dm.width)
    return run(
        join_shards_body,
        (sc, own, near, far),
        deps,
        grid=(1,),
        in_specs=[SMEM, whole(own.shape), whole(near.shape), whole(far.shape)],
        out_specs=[whole(shape)] * 2,
        out_shape=[sds(shape, BF), sds(shape, F32)],
        compiler_params=params(8),
        cost_estimate=cost(),
    )


def select_body(dm, sc, *refs):
    *parts, b, wo, bo = refs
    part = dm.hidden // (dm.item_devs * dm.streams)
    rows = parts[0].shape[1]
    for s in range(dm.streams):

        @pl.when(sc[1] == s)
        def _(s=s):
            starts = [i * part * dm.streams + s * part for i in range(dm.item_devs)]
            for k, w in enumerate(parts):
                wo[0, k * rows : (k + 1) * rows] = jnp.concatenate([w[0, :, at : at + part] for at in starts], axis=1)
            bo[0] = jnp.concatenate([b[0, :, at : at + part].astype(F32) for at in starts], axis=1)


def select_quarter(dm, sc, ffn_in, ffn_in_bias):
    d, hid = dm.width, dm.hidden
    count = ffn_in.shape[0]
    pieces = 4
    return run(
        functools.partial(select_body, dm),
        (sc, *[hbm(ffn_in)] * pieces, ffn_in_bias[:, None]),
        grid=(count,),
        in_specs=[SMEM]
        + [pl.BlockSpec((1, d // pieces, hid), lambda e, k=k: (e, k, 0)) for k in range(pieces)]
        + [pl.BlockSpec((1, 1, hid), lambda e: (e, 0, 0))],
        out_specs=[
            pl.BlockSpec((1, d, d), lambda e: (e, 0, 0)),
            pl.BlockSpec((1, 1, d), lambda e: (e, 0, 0)),
        ],
        out_shape=[sds((count, d, d), BF), sds((count, 1, d), F32)],
        compiler_params=params(60),
        cost_estimate=cost(),
    )


def fwd_attn_body(dm, own_len, xv, gain, offset, win, bias, wout, obias, nco, qo, ko, vo, po, x1o, n2o, n2live, ctx_s):
    width = dm.width
    scaled, _ = norm_stats(xv)
    n1 = (scaled * gain[0, 0:1].astype(F32) + offset[0, 0:1].astype(F32)).astype(BF)
    nco[0] = n1[: dm.live]
    w = win.at[0]
    q = (dot(n1, w[:, 0:width]) + bias[0, 0:1].astype(F32)).astype(BF) * 0.125
    q = q.astype(BF)
    k = dot(n1[: dm.keys], w[:, width : 2 * width]).astype(BF)
    v = (dot(n1[: dm.keys], w[:, 2 * width :]) + bias[0, 1:2].astype(F32)).astype(BF)
    qo[...] = q[: dm.live]
    ko[...] = k
    vo[...] = v
    col = lax.broadcasted_iota(jnp.int32, (1, dm.keys), 1)
    valid = (col < PATCHES) | ((col >= dm.text_at) & (col < dm.text_at + own_len))
    low_lane = lax.broadcasted_iota(jnp.int32, (1, 128), 1) < 64
    for pair in range(HEADS // 2):
        lanes = slice(pair * 128, pair * 128 + 128)
        qp, kp, vp = q[:, lanes], k[:, lanes], v[:, lanes]
        outs = []
        for j in range(2):
            qm = jnp.where(low_lane if j == 0 else ~low_lane, qp, jnp.zeros_like(qp))
            scores = jnp.where(valid, dot(qm, kp, NT), FILL)
            top = jnp.max(scores, axis=-1, keepdims=True)
            expo = jnp.exp(scores - top)
            probs = (expo * (1.0 / jnp.sum(expo, axis=-1, keepdims=True))).astype(BF)
            po[2 * pair + j] = probs[: dm.live]
            outs.append(dot(probs, vp))
        ctx_s[:, lanes] = jnp.where(low_lane, outs[0], outs[1]).astype(BF)
    ctx = ctx_s[...]
    nco[1] = ctx[: dm.live]
    x1 = xv + (dot(ctx, wout[0]) + obias[0].astype(F32))
    x1o[...] = x1
    scaled, _ = norm_stats(x1)
    n2 = (scaled * gain[0, 1:2].astype(F32) + offset[0, 1:2].astype(F32)).astype(BF)
    n2o[...] = n2
    n2live[...] = n2[: dm.live]


def fwd_attn_next_body(dm, sc, lens, x, *refs):
    fwd_attn_body(dm, lens[sc[1]], x[...], *refs)


def fwd_attn_first_body(dm, sc, lens, tokens, near, far, *refs):
    stream = sc[1]
    *refs, x0, ctx_s, stage = refs
    put_stage(dm, stage, [tokens[stream], near[0], far[stream & 1], near[1]])
    pick, _ = slot_select(dm, dm.full, stream)
    xv = dot(pick.astype(BF), stage[...])
    x0[...] = xv.astype(BF)
    fwd_attn_body(dm, lens[stream], xv, *refs, ctx_s)


def fwd_attn(dm, layer, sc, lens, inputs, norm_gain, norm_bias, attn_in, attn_bias, attn_out, out_bias, deps=()):
    d, full, live, keys = dm.width, dm.full, dm.live, dm.keys
    shapes = [
        sds((2, live, d), BF),
        sds((live, d), BF),
        sds((keys, d), BF),
        sds((keys, d), BF),
        sds((HEADS, live, keys), BF),
        sds((full, d), F32),
        sds((full, d), BF),
        sds((live, d), BF),
    ]
    scratch = [pltpu.VMEM((full, d), BF)]
    body = fwd_attn_next_body
    if len(inputs) > 1:
        body = fwd_attn_first_body
        shapes.append(sds((full, d), BF))
        scratch.append(pltpu.VMEM((4 * PAD, d), BF))
    return run(
        functools.partial(body, dm),
        (sc, lens, *inputs, norm_gain, norm_bias, hbm(attn_in), attn_bias, hbm(attn_out), out_bias[:, None]),
        deps,
        grid=(1,),
        in_specs=[SMEM, SMEM]
        + [whole(value.shape) for value in inputs]
        + [
            layer_block((2, d), layer),
            layer_block((2, d), layer),
            layer_block((d, 3 * d), layer),
            layer_block((2, d), layer),
            layer_block((d, d), layer),
            layer_block((1, d), layer),
        ],
        out_specs=[whole(s.shape) for s in shapes],
        out_shape=shapes,
        scratch_shapes=scratch,
        compiler_params=params(16),
        cost_estimate=cost(),
    )


def fwd_ff_two_body(dm, n2, x1, wv, wl, bi, wov, wol, bo, slope_v, slope_l, x2, acc):
    t = pl.program_id(0)
    vis, lang, text_at = dm.vis, dm.lang, dm.text_at
    rows_v = lax.broadcasted_iota(jnp.int32, (vis, 1), 0) < text_at
    rows_l = lax.broadcasted_iota(jnp.int32, (dm.full - lang, 1), 0) + lang >= text_at
    act_v, sv = gelu_parts(dot(n2[0:vis], wv[0]) + bi[0, 0:1].astype(F32))
    act_l, sl = gelu_parts(dot(n2[lang:], wl[0]) + bi[1, 0:1].astype(F32))
    slope_v[...] = sv.astype(BF)
    slope_l[...] = sl[: dm.live - lang].astype(BF)
    part_v = dot(act_v.astype(BF), wov[0])
    part_l = dot(act_l.astype(BF), wol[0])

    @pl.when(t == 0)
    def _():
        acc[...] = x1[...]
        part_vb = part_v + bo[0, 0:1].astype(F32)
        part_lb = part_l + bo[1, 0:1].astype(F32)
        acc[0:vis] += jnp.where(rows_v, part_vb, 0.0)
        acc[lang:] += jnp.where(rows_l, part_lb, 0.0)

    @pl.when(t > 0)
    def _():
        acc[0:vis] += jnp.where(rows_v, part_v, 0.0)
        acc[lang:] += jnp.where(rows_l, part_l, 0.0)

    @pl.when(t == pl.num_programs(0) - 1)
    def _():
        x2[...] = acc[...]


def fwd_ff_two(dm, n2, x1, ffn_in, ffn_in_bias, ffn_out, ffn_out_bias, deps=()):
    d, full, hid = dm.width, dm.full, dm.hidden
    count = ffn_in.shape[0]
    return run(
        functools.partial(fwd_ff_two_body, dm),
        (n2, x1, hbm(ffn_in), hbm(ffn_in), ffn_in_bias[:, None], hbm(ffn_out), hbm(ffn_out), ffn_out_bias[:, None]),
        deps,
        grid=(hid // TILE,),
        in_specs=[
            whole((full, d)),
            whole((full, d)),
            pl.BlockSpec((1, d, TILE), lambda t: (0, 0, t)),
            pl.BlockSpec((1, d, TILE), lambda t: (1, 0, t)),
            pl.BlockSpec((count, 1, TILE), lambda t: (0, 0, t)),
            pl.BlockSpec((1, TILE, d), lambda t: (0, t, 0)),
            pl.BlockSpec((1, TILE, d), lambda t: (1, t, 0)),
            whole((count, 1, d)),
        ],
        out_specs=[
            pl.BlockSpec((dm.vis, TILE), lambda t: (0, t)),
            pl.BlockSpec((dm.live - dm.lang, TILE), lambda t: (0, t)),
            whole((full, d)),
        ],
        out_shape=[sds((dm.vis, hid), BF), sds((dm.live - dm.lang, hid), BF), sds((full, d), F32)],
        scratch_shapes=[pltpu.VMEM((full, d), F32)],
        compiler_params=params(36),
        cost_estimate=cost(),
    )


def finish_ff_back(dm, g, gn, x1, gain, go, ga, sums):
    grad_in, gain_sum, offset_sum = norm_back(gn, x1[0 : dm.live], gain[0, 1:2].astype(F32))
    out = g + grad_in
    go[...] = out
    low = out.astype(BF)
    ga[...] = low
    sums[0:1] = gain_sum
    sums[1:2] = offset_sum
    sums[2:3] = jnp.sum(low.astype(F32), axis=0, keepdims=True)


def top_ff_body(dm, sc, n2, gf, x1, gain, wi, bi, wo, bo, mix, go, ga, sums, hsum, accm, accg):
    t = pl.program_id(0)
    act, slope = gelu_parts(dot(n2[...], wi[0]) + bi[0].astype(F32))
    gpre = (dot(gf[0], wo[0], NT) * slope[: dm.live]).astype(BF)
    hsum[...] = jnp.sum(gpre.astype(F32), axis=0, keepdims=True)
    part = dot(act.astype(BF), wo[0])
    back = dot(gpre, wi[0], NT)

    @pl.when(t == 0)
    def _():
        accm[...] = part + (x1[...] + bo[0].astype(F32))
        accg[...] = back

    @pl.when(t > 0)
    def _():
        accm[...] += part
        accg[...] += back

    @pl.when(t == pl.num_programs(0) - 1)
    def _():
        split_shards(dm, accm[...].astype(BF), sc[1], [mix.at[r] for r in range(4)])
        g = gf[0].astype(F32)
        sums[3:4] = jnp.sum(g, axis=0, keepdims=True)
        finish_ff_back(dm, g, accg[...], x1, gain, go, ga, sums)


def top_ff(dm, layer, expert, sc, n2, gf, x1, norm_gain, ffn_in, ffn_in_bias, ffn_out, ffn_out_bias, deps=()):
    d, full, live, hid, slots = dm.width, dm.full, dm.live, dm.hidden, dm.slots
    shapes = [
        sds((4, slots, d), BF),
        sds((live, d), F32),
        sds((live, d), BF),
        sds((4, d), F32),
    ]
    return run(
        functools.partial(top_ff_body, dm),
        (sc, n2, gf, x1, norm_gain, hbm(ffn_in), ffn_in_bias[:, None], hbm(ffn_out), ffn_out_bias[:, None]),
        deps,
        grid=(hid // TILE,),
        in_specs=[
            SMEM,
            whole((full, d)),
            layer_block((live, d), 0),
            whole((full, d)),
            layer_block((2, d), layer),
            pl.BlockSpec((1, d, TILE), lambda t: (expert, 0, t)),
            pl.BlockSpec((1, 1, TILE), lambda t: (expert, 0, t)),
            pl.BlockSpec((1, TILE, d), lambda t: (expert, t, 0)),
            layer_block((1, d), expert),
        ],
        out_specs=[whole(s.shape) for s in shapes] + [pl.BlockSpec((1, TILE), lambda t: (0, t))],
        out_shape=shapes + [sds((1, hid), F32)],
        scratch_shapes=[pltpu.VMEM((full, d), F32), pltpu.VMEM((live, d), F32)],
        compiler_params=params(36),
        cost_estimate=cost(),
    )


def back_ff_two_body(dm, g, gf, x1, gain, slv, sll, wov, wol, wv, wl, go, ga, sums, hsum, acc):
    t = pl.program_id(0)
    vis, lang, text_at, live = dm.vis, dm.lang, dm.text_at, dm.live
    rows_v = lax.broadcasted_iota(jnp.int32, (vis, 1), 0) < text_at
    rows_l = lax.broadcasted_iota(jnp.int32, (live - lang, 1), 0) + lang >= text_at
    gv = jnp.where(rows_v, gf[0:vis].astype(F32), 0.0)
    gl = jnp.where(rows_l, gf[lang:].astype(F32), 0.0)
    pre_v = (dot(gv.astype(BF), wov[0], NT) * slv[...].astype(F32)).astype(BF)
    pre_l = (dot(gl.astype(BF), wol[0], NT) * sll[...].astype(F32)).astype(BF)
    hsum[0:1] = jnp.sum(pre_v.astype(F32), axis=0, keepdims=True)
    hsum[1:2] = jnp.sum(pre_l.astype(F32), axis=0, keepdims=True)
    part_v = dot(pre_v, wv[0], NT)
    part_l = dot(pre_l, wl[0], NT)

    @pl.when(t == 0)
    def _():
        acc[...] = jnp.zeros_like(acc)

    acc[0:vis] += part_v
    acc[lang:] += part_l

    @pl.when(t == pl.num_programs(0) - 1)
    def _():
        sums[3:4] = jnp.sum(gv, axis=0, keepdims=True)
        sums[4:5] = jnp.sum(gl, axis=0, keepdims=True)
        finish_ff_back(dm, g[...], acc[...], x1, gain, go, ga, sums)


def back_ff_two(dm, layer, g, gf, x1, norm_gain, slope_v, slope_l, ffn_in, ffn_out, deps=()):
    d, live, hid = dm.width, dm.live, dm.hidden
    return run(
        functools.partial(back_ff_two_body, dm),
        (g, gf, x1, norm_gain, slope_v, slope_l, hbm(ffn_out), hbm(ffn_out), hbm(ffn_in), hbm(ffn_in)),
        deps,
        grid=(hid // TILE,),
        in_specs=[
            whole((live, d)),
            whole((live, d)),
            whole((dm.full, d)),
            layer_block((2, d), layer),
            pl.BlockSpec((dm.vis, TILE), lambda t: (0, t)),
            pl.BlockSpec((live - dm.lang, TILE), lambda t: (0, t)),
            pl.BlockSpec((1, TILE, d), lambda t: (0, t, 0)),
            pl.BlockSpec((1, TILE, d), lambda t: (1, t, 0)),
            pl.BlockSpec((1, d, TILE), lambda t: (0, 0, t)),
            pl.BlockSpec((1, d, TILE), lambda t: (1, 0, t)),
        ],
        out_specs=[
            whole((live, d)),
            whole((live, d)),
            whole((5, d)),
            pl.BlockSpec((2, TILE), lambda t: (0, t)),
        ],
        out_shape=[sds((live, d), F32), sds((live, d), BF), sds((5, d), F32), sds((2, hid), F32)],
        scratch_shapes=[pltpu.VMEM((live, d), F32)],
        compiler_params=params(36),
        cost_estimate=cost(),
    )


def back_attn_body(dm, bottom, sc, g, ga, q, k, v, p, x, gain, win, wout, *refs):
    width, live = dm.width, dm.live
    *refs, parts = refs
    mine, other_near, other_far, sums, *outs = refs[1:] if bottom else refs
    gc = dot(ga[...], wout[0], NT).astype(BF)
    low_lane = lax.broadcasted_iota(jnp.int32, (1, 128), 1) < 64
    for pair in range(HEADS // 2):
        lanes = slice(pair * 128, pair * 128 + 128)
        gp, qp, kp, vp = gc[:, lanes], q[:, lanes], k[:, lanes], v[:, lanes]
        dqs, dks, dvs = [], [], []
        for j in range(2):
            gm = jnp.where(low_lane if j == 0 else ~low_lane, gp, jnp.zeros_like(gp))
            dprob = dot(gm, vp, NT)
            prob_low = p[2 * pair + j]
            prob = prob_low.astype(F32)
            inner = jnp.sum(prob * dprob, axis=-1, keepdims=True)
            ds = (prob * (dprob - inner)).astype(BF)
            dqs.append(dot(ds, kp))
            dks.append(dot(ds, qp, TN))
            dvs.append(dot(prob_low, gp, TN))
        dq = jnp.where(low_lane, dqs[0], dqs[1]) * 0.125
        dk = jnp.where(low_lane, dks[0], dks[1])
        dv = jnp.where(low_lane, dvs[0], dvs[1])
        parts[0, :, lanes] = dq.astype(BF)
        parts[1, :, lanes] = dk[:live].astype(BF)
        parts[2, :, lanes] = dv[:live].astype(BF)
    parts[3] = ga[...]
    mine[0] = parts[sc[1]]
    mine[1] = parts[sc[1] ^ 2]
    other_near[...] = parts[sc[1] ^ 1]
    other_far[...] = parts[sc[1] ^ 3]
    gn = sum(dot(parts[k], win[0, :, k * width : (k + 1) * width], NT) for k in range(3))
    grad_in, gain_sum, offset_sum = norm_back(gn, x[0:live].astype(F32), gain[0, 0:1].astype(F32))
    out = g[...] + grad_in
    if bottom:
        own, near, far = outs
        split_shards(dm, out.astype(BF), sc[1], (own.at[1], near.at[1], far.at[2], far.at[3]))
        for r, ref in enumerate((own.at[0], near.at[0], far.at[0], far.at[1])):
            ref[...] = refs[0][r]
    else:
        outs[0][...] = out
        outs[1][...] = out.astype(BF)
    sums[0:1] = gain_sum
    sums[1:2] = offset_sum
    sums[2:3] = jnp.sum(parts[0].astype(F32), axis=0, keepdims=True)
    sums[3:4] = jnp.sum(parts[2].astype(F32), axis=0, keepdims=True)


def back_attn(dm, layer, sc, g, ga, q, k, v, p, x, norm_gain, attn_in, attn_out, mix=None, deps=()):
    d, live, keys, slots = dm.width, dm.live, dm.keys, dm.slots
    bottom = layer == 0
    shapes = [sds((2, live, d), BF), sds((live, d), BF), sds((live, d), BF), sds((4, d), F32)]
    if bottom:
        shapes += [sds((2, slots, d), BF), sds((2, slots, d), BF), sds((4, slots, d), BF)]
    else:
        shapes += [sds((live, d), F32), sds((live, d), BF)]
    return run(
        functools.partial(back_attn_body, dm, bottom),
        (sc, g, ga, q, k, v, p, x, norm_gain, hbm(attn_in), hbm(attn_out)) + ((mix,) if bottom else ()),
        deps,
        grid=(1,),
        in_specs=[
            SMEM,
            whole((live, d)),
            whole((live, d)),
            whole((live, d)),
            whole((keys, d)),
            whole((keys, d)),
            whole((HEADS, live, keys)),
            whole((dm.full, d)),
            layer_block((2, d), layer),
            layer_block((d, 3 * d), layer),
            layer_block((d, d), layer),
        ]
        + ([whole(mix.shape)] if bottom else []),
        out_specs=[whole(s.shape) for s in shapes],
        out_shape=shapes,
        scratch_shapes=[pltpu.VMEM((4, live, d), BF)],
        compiler_params=params(16),
        cost_estimate=cost(),
    )


def store_shares(dm, refs, row, value, order, flip, stage):
    keep, send = refs
    n, share = dm.item_devs, dm.share
    half = n // 2
    for i in range(n):
        stage[i] = value[i * share : (i + 1) * share]
    for p in range(n):
        ref = keep if p < half else send
        index = unplace(dm, p ^ flip, order)
        ref[p % half, row : row + share] = stage[index]


def unplace(dm, place, order):
    out = place * 0
    for k, bit in enumerate(order):
        out = out | (((place >> (dm.bits - 1 - k)) & 1) << bit)
    return out


def wgrad_attn_body(dm, sc, nc, nc_near, mine, got_near, got_far, keep, send, left, right):
    n, live = dm.item_devs, dm.live
    for k, (got, ref) in enumerate(((got_near, keep), (got_far, send))):
        side = jnp.where((sc[1] ^ (2 * k)) == 3, 1, 0)
        left[0:live] = nc[side]
        left[live:] = nc_near[side]
        right[0:live] = mine[k]
        right[live:] = got[...]
        value = dot(left[...], right[...], TN).astype(BF)
        if dm.tiled:
            for i in range(n):
                ref[dm.place(i, dm.order_a) ^ sc[2]] = value[i * dm.share : (i + 1) * dm.share]
        else:
            ref[...] = value


def wgrad_attn(dm, sc, nc, nc_near, mine, got_near, got_far, deps=()):
    d, live, n, share = dm.width, dm.live, dm.item_devs, dm.share
    shape = (n, share, d) if dm.tiled else (d, d)
    args = (sc, nc, nc_near, mine, got_near, got_far)
    return run(
        functools.partial(wgrad_attn_body, dm),
        args,
        deps,
        grid=(1,),
        in_specs=[SMEM] + [whole(value.shape) for value in args[1:]],
        out_specs=[whole(shape)] * 2,
        out_shape=[sds(shape, BF)] * 2,
        scratch_shapes=[pltpu.VMEM((2 * live, d), BF)] * 2,
        compiler_params=params(12),
        cost_estimate=cost(),
    )


def ff_layout(dm, experts):
    rows, where = [], {}
    for index, (*_, orders) in enumerate(experts):
        for side in range(2):
            if side and orders[0] is orders[1] and dm.tiled:
                rows[-1] += dm.share
            else:
                rows.append(dm.share)
            where[index, side] = (len(rows) - 1, rows[-1] - dm.share)
    return rows, where


def wgrad_ff_body(dm, experts, stacked, sc, *refs):
    d, streams = dm.width, dm.streams
    n2s = refs[0:streams]
    gfs, refs = ([refs[streams].at[r] for r in range(streams)], refs[streams + 1 :]) if stacked else (refs[streams : 2 * streams], refs[2 * streams :])
    count = len(experts)
    wi, wo, bi = refs[:3]
    outs = refs[3:-5]
    n2a, gfa, acta, gpa, stage = refs[-5:]
    _, where = ff_layout(dm, experts)
    for index, (expert, start, stop, low, high, orders) in enumerate(experts):
        size = stop - start
        total = size * streams
        rows = first((size, 1)) + start
        keep = (rows >= low) & (rows < high)
        for r in range(streams):
            n2a[r * size : (r + 1) * size] = n2s[r][start:stop]
            gpart = gfs[r][start:stop]
            if low > start or high < stop:
                gpart = jnp.where(keep, gpart.astype(F32), 0.0).astype(BF)
            gfa[r * size : (r + 1) * size] = gpart
        chunk = size if size >= 128 else total
        wi_e = wi.at[index]
        wo_e = wo[index].reshape(d, d)

        def step(c, carry, chunk=chunk, wi_e=wi_e, wo_e=wo_e, index=index):
            at = slice(c * chunk, (c + 1) * chunk)
            act, slope = gelu_parts(dot(n2a[at], wi_e[...]) + bi[index])
            acta[at] = act.astype(BF)
            gpa[at] = (dot(gfa[at], wo_e, NT) * slope).astype(BF)
            return carry

        for c in range(total // chunk):
            step(c, 0)
        for side, (left, right) in enumerate(((n2a, gpa), (acta, gfa))):
            value = dot(left[0:total], right[0:total], TN).astype(BF)
            pair, row = where[index, side]
            if not dm.tiled:
                outs[pair][...] = value
                continue
            store_shares(dm, outs[2 * pair : 2 * pair + 2], row, value, orders[side], sc[2] if orders[side] == dm.order_a else sc[3], stage)


def wgrad_ff(dm, experts, sc, n2s, gfs, wi, wo, bi, deps=()):
    d, live, n, share, streams = dm.width, dm.live, dm.item_devs, dm.share, dm.streams
    count = len(experts)
    base = experts[0][0]
    part = d // n
    stacked = len(gfs) == 1
    pair_rows, _ = ff_layout(dm, experts)
    shapes = [(n // 2, rows, d) for rows in pair_rows for _ in range(2)] if dm.tiled else [(d, d)] * len(pair_rows)
    top = max(e[2] - e[1] for e in experts) * streams
    if dm.tiled:
        wo = wo.reshape(wo.shape[0], n, streams, part, d)
        wo_spec = pl.BlockSpec((count, n, None, part, d), lambda t, s: (base // count, 0, s[1], 0, 0), pipeline_mode=ONCE)
    else:
        wo_spec = pl.BlockSpec((count, d, d), lambda t, s: (base // count, 0, 0), pipeline_mode=ONCE)

    body = functools.partial(wgrad_ff_body, dm, experts, stacked)
    deps = order_after(deps)
    extra = len(deps)
    args = (*n2s, *gfs, wi, hbm(wo), bi)
    number = len(shapes)

    def wrapped(*refs):
        outs = refs[1 + len(args) + extra :]
        outs[number][...] = jnp.zeros_like(outs[number])
        body(*refs[: 1 + len(args)], *outs[:number], *outs[number + 1 :])

    gf_specs = [pl.BlockSpec((streams, live, d), lambda t, s: (0, 0, 0), pipeline_mode=ONCE)] if stacked else [pl.BlockSpec((live, d), lambda t, s: (0, 0), pipeline_mode=ONCE)] * streams
    *outs, token = pl.pallas_call(
        wrapped,
        grid_spec=pltpu.PrefetchScalarGridSpec(
            num_scalar_prefetch=1,
            grid=(1,),
            in_specs=[pl.BlockSpec((live, d), lambda t, s: (0, 0), pipeline_mode=ONCE)] * streams
            + gf_specs
            + [
                pl.BlockSpec((count, d, d), lambda t, s: (base // count, 0, 0), pipeline_mode=ONCE),
                wo_spec,
                pl.BlockSpec((count, 1, d), lambda t, s: (base // count, 0, 0), pipeline_mode=ONCE),
            ]
            + [ANY] * extra,
            out_specs=[pl.BlockSpec(shape, lambda t, s, shape=shape: (0,) * len(shape), pipeline_mode=ONCE) for shape in [*shapes, (8, 128)]],
            scratch_shapes=[pltpu.VMEM((top, d), BF)] * 4 + [pltpu.VMEM((n, share, d), BF)],
        ),
        out_shape=[sds(shape, BF) for shape in shapes] + [sds((8, 128), F32)],
        compiler_params=params(24),
        cost_estimate=cost(),
        name="wgrad_ff_body",
    )(sc, *args, *deps)
    note(outs, token)
    return outs


def finish_body(dm, sc, *refs):
    *pieces, first_out, second_out, stage = refs
    share, part = dm.share, dm.hidden // (dm.item_devs * dm.streams)
    expert = len(pieces) == 8
    for k, piece in enumerate(pieces):
        stage[k // 4, sc[1] ^ (k % 4)] = piece[...]
    if expert:
        for i in range(dm.item_devs):
            block = [stage[0, q, :, i * part : (i + 1) * part].astype(F32) for q in range(4)]
            first_out[0, :, i * 4 * part : (i + 1) * 4 * part] = jnp.concatenate(block, axis=1)
        for q in range(4):
            second_out[0, q * share : (q + 1) * share] = stage[1, q].astype(F32)
    else:
        for q in range(3):
            first_out[0, :, q * dm.width : (q + 1) * dm.width] = stage[0, q].astype(F32)
        second_out[0] = stage[0, 3].astype(F32)


def finish(dm, sc, sources, index, bases, *deps):
    share, d, hid = dm.share, dm.width, dm.hidden
    expert = len(sources) == 2
    if expert:
        shapes = [(3, share, hid), (3, 4 * share, d)]
    else:
        shapes = [(2, share, 3 * d), (2, share, d)]
    args, specs = [sc], [SMEM]
    for arrays, block in sources:
        args += arrays
        if dm.tiled:
            specs += [pl.BlockSpec((share, d), lambda t, block=block: (block, 0), pipeline_mode=ONCE)] * 4
        else:
            args[-4:] = [value[block * share : (block + 1) * share] for value in arrays]
            specs += [whole((share, d))] * 4
    deps = order_after(deps)
    count, extra = len(args), len(bases)

    def body(*refs):
        outs = refs[count + extra + len(deps) :]
        outs[2][...] = jnp.zeros_like(outs[2])
        finish_body(dm, *refs[:count], *outs[:2], outs[3])

    *outs, token = pl.pallas_call(
        body,
        grid=(1,),
        in_specs=specs + [pl.BlockSpec(memory_space=pltpu.HBM)] * extra + [ANY] * len(deps),
        out_specs=[
            pl.BlockSpec((1,) + shape[1:], lambda t: (index, 0, 0), pipeline_mode=ONCE) for shape in shapes
        ]
        + [whole((8, 128))],
        out_shape=[pltpu.HBM(shape, F32) for shape in shapes] + [sds((8, 128), F32)],
        scratch_shapes=[pltpu.VMEM((len(sources), 4, share, d), BF)],
        input_output_aliases={count + k: k for k in range(extra)},
        compiler_params=params(12),
        cost_estimate=cost(),
        name="finish_body",
    )(*args, *bases, *deps)
    note(outs, token)
    return outs


SMALL_ROWS = 32


def small_body(dm, sc, a0, a1, f0, f1, h0, h1, out):
    out[...] = jnp.zeros_like(out)
    share = dm.share
    wide = jnp.concatenate(
        [
            a0[2:4], a1[2:4],
            f0[2:3], f1[2:3],
            a0[0:1], f0[0:1], a1[0:1], f1[0:1],
            a0[1:2], f0[1:2], a1[1:2], f1[1:2],
            f0[3:5], f1[3:4],
        ],
        axis=0,
    )
    hidden = jnp.concatenate([h0[...], h1[...]], axis=0)
    count = wide.shape[0]
    for i in range(dm.item_devs):
        place = dm.place(i, dm.order_a) ^ sc[2]
        out[place, 0:count, 0:share] = wide[:, i * share : (i + 1) * share]
        for q in range(4):
            at = (i * 4 + q) * share
            out[place, count + 3 * q : count + 3 * q + 3, 0:share] = hidden[:, at : at + share]


def small_pack(dm, sc, values, deps):
    shape = (dm.item_devs, SMALL_ROWS, 128)
    return run(
        functools.partial(small_body, dm),
        (sc, *values),
        deps,
        grid=(1,),
        in_specs=[SMEM] + [whole(value.shape) for value in values],
        out_specs=whole(shape),
        out_shape=sds(shape, F32),
        compiler_params=params(8),
        cost_estimate=cost(),
    )


def small_out_body(dm, near, far, attn_bias, out_bias, gain, offset, hidden, ffn_bias):
    share = dm.share
    total = near[:, 0:share] + far[:, 0:share]
    for l in range(2):
        attn_bias[l] = total[2 * l : 2 * l + 2]
        gain[l] = total[6 + 2 * l : 8 + 2 * l]
        offset[l] = total[10 + 2 * l : 12 + 2 * l]
    out_bias[...] = total[4:6]
    ffn_bias[...] = total[14:17]
    hidden[...] = jnp.concatenate([total[17 + 3 * q : 20 + 3 * q] for q in range(4)], axis=1)


def small_unpack(dm, near, far, *deps):
    share = dm.share
    shapes = [(2, 2, share), (2, share), (2, 2, share), (2, 2, share), (3, 4 * share), (3, share)]
    return run(
        functools.partial(small_out_body, dm),
        (near, far),
        deps,
        grid=(1,),
        in_specs=[whole(near.shape)] * 2,
        out_specs=[whole(shape) for shape in shapes],
        out_shape=[sds(shape, F32) for shape in shapes],
        compiler_params=params(8),
        cost_estimate=cost(),
    )


def swap(value, axis, bit):
    size = lax.axis_size(axis)
    return lax.ppermute(value, axis, [(i, i ^ bit) for i in range(size)])


def by_index(blocks, index):
    return lax.dynamic_index_in_dim(blocks, index, 0, keepdims=False)


def gather_start(value):
    return [value, swap(value, "stream", 1), swap(value, "stream", 2)]


def gather_end(parts, *later):
    far = after(parts[2], *later) if later else parts[2]
    return parts + [swap(far, "stream", 1)]


def gather_rel(value):
    return gather_end(gather_start(value))


def after(value, *others):
    return lax.optimization_barrier((value, *others))[0]


def add_up(values):
    total = values[0].astype(F32)
    for value in values[1:]:
        total = total + value.astype(F32)
    return total


def add_body(count, *refs):
    refs[count][...] = add_up([ref[...] for ref in refs[:count]]).astype(refs[count].dtype)


def add_part(terms, size, index, deps=()):
    shape = (size,) + terms[0].shape[1:]
    return run(
        functools.partial(add_body, len(terms)),
        terms,
        deps,
        grid=(1,),
        in_specs=[pl.BlockSpec(shape, lambda t: (index, 0, 0))] * len(terms),
        out_specs=whole(shape),
        out_shape=sds(shape, terms[0].dtype),
        compiler_params=params(8),
        cost_estimate=cost(),
    )


def pieces_body(counts, *refs):
    out = refs[-1]
    row = at = 0
    for count in counts:
        terms = refs[at : at + count]
        rows = terms[0].shape[1]
        out[row : row + rows] = add_up([term[0] for term in terms]).astype(out.dtype)
        at += count
        row += rows


def add_pieces(sums, deps=()):
    terms = [term for value in sums for term in value.terms]
    rows = sum(value.terms[0].shape[1] for value in sums)
    shape = (rows, terms[0].shape[2])
    return run(
        functools.partial(pieces_body, [len(value.terms) for value in sums]),
        terms,
        deps,
        grid=(1,),
        in_specs=[pl.BlockSpec((1,) + term.shape[1:], lambda t: (0, 0, 0)) for term in terms],
        out_specs=whole(shape),
        out_shape=sds(shape, terms[0].dtype),
        compiler_params=params(8),
        cost_estimate=cost(),
    )


class Halving:
    def __init__(self, order, terms, size, send=None, deps=()):
        self.order = list(order)
        self.terms = list(terms)
        self.size = size
        if send is None:
            self.more(deps)
        else:
            self.send(send)

    def send(self, value):
        self.size //= 2
        self.last = value
        self.terms.append(swap(value, "items", 1 << self.order.pop(0)))

    def more(self, deps=()):
        if self.order:
            self.send(add_part(self.terms, self.size // 2, 1, deps))
        return self.last

    def drain(self):
        while self.order:
            self.more()
        return self


def per_device(
    tokens,
    cotangent,
    text_len,
    attn_in,
    attn_bias,
    attn_out,
    out_bias,
    norm_gain,
    norm_bias,
    ffn_in,
    ffn_in_bias,
    ffn_out,
    ffn_out_bias,
):
    streams = lax.axis_size("stream")
    item_devs = lax.axis_size("items")
    stream = lax.axis_index("stream")
    item = lax.axis_index("items")
    _, slots, width = tokens.shape
    hidden = ffn_in.shape[2]
    dm = Dims(slots, streams, width, hidden, item_devs)
    share = dm.share
    sc = jnp.stack([stream * 0, stream, dm.place(item, dm.order_a), dm.place(item, dm.order_b)]).astype(jnp.int32)

    part = hidden // (item_devs * streams)
    if dm.tiled:
        wi_q, bi_q = select_quarter(dm, sc, ffn_in, ffn_in_bias)
        wo_q = ffn_out
    else:
        wi_q = by_index(jnp.moveaxis(ffn_in.reshape(3, width, item_devs, streams, part), 3, 0), stream).reshape(3, width, width)
        wo_q = by_index(jnp.moveaxis(ffn_out.reshape(3, item_devs, streams, part, width), 2, 0), stream).reshape(3, width, width)
        bi_q = by_index(jnp.moveaxis(ffn_in_bias.reshape(3, item_devs, streams, part), 2, 0), stream).reshape(3, 1, width).astype(F32)

    far = swap(lax.dynamic_slice_in_dim(tokens, 2 * (1 - stream // 2), 2, 0), "stream", 2)
    far = after(far, bi_q)
    near = swap(jnp.stack([by_index(tokens, stream ^ 1), by_index(far, 1 - stream % 2)]), "stream", 1)
    cots = gather_start(after(cotangent, near))

    layer_params = (norm_gain, norm_bias, attn_in, attn_bias, attn_out, out_bias)
    a0 = fwd_attn(dm, 0, sc, text_len, (tokens, near, far), *layer_params)
    nc_0, q_0, k_0, v_0, p_0, x1_0, n2_0, n2l_0, x_0 = a0
    nc_near_0 = swap(nc_0, "stream", 1)
    n2_all_0 = gather_start(n2l_0)
    sv_0, sl_0, x_1 = fwd_ff_two(dm, n2_0, x1_0, ffn_in, ffn_in_bias, ffn_out, ffn_out_bias)
    cots = gather_end(cots, sv_0)
    n2_all_0 = gather_end(n2_all_0, sv_0)
    a1 = fwd_attn(dm, 1, sc, text_len, (x_1,), *layer_params)
    nc_1, q_1, k_1, v_1, p_1, x1_1, n2_1, n2l_1 = a1
    nc_near_1 = swap(nc_1, "stream", 1)
    n2_all_1 = gather_start(n2l_1)
    gf_all_1 = cot_prep(dm, sc, text_len, cots, (n2l_1, n2_all_0[3]))
    mix, g, ga_1, fs_1, hs_1 = top_ff(
        dm, 1, 2, sc, n2_1, gf_all_1, x1_1, norm_gain, ffn_in, ffn_in_bias, ffn_out, ffn_out_bias
    )
    n2_all_1 = gather_end(n2_all_1, fs_1)

    live, vis, lang, text_at = dm.live, dm.vis, dm.lang, dm.text_at
    half = item_devs // 2
    a, b = dm.order_a, dm.order_b

    def reorder(value, order):
        places = jnp.stack([dm.place(jnp.int32(i), order) for i in range(item_devs)])
        source = jnp.zeros((item_devs,), jnp.int32).at[places ^ dm.place(item, order)].set(jnp.arange(item_devs, dtype=jnp.int32))
        value = value.reshape(value.shape[:-2] + (item_devs, share, width))
        return jnp.take(value, source, axis=value.ndim - 3)

    def pairs(values, experts):
        if dm.tiled:
            return [values[2 * k : 2 * k + 2] for k in range(len(values) // 2)]
        out = []
        for index, (*_, orders) in enumerate(experts):
            sides = [reorder(values[2 * index + side], orders[side]) for side in range(2)]
            if orders[0] is orders[1]:
                sides = [jnp.concatenate(sides, axis=1)]
            out += [(value[:half], value[half:]) for value in sides]
        return out

    def halving(pair, order, *later):
        return Halving(order, [pair[0]], item_devs, after(pair[1], *later) if later else pair[1])

    def attn_sum(keep, send, *later):
        if not dm.tiled:
            keep, send = reorder(keep, a), reorder(send, a)
        return [keep, swap(after(send, *later) if later else send, "stream", 2)]

    experts = ((2, 0, live, 0, live, (a, a)),)
    join = wgrad_ff(dm, experts, sc, n2_all_1, (gf_all_1,), wi_q, wo_q, bi_q, deps=(fs_1,))
    join_sum = halving(pairs(join, experts)[0], a)
    mine_1, near_1, far_1, as_1, g, gf_0 = back_attn(
        dm, 1, sc, g, ga_1, q_1, k_1, v_1, p_1, x_1, norm_gain, attn_in, attn_out, deps=(join[0],)
    )
    gf_all_0 = gather_start(gf_0)
    near_1, far_1 = swap(near_1, "stream", 1), swap(far_1, "stream", 1)
    g, ga_0, fs_0, hs_0 = back_ff_two(dm, 0, g, gf_0, x1_0, norm_gain, sv_0, sl_0, ffn_in, ffn_out)
    gf_all_0 = gather_end(gf_all_0, fs_0)
    att_1 = wgrad_attn(dm, sc, nc_1, nc_near_1, mine_1, near_1, far_1, deps=(fs_0,))
    att_1_terms = attn_sum(*att_1)
    experts = ((0, 0, vis, 0, text_at, (a, list(a))), (1, lang, live, text_at, live, (a, b)))
    last = join_sum.more((att_1[0],))
    two = wgrad_ff(dm, experts, sc, n2_all_0, gf_all_0, wi_q, wo_q, bi_q, deps=(last,))
    va, vb, la, lb = pairs(two, experts)
    va_sum = halving(va, a)
    lb_sum = halving(lb, b)
    last = join_sum.more((two[0],))
    mine_0, near_0, far_0, as_0, tg_own, tg_near, tg_far = back_attn(
        dm, 0, sc, g, ga_0, q_0, k_0, v_0, p_0, x_0, norm_gain, attn_in, attn_out, mix=mix, deps=(last,)
    )
    near_0, far_0 = swap(near_0, "stream", 1), swap(far_0, "stream", 1)
    small = small_pack(dm, sc, (as_0, as_1, fs_0, fs_1, hs_0, hs_1), ())
    last = va_sum.more((small,))
    vb_sum = halving(vb, a, last)
    att_1_sum = Halving(a, att_1_terms, item_devs, deps=(last,))
    last = lb_sum.more((att_1_sum.last,))
    att_0 = wgrad_attn(dm, sc, nc_0, nc_near_0, mine_0, near_0, far_0, deps=(last,))
    att_0_terms = attn_sum(*att_0)
    last = va_sum.more((att_0[0],))
    last = vb_sum.more((last,))
    join_piece = add_pieces([join_sum.drain()], deps=(last,))
    last = vb_sum.more((join_piece,))
    att_0_sum = Halving(a, att_0_terms, item_devs, deps=(last,))
    last = att_1_sum.more((att_0_sum.last,))
    va_piece = add_pieces([va_sum.drain()], deps=(last,))
    last = lb_sum.more((va_piece,))
    la_sum = halving(la, a, last)
    last = att_1_sum.more((last,))
    tg_far = swap(after(tg_far, va_piece), "stream", 2)
    lb_piece = add_pieces([lb_sum.drain()], deps=(last,))
    vb_piece = add_pieces([vb_sum.drain()], deps=(lb_piece,))
    tg_near = swap(jnp.concatenate([tg_near, after(tg_far, vb_piece)[1::2]]), "stream", 1)
    all_1 = gather_start(jnp.concatenate([join_piece, va_piece, vb_piece, lb_piece]))
    last = att_0_sum.more((vb_piece,))
    small_sum = Halving(a, [small[:half]], item_devs, after(small[half:], last))
    att_1_piece = add_pieces([att_1_sum.drain()], deps=(last,))
    last = la_sum.more((att_1_piece,))
    last = att_0_sum.more((last,))
    last = small_sum.more((last,))
    att_0_piece = add_pieces([att_0_sum.drain()], deps=(last,))
    last = la_sum.more((att_0_piece,))
    all_1 = gather_end(all_1, last)
    all_2 = gather_start(after(jnp.concatenate([att_0_piece, att_1_piece]), all_1[2]))
    results = finish(dm, sc, [(all_1, 0), (all_1, 1)], 2, (), last)
    last = small_sum.more((results[0],))
    mixed, tokens_grad = join_shards(dm, sc, tg_own, tg_near, tg_far, last)
    results = finish(dm, sc, [(all_1, 2), (all_1, 3)], 0, results, mixed)
    la_piece = add_pieces([la_sum.drain()], deps=(results[0],))
    all_2 = gather_end(all_2, la_piece)
    all_3 = gather_start(after(la_piece, all_2[2]))
    attn_results = finish(dm, sc, [(all_2, 1)], 1, (), la_piece)
    attn_results = finish(dm, sc, [(all_2, 0)], 0, attn_results)
    small_own = add_pieces([small_sum.drain()], deps=(attn_results[0],))
    small_near = small_own + swap(small_own, "stream", 1)
    small_all = swap(small_near, "stream", 2)
    all_3 = gather_end(all_3, small_own)
    ffn_results = finish(dm, sc, [(all_3, 0), (all_1, 4)], 1, results, small_own)
    outs = small_unpack(dm, small_near, small_all, ffn_results[0])

    return (
        mixed,
        tokens_grad,
        attn_results[0],
        outs[0],
        attn_results[1],
        outs[1],
        outs[2],
        outs[3],
        ffn_results[0],
        outs[4],
        ffn_results[1],
        outs[5],
    )


def solution(mesh):
    return jax.shard_map(
        per_device,
        mesh=mesh,
        in_specs=(
            P("items", "stream", None),
            P("items", "stream", None),
            P("items"),
            P(),
            P(),
            P(),
            P(),
            P(),
            P(),
            P(),
            P(),
            P(),
            P(),
        ),
        out_specs=(
            P("items", "stream", None),
            P("items", "stream", None),
            P(None, "items", None),
            P(None, None, "items"),
            P(None, "items", None),
            P(None, "items"),
            P(None, None, "items"),
            P(None, None, "items"),
            P(None, "items", None),
            P(None, "items"),
            P(None, "items", None),
            P(None, "items"),
        ),
        check_vma=False,
    )
```
